32 devices in a mesh: dp: 4 (over y, x), fsdp: 8 (over z, core).
Axes of the slice: x: 2, y: 2, z: 4, core: 2. Of those that a mesh axis runs over, the one named last changes fastest.
Arguments:
- prefix_in: bfloat16 [16, 816, 2048], P('fsdp', 'dp'), may hold values from -6 to 6
- action_in: bfloat16 [16, 48, 1024], P('fsdp', 'dp'), may hold values from -6 to 6
- valid_count: int32 [16], P('fsdp'), may hold values from 1 to 48, as said below
- prefix_before: bfloat16 [2048], P('fsdp'), may hold values from 0.5 to 1.5
- prefix_query: bfloat16 [2048, 2048], P('fsdp'), may hold values from -0.125 to 0.125
- prefix_key: bfloat16 [2048, 256], P('fsdp'), may hold values from -0.125 to 0.125
- prefix_value: bfloat16 [2048, 256], P('fsdp'), may hold values from -0.125 to 0.125
- prefix_output: bfloat16 [2048, 2048], P('fsdp'), may hold values from -4 to 4
- prefix_middle: bfloat16 [2048], P('fsdp'), may hold values from 0.5 to 1.5
- prefix_gate: bfloat16 [2048, 16384], P(None, 'fsdp'), may hold values from -0.125 to 0.125
- prefix_up: bfloat16 [2048, 16384], P(None, 'fsdp'), may hold values from -0.125 to 0.125
- prefix_down: bfloat16 [16384, 2048], P('fsdp'), may hold values from -0.046875 to 0.046875
- action_before: bfloat16 [1024], P('fsdp'), may hold values from 0.5 to 1.5
- action_query: bfloat16 [1024, 2048], P('fsdp'), may hold values from -0.1875 to 0.1875
- action_key: bfloat16 [1024, 256], P('fsdp'), may hold values from -0.1875 to 0.1875
- action_value: bfloat16 [1024, 256], P('fsdp'), may hold values from -0.1875 to 0.1875
- action_output: bfloat16 [2048, 1024], P('fsdp'), may hold values from -4 to 4
- action_middle: bfloat16 [1024], P('fsdp'), may hold values from 0.5 to 1.5
- action_gate: bfloat16 [1024, 4096], P(None, 'fsdp'), may hold values from -0.1875 to 0.1875
- action_up: bfloat16 [1024, 4096], P(None, 'fsdp'), may hold values from -0.1875 to 0.1875
- action_down: bfloat16 [4096, 1024], P('fsdp'), may hold values from -0.09375 to 0.09375
- prefix_cotangent: bfloat16 [16, 816, 2048], P('fsdp', 'dp'), may hold values from -6 to 6
- action_cotangent: bfloat16 [16, 48, 1024], P('fsdp', 'dp'), may hold values from -6 to 6
Outputs:
- prefix_out: bfloat16 [16, 816, 2048], P('fsdp', 'dp')
- action_out: bfloat16 [16, 48, 1024], P('fsdp', 'dp')
- prefix_grad: float32 [16, 816, 2048], P('fsdp', 'dp')
- action_grad: float32 [16, 48, 1024], P('fsdp', 'dp')
- prefix_before_grad: float32 [2048], P('fsdp')
- prefix_query_grad: float32 [2048, 2048], P('fsdp')
- prefix_key_grad: float32 [2048, 256], P('fsdp')
- prefix_value_grad: float32 [2048, 256], P('fsdp')
- prefix_output_grad: float32 [2048, 2048], P('fsdp')
- prefix_middle_grad: float32 [2048], P('fsdp')
- prefix_gate_grad: float32 [2048, 16384], P(None, 'fsdp')
- prefix_up_grad: float32 [2048, 16384], P(None, 'fsdp')
- prefix_down_grad: float32 [16384, 2048], P('fsdp')
- action_before_grad: float32 [1024], P('fsdp')
- action_query_grad: float32 [1024, 2048], P('fsdp')
- action_key_grad: float32 [1024, 256], P('fsdp')
- action_value_grad: float32 [1024, 256], P('fsdp')
- action_output_grad: float32 [2048, 1024], P('fsdp')
- action_middle_grad: float32 [1024], P('fsdp')
- action_gate_grad: float32 [1024, 4096], P(None, 'fsdp')
- action_up_grad: float32 [1024, 4096], P(None, 'fsdp')
- action_down_grad: float32 [4096, 1024], P('fsdp')
The draws below stay inside these ranges and needn't reach their ends.
Inputs may be any that keep to these rules, and one draw needn't show every extreme that they name: The first valid_count of an item's 48 action tokens are valid. In every draw some item has exactly 48 valid action tokens and another exactly 1.
All inputs are finite; a program needn't handle non-finite values.
Results may differ from the reference program's by a relative error of at most 0.022.
Values may be sent and summed in bfloat16 or wider, within the bound.
A program may use at most 384 MiB of HBM per device.

```python
import jax
import jax.numpy as jnp
from jax import lax

D = 2048
DA = 1024
H = 8
HD = 256
FF = 16384
FFA = 4096
PREFIX = 816
ACTION = 48
ITEMS = 16


def draw_valid_count(key, part):
    key = jax.random.fold_in(key, 7)
    first, second = jax.random.split(key)
    counts = jax.random.randint(first, (ITEMS,), 1, ACTION + 1)
    chosen = jax.random.randint(second, (), 0, ITEMS)
    place = jnp.arange(ITEMS)
    counts = jnp.where(place == chosen, ACTION, counts)
    counts = jnp.where(place == (chosen + 1) % ITEMS, 1, counts)
    return counts.astype(jnp.int32)


def level_of(rng, shape, cuts, least, high):
    level, own = 1.0, jax.random.fold_in(rng, 6)
    for dim, shards_of in cuts:
        steps = jnp.exp(jax.random.uniform(jax.random.fold_in(own, dim), (shards_of,), jnp.float32, least / len(cuts), high / len(cuts)))
        level = level * jnp.repeat(steps, shape[dim] // shards_of).reshape([-1 if axis == dim else 1 for axis in range(len(shape))])
    return level


def centred(key, shape, deviation, most, cuts=(), kind=jnp.bfloat16):
    level = level_of(key, shape, cuts, -0.22, 0.18) if cuts else 1.0
    values = jax.random.normal(key, shape, jnp.float32) * deviation * level
    return jnp.minimum(jnp.maximum(values, -most), most).astype(kind)


def setup_inputs(seed: int = 0) -> dict:
    key_of = jax.random.split(jax.random.key(seed), 24)
    return {
        "prefix_in": centred(key_of[0], (ITEMS, PREFIX, D), 1.0, 6.0, ((0, 8), (1, 4))),
        "action_in": centred(key_of[1], (ITEMS, ACTION, DA), 1.0, 6.0, ((0, 8), (1, 4))),
        "valid_count": draw_valid_count(jax.random.fold_in(key_of[23], 71), 0),
        "prefix_before": jnp.clip(1.0 + 0.1 * jax.random.normal(key_of[3], (D,), jnp.float32), 0.5, 1.5).astype(jnp.bfloat16),
        "prefix_query": centred(key_of[4], (D, H * HD), D ** -0.5, 0.125, ((0, 8),)),
        "prefix_key": centred(key_of[5], (D, HD), D ** -0.5, 0.125, ((0, 8),)),
        "prefix_value": centred(key_of[6], (D, HD), D ** -0.5, 0.125, ((0, 8),)),
        "prefix_output": centred(key_of[7], (H * HD, D), (max(1, H * HD // PREFIX)) ** -0.5, 4.0, ((0, 8),)),
        "prefix_middle": jnp.clip(1.0 + 0.1 * jax.random.normal(key_of[8], (D,), jnp.float32), 0.5, 1.5).astype(jnp.bfloat16),
        "prefix_gate": centred(key_of[9], (D, FF), D ** -0.5, 0.125, ((1, 8),)),
        "prefix_up": centred(key_of[10], (D, FF), D ** -0.5, 0.125, ((1, 8),)),
        "prefix_down": centred(key_of[11], (FF, D), FF ** -0.5, 0.046875, ((0, 8),)),
        "action_before": jnp.clip(1.0 + 0.1 * jax.random.normal(key_of[12], (DA,), jnp.float32), 0.5, 1.5).astype(jnp.bfloat16),
        "action_query": centred(key_of[13], (DA, H * HD), DA ** -0.5, 0.1875, ((0, 8),)),
        "action_key": centred(key_of[14], (DA, HD), DA ** -0.5, 0.1875, ((0, 8),)),
        "action_value": centred(key_of[15], (DA, HD), DA ** -0.5, 0.1875, ((0, 8),)),
        "action_output": centred(key_of[16], (H * HD, DA), (max(1, H * HD // PREFIX)) ** -0.5, 4.0, ((0, 8),)),
        "action_middle": jnp.clip(1.0 + 0.1 * jax.random.normal(key_of[17], (DA,), jnp.float32), 0.5, 1.5).astype(jnp.bfloat16),
        "action_gate": centred(key_of[18], (DA, FFA), DA ** -0.5, 0.1875, ((1, 8),)),
        "action_up": centred(key_of[19], (DA, FFA), DA ** -0.5, 0.1875, ((1, 8),)),
        "action_down": centred(key_of[20], (FFA, DA), FFA ** -0.5, 0.09375, ((0, 8),)),
        "prefix_cotangent": centred(key_of[21], (ITEMS, PREFIX, D), 1.0, 6.0, ((0, 8), (1, 4))),
        "action_cotangent": centred(key_of[22], (ITEMS, ACTION, DA), 1.0, 6.0, ((0, 8), (1, 4))),
    }


EPS = 1e-06

@jax.custom_vjp
def low(v):
    return lax.optimization_barrier(v.astype(jnp.bfloat16)).astype(jnp.float32)

@jax.custom_vjp
def low_back(v):
    return v

def low_keep(v):
    return (low(v), None)

def low_pass(kept, grad):
    return (grad,)

def back_keep(v):
    return (v, None)

def back_low(kept, grad):
    return (low(grad),)
low.defvjp(low_keep, low_pass)
low_back.defvjp(back_keep, back_low)

def product(left, right):
    return jnp.dot(left, right, precision=lax.Precision.HIGHEST)

def normalize(rows, gain):
    return rows * lax.rsqrt(lax.optimization_barrier(jnp.mean(rows * rows, axis=-1, keepdims=True)) + EPS) * gain

def project(rows, weight):
    return low(low_back(product(rows, weight)))

def feed(rows, gain, gate_weight, up_weight, down_weight):
    hidden = low(normalize(rows, gain))
    gate = low_back(product(hidden, gate_weight))
    upper = low_back(product(hidden, up_weight))
    inner = low(jax.nn.gelu(gate, approximate=True) * upper)
    return product(inner, down_weight)

def item_forward(weights, prefix_rows, action_rows, count):
    prefix_before, prefix_query, prefix_key, prefix_value, prefix_output, prefix_middle, prefix_gate, prefix_up, prefix_down, action_before, action_query, action_key, action_value, action_output, action_middle, action_gate, action_up, action_down = weights
    prefix_hidden = low(normalize(prefix_rows, prefix_before))
    action_hidden = low(normalize(action_rows, action_before))
    queries = jnp.concatenate([project(prefix_hidden, prefix_query), project(action_hidden, action_query)], axis=0)
    keys = jnp.concatenate([project(prefix_hidden, prefix_key), project(action_hidden, action_key)], axis=0)
    values = jnp.concatenate([project(prefix_hidden, prefix_value), project(action_hidden, action_value)], axis=0)
    length = PREFIX + ACTION
    queries = queries.reshape(length, H, HD)
    scores = low_back(jnp.einsum('thd,sd->hts', queries, keys, precision=lax.Precision.HIGHEST) * HD ** (-0.5))
    position = jnp.arange(length)
    allowed = (position[None, :] < PREFIX) | (position[:, None] >= PREFIX) & (position[None, :] <= position[:, None]) & (position[None, :] < PREFIX + count)
    probs = low(jax.nn.softmax(jnp.where(allowed[None], scores, -1e+30), axis=-1))
    mixed = jnp.einsum('hts,sd->thd', probs, values, precision=lax.Precision.HIGHEST).reshape(length, H * HD)
    mixed = low(low_back(mixed))
    prefix_mid = prefix_rows + low_back(product(mixed[:PREFIX], prefix_output))
    action_mid = action_rows + low_back(product(mixed[PREFIX:], action_output))
    prefix_out = prefix_mid + feed(prefix_mid, prefix_middle, prefix_gate, prefix_up, prefix_down)
    action_out = action_mid + feed(action_mid, action_middle, action_gate, action_up, action_down)
    return (prefix_out, action_out)

def reference(prefix_in, action_in, valid_count, prefix_before, prefix_query, prefix_key, prefix_value, prefix_output, prefix_middle, prefix_gate, prefix_up, prefix_down, action_before, action_query, action_key, action_value, action_output, action_middle, action_gate, action_up, action_down, prefix_cotangent, action_cotangent):
    weights = tuple((weight.astype(jnp.float32) for weight in (prefix_before, prefix_query, prefix_key, prefix_value, prefix_output, prefix_middle, prefix_gate, prefix_up, prefix_down, action_before, action_query, action_key, action_value, action_output, action_middle, action_gate, action_up, action_down)))
    live = jnp.arange(ACTION)[None, :] < valid_count[:, None]
    action_back = jnp.where(live[:, :, None], action_cotangent.astype(jnp.float32), jnp.zeros((), jnp.float32))

    def step(totals, item):
        prefix_rows, action_rows, count, prefix_grad_out, action_grad_out = item

        def forward(weight_set, prefix_x, action_x):
            return item_forward(weight_set, prefix_x, action_x, count)
        outputs, pull = jax.vjp(forward, weights, prefix_rows, action_rows)
        weight_grads, prefix_grad, action_grad = pull((prefix_grad_out, action_grad_out))
        totals = jax.tree.map(jnp.add, totals, weight_grads)
        return (totals, (outputs[0], outputs[1], prefix_grad, action_grad))
    zeros = tuple((jnp.zeros_like(weight) for weight in weights))
    totals, stacked = lax.scan(step, zeros, (prefix_in.astype(jnp.float32), action_in.astype(jnp.float32), valid_count, prefix_cotangent.astype(jnp.float32), action_back))
    return (stacked[0].astype(jnp.bfloat16), stacked[1].astype(jnp.bfloat16), stacked[2], stacked[3], totals[0], totals[1], totals[2], totals[3], totals[4], totals[5], totals[6], totals[7], totals[8], totals[9], totals[10], totals[11], totals[12], totals[13], totals[14], totals[15], totals[16], totals[17])
```

```python
import functools
import math

import jax
import jax.numpy as jnp
from jax import lax
from jax.experimental import pallas as pl
from jax.experimental.pallas import tpu as pltpu
from jax.sharding import PartitionSpec as P

EPS = 1e-06
NEGATIVE = -1e30
LOW = jnp.bfloat16
FULL = jnp.float32
TILE = 16
MIB = 1 << 20


def normalize(rows, gain):
    return rows * lax.rsqrt(jnp.mean(rows * rows, axis=-1, keepdims=True) + EPS) * gain


def multiply(left, right):
    return jnp.dot(left, right, preferred_element_type=FULL)


def multiply_left(left, right):
    return lax.dot_general(
        left, right, (((0,), (0,)), ((), ())), preferred_element_type=FULL
    )


def multiply_right(left, right):
    return lax.dot_general(
        left, right, (((1,), (1,)), ((), ())), preferred_element_type=FULL
    )


def activate(gate, upper):
    return jax.nn.gelu(gate, approximate=True) * upper


class Line:
    def __init__(self):
        self.size = lax.axis_size("fsdp")
        self.chips = self.size // 2
        self.place = lax.axis_index("fsdp")
        self.chip = self.place // 2
        self.core = self.place % 2
        self.order = [
            sorted(range(self.chips), key=lambda other: (abs(other - chip), other))
            for chip in range(self.chips)
        ]

    def is_one_of(self, chips):
        found = self.chip == chips[0]
        for chip in chips[1:]:
            found = found | (self.chip == chip)
        return found

    def move(self, value, chips, step):
        pairs = [
            (2 * chip + core, 2 * (chip + step) + core) for chip in chips for core in range(2)
        ]
        return lax.ppermute(value, "fsdp", pairs)

    def partner(self, value):
        return lax.ppermute(value, "fsdp", [(i, i ^ 1) for i in range(self.size)])

    def choose(self, options):
        items = list(options.values())
        result = items[-1][1]
        for chips, value in items[:-1]:
            result = jnp.where(self.is_one_of(chips), value, result)
        return result

    def gather(self, block):
        count = self.chips
        from_left, from_right = {0: block}, {0: block}
        for step in range(1, count):
            from_left[step] = self.move(from_left[step - 1], range(step - 1, count - 1), 1)
            from_right[step] = self.move(from_right[step - 1], range(1, count - step + 1), -1)
        chunks = [(block, self.partner(block))]
        for position in range(1, count):
            options = {}
            for chip in range(count):
                source = self.order[chip][position]
                key = source - chip
                value = from_left[-key] if key < 0 else from_right[key]
                options.setdefault(key, ([], value))[0].append(chip)
            mine = self.choose(options)
            chunks.append((mine, self.partner(mine)))
        return chunks

    def scatter(self, far, own):
        count = self.chips
        total = own.astype(FULL)
        for side in (1, -1):
            arrived = None
            for step in range(1, count):
                payload = far(step, side)
                if arrived is not None:
                    payload = (payload.astype(FULL) + arrived.astype(FULL)).astype(LOW)
                chips = range(0, step) if side == 1 else range(count - step, count)
                arrived = self.move(payload, chips, side)
            if arrived is not None:
                total = total + arrived.astype(FULL)
        return total

    def scatter_chunks(self, chunks):
        summed = [
            mine.astype(FULL) + self.partner(other).astype(FULL) for mine, other in chunks
        ]
        low = [value.astype(LOW) for value in summed]

        def far(step, side):
            options = {}
            for chip in range(self.chips):
                target = chip + side * (self.chips - step)
                if 0 <= target < self.chips:
                    position = self.order[chip].index(target)
                    options.setdefault(position, ([], low[position]))[0].append(chip)
            return self.choose(options)

        return self.scatter(far, summed[0])

    def scatter_rows(self, rows):
        pairs = rows.reshape(self.chips, 2, *rows.shape[1:])
        mine = lax.dynamic_index_in_dim(pairs, self.core, 1, keepdims=False)
        other = lax.dynamic_index_in_dim(pairs, 1 - self.core, 1, keepdims=False)
        summed = (mine.astype(FULL) + self.partner(other).astype(FULL)).astype(LOW)

        def far(step, side):
            target = jnp.clip(self.chip + side * (self.chips - step), 0, self.chips - 1)
            return lax.dynamic_index_in_dim(summed, target, 0, keepdims=False)

        own = lax.dynamic_index_in_dim(summed, self.chip, 0, keepdims=False)
        return self.scatter(far, own)


def gather_copies(value, shift_back=False):
    count = lax.axis_size("dp")
    return [value] + [
        lax.ppermute(value, "dp", [(i, (i + k) % count) for i in range(count)])
        for k in range(1, count)
    ]


def scatter_copies(blocks):
    count = lax.axis_size("dp")
    total = blocks[0]
    for k in range(1, count):
        sent = blocks[k].astype(LOW)
        total = total + lax.ppermute(
            sent, "dp", [(i, (i - k) % count) for i in range(count)]
        ).astype(FULL)
    return total


def rounded(count, unit=TILE):
    return -(-count // unit) * unit


def gather_kernel(shares, *refs):
    count = len(shares)
    shards, wholes = refs[:count], refs[count : 2 * count]
    local_sem, pair_send, pair_recv = refs[2 * count : 2 * count + 3]
    line_send, line_recv, copy_send, copy_recv, core_send, core_recv = refs[2 * count + 3 :]
    mesh = pl.DeviceIdType.MESH
    copies = lax.axis_size("dp")
    place = lax.axis_index("dp")
    size = lax.axis_size("fsdp")
    chips = size // 2
    me = lax.axis_index("fsdp")
    chip, core = me // 2, me % 2
    partner = 2 * chip + 1 - core
    has_left, has_right = chip > 0, chip < chips - 1

    barrier = pltpu.get_barrier_semaphore()
    pl.semaphore_signal(barrier, inc=1, device_id=(place, partner), device_id_type=mesh)
    for k in range(1, copies):
        peer = lax.rem(place + k, copies)
        pl.semaphore_signal(barrier, inc=1, device_id=(peer, me), device_id_type=mesh)

    @pl.when(has_left)
    def _():
        pl.semaphore_signal(barrier, inc=1, device_id=(place, me - 2), device_id_type=mesh)

    @pl.when(has_right)
    def _():
        pl.semaphore_signal(barrier, inc=1, device_id=(place, me + 2), device_id_type=mesh)

    neighbours = jnp.minimum(chip, 1) + jnp.minimum(chips - 1 - chip, 1)
    pl.semaphore_wait(barrier, copies + neighbours)

    def rows(a, owner, share):
        whole = shards[a].shape[0]
        part = whole // shares[a]
        return pl.ds(pl.multiple_of(owner * whole + share * part, TILE), part)

    def remote(source, target, send, recv, device):
        return pltpu.make_async_remote_copy(
            src_ref=source,
            dst_ref=target,
            send_sem=send,
            recv_sem=recv,
            device_id=device,
            device_id_type=mesh,
        )

    def my_share(a):
        return place if shares[a] > 1 else 0

    def line_copy(a, side, step):
        owner = me - 2 * step if side == 0 else me + 2 * step
        where = rows(a, owner, my_share(a))
        target = me + 2 if side == 0 else me - 2
        return remote(
            wholes[a].at[where],
            wholes[a].at[where],
            line_send.at[a, side, step],
            line_recv.at[a, side, step],
            (place, target),
        )

    def first_copy(a, side):
        part = shards[a].shape[0] // shares[a]
        target = me + 2 if side == 0 else me - 2
        return remote(
            shards[a].at[pl.ds(pl.multiple_of(my_share(a) * part, TILE), part)],
            wholes[a].at[rows(a, me, my_share(a))],
            line_send.at[a, side, 0],
            line_recv.at[a, side, 0],
            (place, target),
        )

    def owner_of(side, step):
        return me - 2 * step if side == 0 else me + 2 * step

    def peer_copy(a, side, step, k):
        where = rows(a, owner_of(side, step), place)
        return remote(
            wholes[a].at[where],
            wholes[a].at[where],
            copy_send.at[a, side, step, k],
            copy_recv.at[a, side, step, k],
            (lax.rem(place + k, copies), me),
        )

    def core_copy(a, side, step, k):
        share = lax.rem(place + copies - k, copies) if shares[a] > 1 else 0
        where = rows(a, owner_of(side, step), share)
        return remote(
            wholes[a].at[where],
            wholes[a].at[where],
            core_send.at[a, side, step, k],
            core_recv.at[a, side, step, k],
            (place, partner),
        )

    def pair_copy(a):
        return remote(
            shards[a],
            wholes[a].at[rows_all(a)],
            pair_send.at[a],
            pair_recv.at[a],
            (place, partner),
        )

    def rows_all(a):
        whole = shards[a].shape[0]
        return pl.ds(pl.multiple_of(me * whole, TILE), whole)

    def local_copy(a):
        return pltpu.make_async_copy(shards[a], wholes[a].at[rows_all(a)], local_sem.at[a])

    def sends(side):
        return has_right if side == 0 else has_left

    def has(side, step):
        return chip >= step if side == 0 else chip + step <= chips - 1

    for a in range(count):
        for side in range(2):

            @pl.when(sends(side))
            def _(a=a, side=side):
                first_copy(a, side).start()

    for a in range(count):
        pair_copy(a).start()
        local_copy(a).start()

    def peers(a):
        return range(1, copies) if shares[a] > 1 else range(0)

    def hand_over(a, side, step):
        for k in peers(a):
            peer_copy(a, side, step, k).wait_recv()
            core_copy(a, side, step, k).start()

    def advance(step, _):
        for a in range(count):
            for side in range(2):

                @pl.when(has(side, step))
                def _(a=a, side=side):
                    line_copy(a, side, step - 1).wait_recv()

                    @pl.when(sends(side))
                    def _():
                        line_copy(a, side, step).start()

                    for k in peers(a):
                        peer_copy(a, side, step, k).start()
                    core_copy(a, side, step, 0).start()

        for a in range(count):
            for side in range(2):

                @pl.when((step > 1) & has(side, step - 1))
                def _(a=a, side=side):
                    hand_over(a, side, step - 1)

        return 0

    lax.fori_loop(1, chips, advance, 0)
    for a in range(count):
        for side in range(2):

            @pl.when(has(side, chips - 1))
            def _(a=a, side=side):
                hand_over(a, side, chips - 1)

    def finish(step, _):
        for a in range(count):
            for side in range(2):

                @pl.when(has(side, step))
                def _(a=a, side=side):
                    @pl.when(sends(side))
                    def _():
                        line_copy(a, side, step).wait_send()

                    for k in peers(a):
                        peer_copy(a, side, step, k).wait_send()
                        core_copy(a, side, step, k).wait_send()
                        core_copy(a, side, step, k).wait_recv()
                    core_copy(a, side, step, 0).wait_send()
                    core_copy(a, side, step, 0).wait_recv()

        return 0

    lax.fori_loop(1, chips, finish, 0)
    for a in range(count):
        for side in range(2):

            @pl.when(sends(side))
            def _(a=a, side=side):
                first_copy(a, side).wait_send()

        pair_copy(a).wait_send()
        pair_copy(a).wait_recv()
        local_copy(a).wait()


def gather_shards(*shards):
    copies, size = lax.axis_size("dp"), lax.axis_size("fsdp")
    chips = size // 2
    shares = [copies if shard.shape[0] % (TILE * copies) == 0 else 1 for shard in shards]
    count = len(shards)
    dma = pltpu.SemaphoreType.DMA
    anywhere = pl.BlockSpec(memory_space=pl.ANY)
    return pl.pallas_call(
        functools.partial(gather_kernel, shares),
        out_shape=[
            jax.ShapeDtypeStruct((size * shard.shape[0], *shard.shape[1:]), shard.dtype)
            for shard in shards
        ],
        in_specs=[anywhere] * count,
        out_specs=[anywhere] * count,
        scratch_shapes=[
            dma((count,)),
            dma((count,)),
            dma((count,)),
            dma((count, 2, chips)),
            dma((count, 2, chips)),
            dma((count, 2, chips, copies)),
            dma((count, 2, chips, copies)),
            dma((count, 2, chips, copies)),
            dma((count, 2, chips, copies)),
        ],
        compiler_params=pltpu.CompilerParams(collective_id=0, has_side_effects=True),
        name="gather_shards",
    )(*shards)


def feed_kernel(
    valid,
    mine_ref,
    other_ref,
    back_mine_ref,
    back_other_ref,
    gate_ref,
    up_ref,
    down_ref,
    *refs,
):
    inner_ref, gate_grad_ref, up_grad_ref, rows_ref, back_ref = refs[-5:]
    root = math.sqrt(2.0 / math.pi)
    for half, (rows, back) in enumerate(((mine_ref, back_mine_ref), (other_ref, back_other_ref))):
        where = slice(half * valid, (half + 1) * valid)
        rows, back = rows[:valid], back[:valid]

        @pl.when(pl.program_id(0) == 0)
        def _():
            rows_ref[where] = rows
            back_ref[where] = back

        gate = multiply(rows, gate_ref[...])
        upper = multiply(rows, up_ref[...])
        inner_grad = multiply_right(back, down_ref[...])
        square = gate * gate
        bent = jnp.tanh(root * gate * (1.0 + 0.044715 * square))
        half_up = 0.5 + 0.5 * bent
        active = gate * half_up
        slope = half_up + (0.5 * root) * gate * (1.0 - bent * bent) * (1.0 + 0.134145 * square)
        inner_ref[where] = (active * upper).astype(LOW)
        gate_grad_ref[where] = (inner_grad * upper * slope).astype(LOW)
        up_grad_ref[where] = (inner_grad * active).astype(LOW)


def feed_chunk(position, chunks, valid, pair, back_pair, gate, up, down, before):
    block, width = pair[0].shape
    hidden = gate.shape[1]
    tile = math.gcd(hidden, 512)
    whole = pl.BlockSpec((block, width), lambda j: (0, 0))
    column = pl.BlockSpec((width, tile), lambda j: (0, j))
    outs = [pl.BlockSpec((2 * valid, tile), lambda j: (position, j))] * 3
    outs += [pl.BlockSpec((2 * valid, width), lambda j: (position, 0))] * 2
    shapes = [jax.ShapeDtypeStruct((chunks * 2 * valid, hidden), LOW)] * 3
    shapes += [jax.ShapeDtypeStruct((chunks * 2 * valid, width), LOW)] * 2
    extra = [] if before is None else list(before)
    return pl.pallas_call(
        functools.partial(feed_kernel, valid),
        out_shape=shapes,
        grid=(hidden // tile,),
        in_specs=[whole] * 4
        + [column, column, pl.BlockSpec((tile, width), lambda j: (j, 0))]
        + [pl.BlockSpec(memory_space=pl.ANY)] * len(extra),
        out_specs=outs,
        input_output_aliases={7 + i: i for i in range(len(extra))},
        compiler_params=pltpu.CompilerParams(vmem_limit_bytes=56 * MIB),
        cost_estimate=pl.CostEstimate(
            flops=12 * valid * width * hidden,
            bytes_accessed=2 * (3 * width * hidden + 10 * valid * width + 6 * valid * hidden),
            transcendentals=2 * valid * hidden,
        ),
        name="feed_chunk",
    )(*pair, *back_pair, gate, up, down, *extra)


def back_kernel(valid, gate_grad_ref, up_grad_ref, gate_ref, up_ref, small_ref, mine_ref, other_ref):
    for half, out in enumerate((mine_ref, other_ref)):
        where = slice(half * valid, (half + 1) * valid)
        part = multiply_right(gate_grad_ref[where], gate_ref[...])
        part = part + multiply_right(up_grad_ref[where], up_ref[...])
        out[:valid] = part.astype(LOW)
        out[valid:] = small_ref[half]


def down_kernel(valid, inner_ref, down_ref, small_ref, mine_ref, other_ref):
    for half, out in enumerate((mine_ref, other_ref)):
        where = slice(half * valid, (half + 1) * valid)
        out[:valid] = multiply(inner_ref[where], down_ref[...]).astype(LOW)
        out[valid:] = small_ref[half]


def part_chunk(kernel, position, valid, grads, weights, weight_block, small, width):
    hidden = grads[0].shape[1]
    tile = math.gcd(width, 512)
    extra = small.shape[1]
    rows = pl.BlockSpec((2 * valid, hidden), lambda j: (position, 0))
    out = pl.BlockSpec((valid + extra, tile), lambda j: (0, j))
    return pl.pallas_call(
        functools.partial(kernel, valid),
        out_shape=[jax.ShapeDtypeStruct((valid + extra, width), LOW)] * 2,
        grid=(width // tile,),
        in_specs=[rows] * len(grads)
        + [weight_block(tile)] * len(weights)
        + [pl.BlockSpec((2, extra, tile), lambda j: (0, 0, j))],
        out_specs=[out] * 2,
        compiler_params=pltpu.CompilerParams(vmem_limit_bytes=48 * MIB),
        cost_estimate=pl.CostEstimate(
            flops=4 * len(grads) * valid * width * hidden,
            bytes_accessed=2 * len(grads) * (width * hidden + 2 * valid * hidden)
            + 4 * valid * width,
            transcendentals=0,
        ),
        name="part_chunk",
    )(*grads, *weights, small)


def stacked(refs, columns=slice(None)):
    return jnp.concatenate([ref[0, :, columns] for ref in refs], axis=0)


def softmax_of(queries, keys, bias, scale):
    scores = multiply_right(queries, keys) * scale + bias
    raised = jnp.exp(scores - jnp.max(scores, axis=-1, keepdims=True))
    return raised / jnp.sum(raised, axis=-1, keepdims=True)


def mix_kernel(scale, head_size, *refs):
    prefix_ref, action_ref, bias_ref = refs[:3]
    prefix_out, action_out = refs[-2:]
    queries = stacked((prefix_ref, action_ref))
    kv = stacked(refs[3:-2])
    probs = softmax_of(queries, kv[:, :head_size], bias_ref[0], scale).astype(LOW)
    mixed = multiply(probs, kv[:, head_size:]).astype(LOW)
    rows = prefix_ref.shape[1]
    prefix_out[0] = mixed[:rows]
    action_out[0] = mixed[rows:]


def mix_back_kernel(scale, head_size, *refs):
    prefix_ref, action_ref, prefix_grad_ref, action_grad_ref, bias_ref = refs[:5]
    prefix_out, action_out, kv_out = refs[-3:]
    queries = stacked((prefix_ref, action_ref))
    grads = stacked((prefix_grad_ref, action_grad_ref))
    kv = stacked(refs[5:-3])
    keys, values = kv[:, :head_size], kv[:, head_size:]
    probs = softmax_of(queries, keys, bias_ref[0], scale)
    probs_grad = multiply_right(grads, values)
    delta = jnp.sum(probs * probs_grad, axis=-1, keepdims=True)
    score_grad = (probs * (probs_grad - delta)).astype(LOW)
    query_grad = (multiply(score_grad, keys) * scale).astype(LOW)
    rows = prefix_ref.shape[1]
    prefix_out[0] = query_grad[:rows]
    action_out[0] = query_grad[rows:]

    @pl.when(pl.program_id(1) == 0)
    def _():
        kv_out[...] = jnp.zeros_like(kv_out)

    kv_out[0, :, :head_size] += multiply_left(score_grad, queries) * scale
    kv_out[0, :, head_size:] += multiply_left(probs.astype(LOW), grads)


def mix_call(backward, scale, head_size, heads, prefix, action, kv_blocks, bias, grads=()):
    items, prefix_rows, _ = prefix.shape
    action_rows = action.shape[1]
    rows = prefix_rows + action_rows
    length = bias.shape[2]
    per_head = [
        pl.BlockSpec((1, prefix_rows, head_size), lambda i, h: (i, 0, h)),
        pl.BlockSpec((1, action_rows, head_size), lambda i, h: (i, 0, h)),
    ]
    in_specs = per_head * (2 if backward else 1)
    in_specs += [pl.BlockSpec((1, rows, length), lambda i, h: (i, 0, 0))]
    in_specs += [pl.BlockSpec((1, rows, 2 * head_size), lambda i, h: (i, 0, 0))] * len(kv_blocks)
    out_specs = list(per_head)
    shapes = [
        jax.ShapeDtypeStruct((items, prefix_rows, heads * head_size), LOW),
        jax.ShapeDtypeStruct((items, action_rows, heads * head_size), LOW),
    ]
    if backward:
        out_specs += [pl.BlockSpec((1, length, 2 * head_size), lambda i, h: (i, 0, 0))]
        shapes += [jax.ShapeDtypeStruct((items, length, 2 * head_size), FULL)]
    kernel = mix_back_kernel if backward else mix_kernel
    dots = 5 if backward else 2
    return pl.pallas_call(
        functools.partial(kernel, scale, head_size),
        out_shape=shapes,
        grid=(items, heads),
        in_specs=in_specs,
        out_specs=out_specs,
        compiler_params=pltpu.CompilerParams(vmem_limit_bytes=48 * MIB),
        cost_estimate=pl.CostEstimate(
            flops=2 * dots * items * heads * rows * length * head_size,
            bytes_accessed=8 * items * rows * heads * head_size,
            transcendentals=items * heads * rows * length,
        ),
        name="mix_back" if backward else "mix",
    )(prefix, action, *grads, bias, *kv_blocks)


def body(
    prefix_in,
    action_in,
    valid_count,
    prefix_before,
    prefix_query,
    prefix_key,
    prefix_value,
    prefix_output,
    prefix_middle,
    prefix_gate,
    prefix_up,
    prefix_down,
    action_before,
    action_query,
    action_key,
    action_value,
    action_output,
    action_middle,
    action_gate,
    action_up,
    action_down,
    prefix_cotangent,
    action_cotangent,
):
    line = Line()
    shards = line.size
    copies = lax.axis_size("dp")
    items, prefix_rows, width = prefix_in.shape
    action_rows = action_in.shape[1]
    action_width = action_in.shape[2]
    head_size = prefix_key.shape[1]
    features = prefix_query.shape[1]
    heads = features // head_size
    columns = features + 2 * head_size
    prefix_length = prefix_rows * copies
    scale = head_size ** (-0.5)
    place = lax.axis_index("dp")
    prefix_pad, action_pad = rounded(prefix_rows), rounded(action_rows)
    prefix_tokens, action_tokens = items * prefix_pad, items * action_pad
    folded = action_tokens * action_width // width
    folded_pad = rounded(folded)

    def padded(prefix, action):
        prefix = jnp.pad(prefix, ((0, 0), (0, prefix_pad - prefix_rows), (0, 0)))
        action = jnp.pad(action, ((0, 0), (0, action_pad - action_rows), (0, 0)))
        return prefix.reshape(prefix_tokens, width), action.reshape(action_tokens, action_width)

    def trimmed(prefix, action):
        prefix = prefix.reshape(items, prefix_pad, width)[:, :prefix_rows]
        return prefix, action.reshape(items, action_pad, action_width)[:, :action_rows]

    def fold(action):
        rows = action.reshape(-1, folded, width)
        return jnp.pad(rows, ((0, 0), (0, folded_pad - folded), (0, 0)))

    def unfold(rows):
        return rows[:folded].reshape(action_tokens, action_width)

    def pack(prefix, action):
        return jnp.concatenate([prefix, fold(action)[0]], axis=0)

    def unpack(packed):
        return packed[:prefix_tokens], unfold(packed[prefix_tokens:])

    share, action_share = prefix_before.shape[0], action_before.shape[0]
    cuts = [0, share, 2 * share, 2 * share + action_share, 2 * share + 2 * action_share]
    gain_rows = rounded(-(-cuts[4] // 128))
    gains = jnp.concatenate([prefix_before, prefix_middle, action_before, action_middle])
    gains = jnp.pad(gains, (0, gain_rows * 128 - cuts[4])).reshape(gain_rows, 128)
    prefix_qkv, action_qkv, prefix_o, action_o, gains = gather_shards(
        jnp.concatenate([prefix_query, prefix_key, prefix_value], axis=1),
        jnp.concatenate([action_query, action_key, action_value], axis=1),
        prefix_output,
        action_output,
        gains,
    )
    gains = gains.reshape(shards, gain_rows * 128).astype(FULL)
    prefix_gain_in, prefix_gain, action_gain_in, action_gain = (
        gains[:, cuts[i] : cuts[i + 1]].reshape(-1) for i in range(4)
    )

    live = (place * action_rows + jnp.arange(action_rows))[None, :] < valid_count[:, None]
    prefix_back, action_back = padded(
        prefix_cotangent,
        jnp.where(live[:, :, None], action_cotangent, jnp.zeros_like(action_cotangent)),
    )
    back_chunks = line.gather(pack(prefix_back, action_back))

    prefix_flat, action_flat = padded(prefix_in.astype(FULL), action_in.astype(FULL))
    prefix_hidden = normalize(prefix_flat, prefix_gain_in).astype(LOW)
    action_hidden = normalize(action_flat, action_gain_in).astype(LOW)
    prefix_all = multiply(prefix_hidden, prefix_qkv).astype(LOW)
    prefix_all = prefix_all.reshape(items, prefix_pad, columns)
    action_all = multiply(action_hidden, action_qkv).astype(LOW)
    action_all = action_all.reshape(items, action_pad, columns)
    kv = jnp.concatenate([prefix_all[:, :, features:], action_all[:, :, features:]], axis=1)
    kv_blocks = gather_copies(kv)

    far = copies * (prefix_rows + action_rows)

    def places(owner):
        prefix = jnp.arange(prefix_pad)
        action = jnp.arange(action_pad)
        return jnp.concatenate(
            [
                jnp.where(prefix < prefix_rows, owner * prefix_rows + prefix, far),
                jnp.where(
                    action < action_rows, prefix_length + owner * action_rows + action, far
                ),
            ]
        )

    query_place = places(place)
    key_place = jnp.concatenate([places((place + copies - k) % copies) for k in range(copies)])
    later = (query_place[:, None] >= prefix_length) & (key_place[None, :] <= query_place[:, None])
    allowed = (key_place[None, None, :] < prefix_length) | later[None] & (
        key_place[None, None, :] < prefix_length + valid_count[:, None, None]
    )
    bias = jnp.where(allowed, 0.0, NEGATIVE).astype(FULL)
    mix = functools.partial(
        mix_call,
        scale=scale,
        head_size=head_size,
        heads=heads,
        prefix=prefix_all,
        action=action_all,
        kv_blocks=kv_blocks,
        bias=bias,
    )
    prefix_mixed, action_mixed = mix(False)
    prefix_mixed = prefix_mixed.reshape(prefix_tokens, features)
    action_mixed = action_mixed.reshape(action_tokens, features)
    prefix_mid = prefix_flat + multiply(prefix_mixed, prefix_o)
    action_mid = action_flat + multiply(action_mixed, action_o)

    hidden_chunks = line.gather(
        pack(
            normalize(prefix_mid, prefix_gain).astype(LOW),
            normalize(action_mid, action_gain).astype(LOW),
        )
    )
    arrays = None
    for position in range(line.chips):
        arrays = feed_chunk(
            position,
            line.chips,
            prefix_tokens,
            hidden_chunks[position],
            back_chunks[position],
            prefix_gate,
            prefix_up,
            prefix_down,
            arrays,
        )
    inner, gate_grad, up_grad, all_rows, all_back = arrays
    action_rows_all, action_back_all = (
        jnp.concatenate([unfold(v[prefix_tokens:]) for pair in chunks for v in pair], axis=0)
        for chunks in (hidden_chunks, back_chunks)
    )
    action_inner, pull = jax.vjp(
        activate, multiply(action_rows_all, action_gate), multiply(action_rows_all, action_up)
    )
    action_inner = action_inner.astype(LOW)
    action_gate_grad, action_up_grad = (
        v.astype(LOW) for v in pull(multiply_right(action_back_all, action_down))
    )

    down_grad = multiply_left(inner, all_back).astype(LOW)
    action_feed = tuple(
        v.astype(LOW)
        for v in (
            multiply_left(action_rows_all, action_gate_grad),
            multiply_left(action_rows_all, action_up_grad),
            multiply_left(action_inner, action_back_all),
        )
    )
    gate_grad, up_grad, down_grad = lax.optimization_barrier((gate_grad, up_grad, down_grad))
    first_sums = lax.psum((down_grad, *action_feed), "dp")

    def halves(rows):
        return fold(rows.astype(LOW)).reshape(line.chips, 2, folded_pad, width)

    small = halves(
        multiply_right(action_gate_grad, action_gate) + multiply_right(action_up_grad, action_up)
    )
    part_of = [
        part_chunk(
            back_kernel,
            i,
            prefix_tokens,
            (gate_grad, up_grad),
            (prefix_gate, prefix_up),
            lambda tile: pl.BlockSpec((tile, gate_grad.shape[1]), lambda j: (j, 0)),
            small[i],
            width,
        )
        for i in range(line.chips)
    ]
    feed_back = unpack(line.scatter_chunks(part_of))

    gate_weight_grad = multiply_left(all_rows, gate_grad).astype(LOW)
    gate_weight_grad, first_done = lax.optimization_barrier((gate_weight_grad, first_sums[0]))
    gate_sum = lax.psum(gate_weight_grad, "dp")
    up_weight_grad = multiply_left(all_rows, up_grad).astype(LOW)
    up_weight_grad, gate_done = lax.optimization_barrier((up_weight_grad, gate_sum))
    up_sum = lax.psum(up_weight_grad, "dp")

    small = halves(multiply(action_inner, action_down))
    part_of = [
        part_chunk(
            down_kernel,
            i,
            prefix_tokens,
            (inner,),
            (prefix_down,),
            lambda tile: pl.BlockSpec((inner.shape[1], tile), lambda j: (0, j)),
            small[i],
            width,
        )
        for i in range(line.chips)
    ]
    sums = unpack(line.scatter_chunks(part_of))
    prefix_out, action_out = trimmed(
        (prefix_mid + sums[0]).astype(LOW), (action_mid + sums[1]).astype(LOW)
    )

    _, pull = jax.vjp(normalize, prefix_mid, prefix_gain)
    prefix_inner_grad, prefix_middle_part = pull(feed_back[0])
    _, pull = jax.vjp(normalize, action_mid, action_gain)
    action_inner_grad, action_middle_part = pull(feed_back[1])
    prefix_mid_grad = prefix_back.astype(FULL) + prefix_inner_grad
    action_mid_grad = action_back.astype(FULL) + action_inner_grad
    prefix_low = prefix_mid_grad.astype(LOW)
    action_low = action_mid_grad.astype(LOW)
    output_part = multiply_left(prefix_mixed, prefix_low).astype(LOW)
    output_owned = line.scatter_rows(output_part.reshape(shards, features // shards, width))
    mixed_grads = (
        multiply_right(prefix_low, prefix_o).astype(LOW).reshape(items, prefix_pad, features),
        multiply_right(action_low, action_o).astype(LOW).reshape(items, action_pad, features),
    )
    prefix_query_grad, action_query_grad, kv_grad = mix(True, grads=mixed_grads)
    step = prefix_pad + action_pad
    kv_grad = scatter_copies([kv_grad[:, k * step : (k + 1) * step] for k in range(copies)])
    kv_grad = kv_grad.astype(LOW)
    prefix_qkv_grad = jnp.concatenate([prefix_query_grad, kv_grad[:, :prefix_pad]], axis=2)
    action_qkv_grad = jnp.concatenate([action_query_grad, kv_grad[:, prefix_pad:]], axis=2)
    prefix_qkv_grad = prefix_qkv_grad.reshape(prefix_tokens, columns)
    action_qkv_grad = action_qkv_grad.reshape(action_tokens, columns)
    prefix_hidden_grad = multiply_right(prefix_qkv_grad, prefix_qkv)
    action_hidden_grad = multiply_right(action_qkv_grad, action_qkv)
    _, pull = jax.vjp(normalize, prefix_flat, prefix_gain_in)
    prefix_entry_grad, prefix_before_part = pull(prefix_hidden_grad)
    _, pull = jax.vjp(normalize, action_flat, action_gain_in)
    action_entry_grad, action_before_part = pull(action_hidden_grad)
    prefix_grad, action_grad = trimmed(
        prefix_mid_grad + prefix_entry_grad, action_mid_grad + action_entry_grad
    )

    gain_parts = jnp.concatenate(
        [
            part.reshape(shards, -1)
            for part in (
                prefix_before_part,
                prefix_middle_part,
                action_before_part,
                action_middle_part,
            )
        ],
        axis=1,
    )
    gain_rows = rounded(-(-cuts[4] // columns))
    gain_parts = jnp.pad(gain_parts, ((0, 0), (0, gain_rows * columns - cuts[4])))
    qkv_part = multiply_left(prefix_hidden, prefix_qkv_grad).astype(LOW)
    qkv_owned = line.scatter_rows(
        jnp.concatenate(
            [
                qkv_part.reshape(shards, width // shards, columns),
                gain_parts.astype(LOW).reshape(shards, gain_rows, columns),
            ],
            axis=1,
        )
    )
    tokens_all = jnp.concatenate([action_hidden, action_mixed, action_low, action_qkv_grad], axis=1)
    tokens_all = lax.all_gather(tokens_all, "fsdp", axis=0, tiled=True)
    edges = [0]
    for part in (action_width, features, action_width, columns):
        edges.append(edges[-1] + part)
    rows = action_query.shape[0]
    hidden_slice = lax.dynamic_slice_in_dim(tokens_all[:, : edges[1]], line.place * rows, rows, 1)
    action_qkv_owned = multiply_left(hidden_slice, tokens_all[:, edges[3] :])
    rows = action_output.shape[0]
    mixed_slice = lax.dynamic_slice_in_dim(
        tokens_all[:, edges[1] : edges[2]], line.place * rows, rows, 1
    )
    action_output_owned = multiply_left(mixed_slice, tokens_all[:, edges[2] : edges[3]])

    owned = tuple(
        v.astype(LOW) for v in (qkv_owned, output_owned, action_qkv_owned, action_output_owned)
    )
    owned, up_done = lax.optimization_barrier((owned, up_sum))
    qkv_owned, output_owned, action_qkv_owned, action_output_owned = (
        v.astype(FULL) for v in lax.psum(owned, "dp")
    )
    rows = prefix_query.shape[0]
    gain_owned = qkv_owned[rows:].reshape(-1)
    return (
        prefix_out,
        action_out,
        prefix_grad,
        action_grad,
        gain_owned[cuts[0] : cuts[1]],
        qkv_owned[:rows, :features],
        qkv_owned[:rows, features : features + head_size],
        qkv_owned[:rows, features + head_size :],
        output_owned,
        gain_owned[cuts[1] : cuts[2]],
        gate_done.astype(FULL),
        up_done.astype(FULL),
        first_done.astype(FULL),
        gain_owned[cuts[2] : cuts[3]],
        action_qkv_owned[:, :features],
        action_qkv_owned[:, features : features + head_size],
        action_qkv_owned[:, features + head_size :],
        action_output_owned,
        gain_owned[cuts[3] : cuts[4]],
        *(v.astype(FULL) for v in first_sums[1:]),
    )


def solution(mesh):
    tokens = P("fsdp", "dp", None)
    rows, columns, vector = P("fsdp", None), P(None, "fsdp"), P("fsdp")
    weights = (vector, rows, rows, rows, rows, vector, columns, columns, rows)
    return jax.shard_map(
        body,
        mesh=mesh,
        in_specs=(tokens, tokens, vector, *weights, *weights, tokens, tokens),
        out_specs=(tokens, tokens, tokens, tokens, *weights, *weights),
        check_vma=False,
    )
```

```python
import functools
import math

import jax
import jax.numpy as jnp
from jax import lax
from jax.experimental import pallas as pl
from jax.experimental.pallas import tpu as pltpu
from jax.sharding import PartitionSpec as P

EPS = 1e-06
NEGATIVE = -1e30
LOW = jnp.bfloat16
FULL = jnp.float32
TILE = 16
MIB = 1 << 20
SMALL = pl.CostEstimate(flops=1, bytes_accessed=1, transcendentals=0)


def normalize(rows, gain):
    return rows * lax.rsqrt(jnp.mean(rows * rows, axis=-1, keepdims=True) + EPS) * gain


def multiply(left, right):
    return jnp.dot(left, right, preferred_element_type=FULL)


def multiply_left(left, right):
    return lax.dot_general(
        left, right, (((0,), (0,)), ((), ())), preferred_element_type=FULL
    )


def multiply_right(left, right):
    return lax.dot_general(
        left, right, (((1,), (1,)), ((), ())), preferred_element_type=FULL
    )


def activate(gate, upper):
    return jax.nn.gelu(gate, approximate=True) * upper


class Line:
    def __init__(self):
        self.size = lax.axis_size("fsdp")
        self.chips = self.size // 2
        self.place = lax.axis_index("fsdp")
        self.chip = self.place // 2
        self.core = self.place % 2

    def move(self, value, chips, step):
        pairs = [
            (2 * chip + core, 2 * (chip + step) + core) for chip in chips for core in range(2)
        ]
        return lax.ppermute(value, "fsdp", pairs)

    def pairs(self, identity, *values):
        mine, other = (weight_shares(core, *values) for core in (self.core, 1 - self.core))
        return add_pairs(identity, mine, other)


class Relay:
    def __init__(self, line, summed, index):
        self.line, self.summed, self.index = line, summed, index
        self.taken, self.arrived = 0, []

    def advance(self, part, parts=3):
        line, count = self.line, self.line.chips
        last = -(-(count - 1) * part // parts)
        while self.taken < last:
            self.taken += 1
            step, arrived = self.taken, self.arrived
            self.arrived = []
            for i, side in enumerate((1, -1)):
                target = self.index(jnp.clip(line.chip + side * (count - step), 0, count - 1))
                if arrived:
                    payload = add_block(self.summed, target, [arrived[i]], LOW)
                else:
                    payload = lax.dynamic_index_in_dim(self.summed, target, 0, keepdims=False)
                chips = range(0, step) if side == 1 else range(count - step, count)
                self.arrived.append(line.move(payload, chips, side))

    def after(self, values):
        self.arrived, values = lax.optimization_barrier((self.arrived, values))
        return values

    def finish(self):
        self.advance(1, 1)
        return add_block(self.summed, self.index(self.line.chip), self.arrived, FULL)


def add_kernel(index_ref, value_ref, *refs):
    total = value_ref[0].astype(FULL)
    for ref in refs[:-1]:
        total = total + ref[...].astype(FULL)
    refs[-1][...] = total.astype(refs[-1].dtype)


def add_block(values, index, others, kind):
    shape = values.shape[1:]
    block = pl.BlockSpec(shape, lambda i, index: (0, 0))
    return pl.pallas_call(
        add_kernel,
        out_shape=jax.ShapeDtypeStruct(shape, kind),
        grid_spec=pltpu.PrefetchScalarGridSpec(
            num_scalar_prefetch=1,
            grid=(1,),
            in_specs=[pl.BlockSpec((1, *shape), lambda i, index: (index[0], 0, 0))]
            + [block] * len(others),
            out_specs=block,
        ),
        compiler_params=pltpu.CompilerParams(vmem_limit_bytes=40 * MIB),
        cost_estimate=SMALL,
        name="add_block",
    )(jnp.reshape(index, (1,)).astype(jnp.int32), values, *others)


def pair_kernel(mine_ref, other_ref, out_ref, landed, send_sem, recv_sem):
    place, me = lax.axis_index("dp"), lax.axis_index("fsdp")
    partner = (place, me + 1 - 2 * (me % 2))
    mesh = pl.DeviceIdType.MESH
    turn, count = pl.program_id(0), landed.shape[0]

    def copy(at):
        return pltpu.make_async_remote_copy(
            src_ref=other_ref.at[at],
            dst_ref=landed.at[at],
            send_sem=send_sem.at[at],
            recv_sem=recv_sem.at[at],
            device_id=partner,
            device_id_type=mesh,
        )

    @pl.when(turn == 0)
    def _():
        barrier = pltpu.get_barrier_semaphore()
        pl.semaphore_signal(barrier, inc=1, device_id=partner, device_id_type=mesh)
        pl.semaphore_wait(barrier, 1)
        for at in range(count):
            copy(at).start()

    copy(turn).wait_recv()
    out_ref[0] = (mine_ref[0].astype(FULL) + landed[turn].astype(FULL)).astype(LOW)

    @pl.when(turn == count - 1)
    def _():
        for at in range(count):
            copy(at).wait_send()


def add_pairs(identity, mine, other):
    count, shape = mine.shape[0], mine.shape[1:]
    block = pl.BlockSpec((1, *shape), lambda i: (i, 0, 0))
    dma = pltpu.SemaphoreType.DMA
    return pl.pallas_call(
        pair_kernel,
        out_shape=jax.ShapeDtypeStruct(mine.shape, LOW),
        grid=(count,),
        in_specs=[block, pl.BlockSpec(memory_space=pl.ANY)],
        out_specs=block,
        scratch_shapes=[pltpu.VMEM(mine.shape, LOW), dma((count,)), dma((count,))],
        compiler_params=pltpu.CompilerParams(
            collective_id=identity, has_side_effects=True, vmem_limit_bytes=40 * MIB
        ),
        cost_estimate=SMALL,
        name="add_pairs",
    )(mine, other)


def rounded(count, unit=TILE):
    return -(-count // unit) * unit


def gather_kernel(shares, *refs):
    count = len(shares)
    shards, wholes = refs[:count], refs[count : 2 * count]
    local_sem, pair_send, pair_recv = refs[2 * count : 2 * count + 3]
    line_send, line_recv, copy_send, copy_recv, core_send, core_recv = refs[2 * count + 3 :]
    mesh = pl.DeviceIdType.MESH
    copies = lax.axis_size("dp")
    place = lax.axis_index("dp")
    size = lax.axis_size("fsdp")
    chips = size // 2
    me = lax.axis_index("fsdp")
    chip, core = me // 2, me % 2
    partner = 2 * chip + 1 - core
    has_left, has_right = chip > 0, chip < chips - 1

    barrier = pltpu.get_barrier_semaphore()
    pl.semaphore_signal(barrier, inc=1, device_id=(place, partner), device_id_type=mesh)
    for k in range(1, copies):
        peer = lax.rem(place + k, copies)
        pl.semaphore_signal(barrier, inc=1, device_id=(peer, me), device_id_type=mesh)

    @pl.when(has_left)
    def _():
        pl.semaphore_signal(barrier, inc=1, device_id=(place, me - 2), device_id_type=mesh)

    @pl.when(has_right)
    def _():
        pl.semaphore_signal(barrier, inc=1, device_id=(place, me + 2), device_id_type=mesh)

    neighbours = jnp.minimum(chip, 1) + jnp.minimum(chips - 1 - chip, 1)
    pl.semaphore_wait(barrier, copies + neighbours)

    def rows(a, owner, share):
        whole = shards[a].shape[0]
        part = whole // shares[a]
        return pl.ds(pl.multiple_of(owner * whole + share * part, TILE), part)

    def remote(source, target, send, recv, device):
        return pltpu.make_async_remote_copy(
            src_ref=source,
            dst_ref=target,
            send_sem=send,
            recv_sem=recv,
            device_id=device,
            device_id_type=mesh,
        )

    def my_share(a):
        return place if shares[a] > 1 else 0

    def line_copy(a, side, step):
        owner = me - 2 * step if side == 0 else me + 2 * step
        where = rows(a, owner, my_share(a))
        target = me + 2 if side == 0 else me - 2
        return remote(
            wholes[a].at[where],
            wholes[a].at[where],
            line_send.at[a, side, step],
            line_recv.at[a, side, step],
            (place, target),
        )

    def first_copy(a, side):
        part = shards[a].shape[0] // shares[a]
        target = me + 2 if side == 0 else me - 2
        return remote(
            shards[a].at[pl.ds(pl.multiple_of(my_share(a) * part, TILE), part)],
            wholes[a].at[rows(a, me, my_share(a))],
            line_send.at[a, side, 0],
            line_recv.at[a, side, 0],
            (place, target),
        )

    def owner_of(side, step):
        return me - 2 * step if side == 0 else me + 2 * step

    def peer_copy(a, side, step, k):
        where = rows(a, owner_of(side, step), place)
        return remote(
            wholes[a].at[where],
            wholes[a].at[where],
            copy_send.at[a, side, step, k],
            copy_recv.at[a, side, step, k],
            (lax.rem(place + k, copies), me),
        )

    def core_copy(a, side, step, k):
        share = lax.rem(place + copies - k, copies) if shares[a] > 1 else 0
        where = rows(a, owner_of(side, step), share)
        return remote(
            wholes[a].at[where],
            wholes[a].at[where],
            core_send.at[a, side, step, k],
            core_recv.at[a, side, step, k],
            (place, partner),
        )

    def pair_copy(a):
        return remote(
            shards[a],
            wholes[a].at[rows_all(a)],
            pair_send.at[a],
            pair_recv.at[a],
            (place, partner),
        )

    def rows_all(a):
        whole = shards[a].shape[0]
        return pl.ds(pl.multiple_of(me * whole, TILE), whole)

    def local_copy(a):
        return pltpu.make_async_copy(shards[a], wholes[a].at[rows_all(a)], local_sem.at[a])

    def sends(side):
        return has_right if side == 0 else has_left

    def has(side, step):
        return chip >= step if side == 0 else chip + step <= chips - 1

    for a in range(count):
        for side in range(2):

            @pl.when(sends(side))
            def _(a=a, side=side):
                first_copy(a, side).start()

    for a in range(count):
        pair_copy(a).start()
        local_copy(a).start()

    def peers(a):
        return range(1, copies) if shares[a] > 1 else range(0)

    def hand_over(a, side, step):
        for k in peers(a):
            peer_copy(a, side, step, k).wait_recv()
            core_copy(a, side, step, k).start()

    def advance(step, _):
        for a in range(count):
            for side in range(2):

                @pl.when(has(side, step))
                def _(a=a, side=side):
                    line_copy(a, side, step - 1).wait_recv()

                    @pl.when(sends(side))
                    def _():
                        line_copy(a, side, step).start()

                    for k in peers(a):
                        peer_copy(a, side, step, k).start()
                    core_copy(a, side, step, 0).start()

        for a in range(count):
            for side in range(2):

                @pl.when((step > 1) & has(side, step - 1))
                def _(a=a, side=side):
                    hand_over(a, side, step - 1)

        return 0

    lax.fori_loop(1, chips, advance, 0)
    for a in range(count):
        for side in range(2):

            @pl.when(has(side, chips - 1))
            def _(a=a, side=side):
                hand_over(a, side, chips - 1)

    def finish(step, _):
        for a in range(count):
            for side in range(2):

                @pl.when(has(side, step))
                def _(a=a, side=side):
                    @pl.when(sends(side))
                    def _():
                        line_copy(a, side, step).wait_send()

                    for k in peers(a):
                        peer_copy(a, side, step, k).wait_send()
                        core_copy(a, side, step, k).wait_send()
                        core_copy(a, side, step, k).wait_recv()
                    core_copy(a, side, step, 0).wait_send()
                    core_copy(a, side, step, 0).wait_recv()

        return 0

    lax.fori_loop(1, chips, finish, 0)
    for a in range(count):
        for side in range(2):

            @pl.when(sends(side))
            def _(a=a, side=side):
                first_copy(a, side).wait_send()

        pair_copy(a).wait_send()
        pair_copy(a).wait_recv()
        local_copy(a).wait()


def gather_shards(identity, *shards):
    copies, size = lax.axis_size("dp"), lax.axis_size("fsdp")
    chips = size // 2
    shares = [copies if shard.shape[0] % (TILE * copies) == 0 else 1 for shard in shards]
    count = len(shards)
    dma = pltpu.SemaphoreType.DMA
    anywhere = pl.BlockSpec(memory_space=pl.ANY)
    return pl.pallas_call(
        functools.partial(gather_kernel, shares),
        out_shape=[
            jax.ShapeDtypeStruct((size * shard.shape[0], *shard.shape[1:]), shard.dtype)
            for shard in shards
        ],
        in_specs=[anywhere] * count,
        out_specs=[anywhere] * count,
        scratch_shapes=[
            dma((count,)),
            dma((count,)),
            dma((count,)),
            dma((count, 2, chips)),
            dma((count, 2, chips)),
            dma((count, 2, chips, copies)),
            dma((count, 2, chips, copies)),
            dma((count, 2, chips, copies)),
            dma((count, 2, chips, copies)),
        ],
        compiler_params=pltpu.CompilerParams(collective_id=identity, has_side_effects=True),
        cost_estimate=SMALL,
        name="gather_shards",
    )(*shards)


def across(number, other):
    total, bit = 0, 1
    while bit < lax.axis_size("fsdp") // 2:
        total = total + bit * ((number // bit % 2 + other // bit % 2) % 2)
        bit *= 2
    return total


def greet(place, me, chip, chips):
    mesh = pl.DeviceIdType.MESH
    barrier = pltpu.get_barrier_semaphore()
    partner = 2 * chip + 1 - me % 2
    pl.semaphore_signal(barrier, inc=1, device_id=(place, partner), device_id_type=mesh)

    @pl.when(chip > 0)
    def _():
        pl.semaphore_signal(barrier, inc=1, device_id=(place, me - 2), device_id_type=mesh)

    @pl.when(chip < chips - 1)
    def _():
        pl.semaphore_signal(barrier, inc=1, device_id=(place, me + 2), device_id_type=mesh)

    neighbours = jnp.minimum(chip, 1) + jnp.minimum(chips - 1 - chip, 1)
    pl.semaphore_wait(barrier, 1 + neighbours)


def feed_kernel(
    valid,
    hidden_ref,
    backs_ref,
    gate_ref,
    up_ref,
    down_ref,
    inner_ref,
    gate_grad_ref,
    up_grad_ref,
    rows_ref,
    back_ref,
    small_ref,
    land,
    held,
    line_send,
    line_recv,
    core_send,
    core_recv,
    own_sem,
    back_sem,
    out_sem,
):
    mesh = pl.DeviceIdType.MESH
    place, me = lax.axis_index("dp"), lax.axis_index("fsdp")
    chips = lax.axis_size("fsdp") // 2
    chip, core = me // 2, me % 2
    block = hidden_ref.shape[0]
    position, tile = pl.program_id(0), pl.program_id(1)
    tiles = pl.num_programs(1)
    source = across(chip, position)
    owners = (2 * source + core, 2 * source + 1 - core)
    slot = lax.rem(position, 2)

    def sends(side):
        return chip < chips - 1 if side == 0 else chip > 0

    def has(side, step):
        return chip >= step if side == 0 else chip + step <= chips - 1

    def line_copy(side, step):
        owner = me - 2 * step if side == 0 else me + 2 * step
        target = me + 2 if side == 0 else me - 2
        return pltpu.make_async_remote_copy(
            src_ref=land.at[owner],
            dst_ref=land.at[owner],
            send_sem=line_send.at[side, step],
            recv_sem=line_recv.at[side, step],
            device_id=(place, target),
            device_id_type=mesh,
        )

    def line_arrival(side, step):
        owner = me - 2 * step if side == 0 else me + 2 * step
        return pltpu.make_async_remote_copy(
            src_ref=land.at[owner],
            dst_ref=land.at[owner],
            send_sem=line_send.at[side, step - 1],
            recv_sem=line_recv.at[side, step - 1],
            device_id=(place, me + 2 if side == 0 else me - 2),
            device_id_type=mesh,
        )

    def core_copy(owner_chip):
        owner = 2 * owner_chip + core
        return pltpu.make_async_remote_copy(
            src_ref=land.at[owner],
            dst_ref=land.at[owner],
            send_sem=core_send.at[owner_chip],
            recv_sem=core_recv.at[owner_chip],
            device_id=(place, 2 * chip + 1 - core),
            device_id_type=mesh,
        )

    def back_copies(at):
        origin = across(chip, at)
        to = lax.rem(at, 2)
        return [
            pltpu.make_async_copy(
                backs_ref.at[pl.ds(pl.multiple_of(owner * block, TILE), block)],
                held.at[to, half],
                back_sem.at[to, half],
            )
            for half, owner in enumerate((2 * origin + core, 2 * origin + 1 - core))
        ]

    def out_copies():
        copies = []
        for half in range(2):
            where = pl.ds(pl.multiple_of((2 * position + half) * valid, TILE), valid)
            rows, back = land.at[owners[half]], held.at[slot, half]
            for source_ref, target, small in ((rows, rows_ref, 0), (back, back_ref, 1)):
                copies.append((source_ref.at[pl.ds(0, valid)], target.at[where]))
                copies.append(
                    (
                        source_ref.at[pl.ds(valid, block - valid)],
                        small_ref.at[small, position, half],
                    )
                )
        return [
            pltpu.make_async_copy(source_ref, target, out_sem.at[i])
            for i, (source_ref, target) in enumerate(copies)
        ]

    @pl.when((position == 0) & (tile == 0))
    def _():
        for copy in back_copies(0):
            copy.start()
        own = pltpu.make_async_copy(hidden_ref, land.at[me], own_sem)
        own.start()
        greet(place, me, chip, chips)
        own.wait()
        for side in range(2):

            @pl.when(sends(side))
            def _(side=side):
                line_copy(side, 0).start()

        core_copy(chip).start()

    @pl.when(tile == 0)
    def _():
        for side in range(2):

            @pl.when((position > 0) & has(side, position))
            def _(side=side):
                line_arrival(side, position).wait_recv()

                @pl.when(sends(side))
                def _():
                    line_copy(side, position).start()

                core_copy(chip - position if side == 0 else chip + position).start()

        core_copy(source).wait_recv()
        for copy in back_copies(position):
            copy.wait()
        for copy in out_copies():
            copy.start()

        @pl.when(position < chips - 1)
        def _():
            for copy in back_copies(position + 1):
                copy.start()

    root = math.sqrt(2.0 / math.pi)
    for half in range(2):
        where = slice(half * valid, (half + 1) * valid)
        rows = land[owners[half], :valid]
        back = held[slot, half, :valid]
        gate = multiply(rows, gate_ref[...])
        upper = multiply(rows, up_ref[...])
        inner_grad = multiply_right(back, down_ref[...])
        square = gate * gate
        bent = jnp.tanh(root * gate * (1.0 + 0.044715 * square))
        half_up = 0.5 + 0.5 * bent
        active = gate * half_up
        slope = half_up + (0.5 * root) * gate * (1.0 - bent * bent) * (1.0 + 0.134145 * square)
        inner_ref[where] = (active * upper).astype(LOW)
        gate_grad_ref[where] = (inner_grad * upper * slope).astype(LOW)
        up_grad_ref[where] = (inner_grad * active).astype(LOW)

    @pl.when(tile == tiles - 1)
    def _():
        for copy in out_copies():
            copy.wait()

    @pl.when((tile == tiles - 1) & (position == chips - 1))
    def _():
        for side in range(2):

            @pl.when(sends(side))
            def _(side=side):
                line_copy(side, 0).wait_send()

        for owner in range(chips):
            core_copy(owner).wait_send()

        def finish(step, _):
            for side in range(2):

                @pl.when(sends(side) & has(side, step))
                def _(side=side):
                    line_copy(side, step).wait_send()

            return 0

        lax.fori_loop(1, chips, finish, 0)


def feed_all(valid, hidden, backs, gate, up, down):
    block, width = hidden.shape
    size = lax.axis_size("fsdp")
    chips = size // 2
    units = gate.shape[1]
    tile = math.gcd(units, 512)
    column = pl.BlockSpec((width, tile), lambda p, j: (0, j))
    anywhere = pl.BlockSpec(memory_space=pl.ANY)
    total = chips * 2 * valid
    dma = pltpu.SemaphoreType.DMA
    return pl.pallas_call(
        functools.partial(feed_kernel, valid),
        out_shape=[jax.ShapeDtypeStruct((total, units), LOW)] * 3
        + [jax.ShapeDtypeStruct((total, width), LOW)] * 2
        + [jax.ShapeDtypeStruct((2, chips, 2, block - valid, width), LOW)],
        grid=(chips, units // tile),
        in_specs=[anywhere, anywhere, column, column]
        + [pl.BlockSpec((tile, width), lambda p, j: (j, 0))],
        out_specs=[pl.BlockSpec((2 * valid, tile), lambda p, j: (p, j))] * 3 + [anywhere] * 3,
        scratch_shapes=[
            pltpu.VMEM((size, block, width), LOW),
            pltpu.VMEM((2, 2, block, width), LOW),
            dma((2, chips)),
            dma((2, chips)),
            dma((chips,)),
            dma((chips,)),
            dma,
            dma((2, 2)),
            dma((8,)),
        ],
        compiler_params=pltpu.CompilerParams(
            collective_id=1, has_side_effects=True, vmem_limit_bytes=58 * MIB
        ),
        cost_estimate=SMALL,
        name="feed_all",
    )(hidden, backs, gate, up, down)


def collect_kernel(valid, transposed, count, width, *refs):
    grads, weights = refs[:count], refs[count : 2 * count]
    small_ref, total_ref = refs[2 * count : 2 * count + 2]
    mine, other, pair, arrive = refs[2 * count + 2 : 2 * count + 6]
    line_send, line_recv, core_send, core_recv = refs[2 * count + 6 :]
    mesh = pl.DeviceIdType.MESH
    place, me = lax.axis_index("dp"), lax.axis_index("fsdp")
    chips = lax.axis_size("fsdp") // 2
    chip, core = me // 2, me % 2
    turn, tile = pl.program_id(0), pl.program_id(1)
    tiles = pl.num_programs(1)
    span = small_ref.shape[-1]
    target = across(chip, chips - 1 - turn)
    slot = lax.rem(turn, 2)
    columns = pl.ds(pl.multiple_of(tile * span, 128), span)

    def core_copy(at_turn, at_tile):
        where = pl.ds(pl.multiple_of(at_tile * span, 128), span)
        owner = across(chip, chips - 1 - at_turn)
        return pltpu.make_async_remote_copy(
            src_ref=other.at[lax.rem(at_turn, 2), :, where],
            dst_ref=pair.at[owner, :, where],
            send_sem=core_send.at[lax.rem(at_turn, 2), at_tile],
            recv_sem=core_recv.at[owner, at_tile],
            device_id=(place, 2 * chip + 1 - core),
            device_id_type=mesh,
        )

    def valid_at(side, step):
        return chip <= step - 1 if side == 0 else chip >= chips - step

    def fed(side):
        return chip > 0 if side == 0 else chip < chips - 1

    def owner_at(side, step):
        return chip + chips - step if side == 0 else chip - chips + step

    def line_copy(side, step):
        return pltpu.make_async_remote_copy(
            src_ref=mine.at[owner_at(side, step)],
            dst_ref=arrive.at[side, step - 1],
            send_sem=line_send.at[side, step - 1],
            recv_sem=line_recv.at[side, step - 1],
            device_id=(place, me + 2 if side == 0 else me - 2),
            device_id_type=mesh,
        )

    def line_arrival(side, step):
        return pltpu.make_async_remote_copy(
            src_ref=mine.at[chip],
            dst_ref=arrive.at[side, step - 1],
            send_sem=line_send.at[side, step - 1],
            recv_sem=line_recv.at[side, step - 1],
            device_id=(place, me + 2 if side == 0 else me - 2),
            device_id_type=mesh,
        )

    @pl.when((turn == 0) & (tile == 0))
    def _():
        greet(place, me, chip, chips)

    @pl.when((turn > 0) & (tile == 0))
    def _():
        done = across(chip, chips - turn)

        def take(at_tile, _):
            core_copy(turn - 1, at_tile).wait_recv()
            return 0

        lax.fori_loop(0, tiles, take, 0)
        mine[done] = (mine[done].astype(FULL) + pair[done].astype(FULL)).astype(LOW)
        for side in range(2):

            @pl.when(valid_at(side, turn))
            def _(side=side):
                owner = owner_at(side, turn)

                @pl.when((turn > 1) & fed(side))
                def _():
                    line_arrival(side, turn - 1).wait_recv()
                    mine[owner] = (
                        mine[owner].astype(FULL) + arrive[side, turn - 2].astype(FULL)
                    ).astype(LOW)

                line_copy(side, turn).start()

    @pl.when(turn > 1)
    def _():
        core_copy(turn - 2, tile).wait_send()

    for half in range(2):
        where = slice(half * valid, (half + 1) * valid)
        part = None
        for grad, weight in zip(grads, weights):
            product = (multiply_right if transposed else multiply)(grad[where], weight[...])
            part = product if part is None else part + product
        if half == 0:
            mine[target, :valid, columns] = part.astype(LOW)
            mine[target, valid:, columns] = small_ref[0, 0]
        else:
            other[slot, :valid, columns] = part.astype(LOW)
            other[slot, valid:, columns] = small_ref[0, 1]
    core_copy(turn, tile).start()

    @pl.when((turn == chips - 1) & (tile == tiles - 1))
    def _():
        def take(at_tile, _):
            core_copy(turn, at_tile).wait_recv()
            core_copy(turn, at_tile).wait_send()

            @pl.when(turn > 0)
            def _():
                core_copy(turn - 1, at_tile).wait_send()

            return 0

        lax.fori_loop(0, tiles, take, 0)
        total_ref[...] = mine[chip].astype(FULL) + pair[chip].astype(FULL)
        for side in range(2):

            @pl.when(fed(side))
            def _(side=side):
                line_arrival(side, chips - 1).wait_recv()
                total_ref[...] += arrive[side, chips - 2].astype(FULL)

        def finish(step, _):
            for side in range(2):

                @pl.when(valid_at(side, step))
                def _(side=side):
                    line_copy(side, step).wait_send()

            return 0

        lax.fori_loop(1, chips, finish, 0)


def collect(identity, valid, transposed, grads, weights, small, width):
    chips = lax.axis_size("fsdp") // 2
    units = grads[0].shape[1]
    extra = small.shape[2]
    block = valid + extra
    tile = math.gcd(width, 256)
    count = len(grads)
    rows = pl.BlockSpec((2 * valid, units), lambda t, j: (chips - 1 - t, 0))
    if transposed:
        weight = pl.BlockSpec((tile, units), lambda t, j: (j, 0))
    else:
        weight = pl.BlockSpec((units, tile), lambda t, j: (0, j))
    dma = pltpu.SemaphoreType.DMA
    return pl.pallas_call(
        functools.partial(collect_kernel, valid, transposed, count, width),
        out_shape=jax.ShapeDtypeStruct((block, width), FULL),
        grid=(chips, width // tile),
        in_specs=[rows] * count
        + [weight] * count
        + [pl.BlockSpec((1, 2, extra, tile), lambda t, j: (chips - 1 - t, 0, 0, j))],
        out_specs=pl.BlockSpec((block, width), lambda t, j: (0, 0)),
        scratch_shapes=[
            pltpu.VMEM((chips, block, width), LOW),
            pltpu.VMEM((2, block, width), LOW),
            pltpu.VMEM((chips, block, width), LOW),
            pltpu.VMEM((2, chips - 1, block, width), LOW),
            dma((2, chips - 1)),
            dma((2, chips - 1)),
            dma((2, width // tile)),
            dma((chips, width // tile)),
        ],
        compiler_params=pltpu.CompilerParams(
            collective_id=identity, has_side_effects=True, vmem_limit_bytes=62 * MIB
        ),
        cost_estimate=SMALL,
        name="collect",
    )(*grads, *weights, small)


def part_kernel(valid, inner_ref, down_ref, small_ref, mine_ref, other_ref):
    for half, out in enumerate((mine_ref, other_ref)):
        where = slice(half * valid, (half + 1) * valid)
        out[0, :valid] = multiply(inner_ref[where], down_ref[...]).astype(LOW)
        out[0, valid:] = small_ref[0, half]


def part_chunks(valid, inner, down, small):
    chips, _, extra, width = small.shape
    units = inner.shape[1]
    tile = math.gcd(width, 512)
    out = pl.BlockSpec((1, valid + extra, tile), lambda p, j: (p, 0, j))
    return pl.pallas_call(
        functools.partial(part_kernel, valid),
        out_shape=[jax.ShapeDtypeStruct((chips, valid + extra, width), LOW)] * 2,
        grid=(chips, width // tile),
        in_specs=[
            pl.BlockSpec((2 * valid, units), lambda p, j: (p, 0)),
            pl.BlockSpec((units, tile), lambda p, j: (0, j)),
            pl.BlockSpec((1, 2, extra, tile), lambda p, j: (p, 0, 0, j)),
        ],
        out_specs=[out] * 2,
        compiler_params=pltpu.CompilerParams(vmem_limit_bytes=48 * MIB),
        cost_estimate=SMALL,
        name="part_chunks",
    )(inner, down, small)


def norm_back(rows, gain, grad):
    factor = lax.rsqrt(jnp.mean(rows * rows, axis=-1, keepdims=True) + EPS)
    scaled = gain * grad
    inner = jnp.mean(rows * scaled, axis=-1, keepdims=True)
    rows_grad = factor * scaled - (factor * factor * factor * inner) * rows
    return rows_grad, jnp.sum(grad * rows * factor, axis=0, keepdims=True)


def middle_kernel(grad_ref, rows_ref, back_ref, gain_ref, weight_ref, total_ref, low_ref, mixed_ref, part_ref):
    @pl.when(pl.program_id(0) == 0)
    def _():
        rows_grad, part_ref[...] = norm_back(rows_ref[...], gain_ref[...], grad_ref[...])
        total = back_ref[...].astype(FULL) + rows_grad
        total_ref[...] = total
        low_ref[...] = total.astype(LOW)

    mixed_ref[...] = multiply_right(low_ref[...], weight_ref[...]).astype(LOW)


def middle_back(grad, rows, back, gain, weight):
    count, width = rows.shape
    features = weight.shape[0]
    tile = math.gcd(features, 512)
    whole = pl.BlockSpec((count, width), lambda j: (0, 0))
    return pl.pallas_call(
        middle_kernel,
        out_shape=[
            jax.ShapeDtypeStruct((count, width), FULL),
            jax.ShapeDtypeStruct((count, width), LOW),
            jax.ShapeDtypeStruct((count, features), LOW),
            jax.ShapeDtypeStruct((1, width), FULL),
        ],
        grid=(features // tile,),
        in_specs=[whole, whole, whole, pl.BlockSpec((1, width), lambda j: (0, 0))]
        + [pl.BlockSpec((tile, width), lambda j: (j, 0))],
        out_specs=[whole, whole, pl.BlockSpec((count, tile), lambda j: (0, j))]
        + [pl.BlockSpec((1, width), lambda j: (0, 0))],
        compiler_params=pltpu.CompilerParams(vmem_limit_bytes=56 * MIB),
        cost_estimate=SMALL,
        name="middle_back",
    )(grad, rows, back, gain.reshape(1, width), weight)


def entry_kernel(query_ref, kv_ref, rows_ref, total_ref, gain_ref, weight_ref, out_ref, part_ref, held):
    tile = weight_ref.shape[0]
    where = pl.ds(pl.multiple_of(pl.program_id(0) * tile, 128), tile)
    features = query_ref.shape[1]
    held[:, where] = multiply_right(query_ref[...], weight_ref[:, :features]) + multiply_right(
        kv_ref[...], weight_ref[:, features:]
    )

    @pl.when(pl.program_id(0) == pl.num_programs(0) - 1)
    def _():
        rows_grad, part_ref[...] = norm_back(rows_ref[...], gain_ref[...], held[...])
        out_ref[...] = total_ref[...] + rows_grad


def entry_back(query_grad, kv_grad, rows, total, gain, weight):
    count, width = rows.shape
    tile = math.gcd(width, 512)
    fixed = lambda j: (0, 0)
    whole = pl.BlockSpec((count, width), fixed)
    return pl.pallas_call(
        entry_kernel,
        out_shape=[
            jax.ShapeDtypeStruct((count, width), FULL),
            jax.ShapeDtypeStruct((1, width), FULL),
        ],
        grid=(width // tile,),
        in_specs=[
            pl.BlockSpec(query_grad.shape, fixed),
            pl.BlockSpec(kv_grad.shape, fixed),
            whole,
            whole,
            pl.BlockSpec((1, width), fixed),
            pl.BlockSpec((tile, weight.shape[1]), lambda j: (j, 0)),
        ],
        out_specs=[whole, pl.BlockSpec((1, width), fixed)],
        scratch_shapes=[pltpu.VMEM((count, width), FULL)],
        compiler_params=pltpu.CompilerParams(vmem_limit_bytes=56 * MIB),
        cost_estimate=SMALL,
        name="entry_back",
    )(query_grad, kv_grad, rows, total, gain.reshape(1, width), weight)


def sum_kernel(split, *refs):
    count = len(split)
    values, totals = refs[:count], refs[count : 2 * count]
    arrived, whole = refs[2 * count : 3 * count], refs[3 * count : 4 * count]
    part_send, part_recv, whole_send, whole_recv = refs[4 * count :]
    mesh = pl.DeviceIdType.MESH
    copies = lax.axis_size("dp")
    place, me = lax.axis_index("dp"), lax.axis_index("fsdp")
    barrier = pltpu.get_barrier_semaphore()
    for k in range(1, copies):
        peer = lax.rem(place + k, copies)
        pl.semaphore_signal(barrier, inc=1, device_id=(peer, me), device_id_type=mesh)
    pl.semaphore_wait(barrier, copies - 1)

    def rows(a, owner):
        part = values[a].shape[0] // copies
        return pl.ds(pl.multiple_of(owner * part, TILE), part)

    def part_copy(a, k):
        peer = lax.rem(place + k, copies)
        return pltpu.make_async_remote_copy(
            src_ref=values[a].at[rows(a, peer)] if split[a] else values[a],
            dst_ref=arrived[a].at[k - 1] if split[a] else arrived[a].at[place],
            send_sem=part_send.at[a, k],
            recv_sem=part_recv.at[a, k],
            device_id=(peer, me),
            device_id_type=mesh,
        )

    def whole_copy(a, k):
        return pltpu.make_async_remote_copy(
            src_ref=whole[a].at[rows(a, place)],
            dst_ref=whole[a].at[rows(a, place)],
            send_sem=whole_send.at[a, k],
            recv_sem=whole_recv.at[a, k],
            device_id=(lax.rem(place + k, copies), me),
            device_id_type=mesh,
        )

    for a in range(count):
        for k in range(1, copies):
            part_copy(a, k).start()
    for a in range(count):
        if not split[a]:
            arrived[a][place] = values[a][...]
        for k in range(1, copies):
            part_copy(a, k).wait_recv()
        if split[a]:
            total = values[a][rows(a, place)].astype(FULL)
            for k in range(1, copies):
                total = total + arrived[a][k - 1].astype(FULL)
            whole[a][rows(a, place)] = total.astype(LOW)
            for k in range(1, copies):
                whole_copy(a, k).start()
        else:
            total = arrived[a][0].astype(FULL)
            for k in range(1, copies):
                total = total + arrived[a][k].astype(FULL)
            totals[a][...] = total
    for a in range(count):
        for k in range(1, copies):
            part_copy(a, k).wait_send()
            if split[a]:
                whole_copy(a, k).wait_send()
                whole_copy(a, k).wait_recv()
        if split[a]:
            totals[a][...] = whole[a][...].astype(FULL)


def sum_copies(identity, values):
    copies = lax.axis_size("dp")
    split = [value.shape[0] % (TILE * copies) == 0 for value in values]
    count = len(values)
    dma = pltpu.SemaphoreType.DMA
    arrived, whole = [], []
    for value, parts in zip(values, split):
        rows, columns = value.shape
        arrived.append((copies - 1, rows // copies, columns) if parts else (copies, rows, columns))
        whole.append((rows, columns) if parts else (TILE, 128))
    inside = pl.BlockSpec(memory_space=pltpu.VMEM)
    return pl.pallas_call(
        functools.partial(sum_kernel, split),
        out_shape=[jax.ShapeDtypeStruct(value.shape, FULL) for value in values],
        in_specs=[inside] * count,
        out_specs=[inside] * count,
        scratch_shapes=[pltpu.VMEM(shape, LOW) for shape in arrived + whole]
        + [dma((count, copies))] * 4,
        compiler_params=pltpu.CompilerParams(
            collective_id=identity, has_side_effects=True, vmem_limit_bytes=48 * MIB
        ),
        cost_estimate=SMALL,
        name="sum_copies",
    )(*values)


def widen_kernel(*refs):
    count = len(refs) - 1
    for k, ref in enumerate(refs[:-1]):

        @pl.when(pl.program_id(0) == k)
        def _(ref=ref):
            refs[-1][...] = ref[...].astype(FULL)


def widen(*values):
    count, (rows, columns) = len(values), values[0].shape
    tile = math.gcd(rows, 256)
    return pl.pallas_call(
        widen_kernel,
        out_shape=jax.ShapeDtypeStruct((count * rows, columns), FULL),
        grid=(count, rows // tile),
        in_specs=[pl.BlockSpec((tile, columns), lambda k, i: (i, 0))] * count,
        out_specs=pl.BlockSpec((tile, columns), lambda k, i: (k * (rows // tile) + i, 0)),
        compiler_params=pltpu.CompilerParams(vmem_limit_bytes=32 * MIB),
        cost_estimate=SMALL,
        name="widen",
    )(*values)


def share_kernel(per, core_ref, left_ref, right_ref, action_left_ref, action_right_ref, *refs):
    out_ref = refs[-1]
    rows = left_ref.shape[1]
    out_ref[0, :rows] = multiply_left(left_ref[...], right_ref[...]).astype(LOW)
    product = multiply_left(action_left_ref[...], action_right_ref[...])
    count = product.shape[0] // per
    small = product[:count]
    which = lax.rem(2 * pl.program_id(0) + core_ref[0], per)
    for i in range(1, per):
        small = jnp.where(which == i, product[i * count : (i + 1) * count], small)
    small = small.astype(LOW)
    fold = out_ref.shape[2] // small.shape[1]
    extra = small.shape[0] // fold
    for i in range(fold):
        columns = slice(i * small.shape[1], (i + 1) * small.shape[1])
        out_ref[0, rows : rows + extra, columns] = small[i * extra : (i + 1) * extra]
    if len(refs) > 1:
        out_ref[0, rows + extra :] = refs[0][0]


def weight_shares(core, left, right, action_left, action_right, gains=None):
    size = lax.axis_size("fsdp")
    chips = size // 2
    count, rows = left.shape[0], left.shape[1] // size
    action_count, action_rows = action_left.shape[0], action_left.shape[1] // size
    width, action_width = right.shape[1], action_right.shape[1]
    total = rows + action_rows * action_width // width
    per = max(1, 128 // action_rows)
    extra = []
    if gains is not None:
        total += gains.shape[1]
        extra = [pl.BlockSpec((1, *gains.shape[1:]), lambda c, core: (2 * c + core[0], 0, 0))]
    return pl.pallas_call(
        functools.partial(share_kernel, per),
        out_shape=jax.ShapeDtypeStruct((chips, total, width), LOW),
        grid_spec=pltpu.PrefetchScalarGridSpec(
            num_scalar_prefetch=1,
            grid=(chips,),
            in_specs=[
                pl.BlockSpec((count, rows), lambda c, core: (0, 2 * c + core[0])),
                pl.BlockSpec((count, width), lambda c, core: (0, 0)),
                pl.BlockSpec(
                    (action_count, per * action_rows), lambda c, core: (0, (2 * c + core[0]) // per)
                ),
                pl.BlockSpec((action_count, action_width), lambda c, core: (0, 0)),
            ]
            + extra,
            out_specs=pl.BlockSpec((1, total, width), lambda c, core: (c, 0, 0)),
        ),
        compiler_params=pltpu.CompilerParams(vmem_limit_bytes=48 * MIB),
        cost_estimate=SMALL,
        name="weight_shares",
    )(
        jnp.reshape(core, (1,)).astype(jnp.int32),
        left,
        right,
        action_left,
        action_right,
        *([] if gains is None else [gains]),
    )


def stacked(refs, columns=slice(None)):
    return jnp.concatenate([ref[0, :, columns] for ref in refs], axis=0)


def softmax_of(queries, keys, bias, scale):
    scores = multiply_right(queries, keys) * scale + bias
    raised = jnp.exp(scores - jnp.max(scores, axis=-1, keepdims=True))
    return raised / jnp.sum(raised, axis=-1, keepdims=True)


def greet_copies():
    copies = lax.axis_size("dp")
    place, me = lax.axis_index("dp"), lax.axis_index("fsdp")
    barrier = pltpu.get_barrier_semaphore()
    for k in range(1, copies):
        pl.semaphore_signal(
            barrier,
            inc=1,
            device_id=(lax.rem(place + k, copies), me),
            device_id_type=pl.DeviceIdType.MESH,
        )
    pl.semaphore_wait(barrier, copies - 1)


def mix_kernel(
    scale,
    features,
    prefix_ref,
    action_ref,
    prefix_all_ref,
    action_all_ref,
    bias_ref,
    prefix_out,
    action_out,
    kv_out,
    held,
    send_sem,
    recv_sem,
    out_sem,
):
    copies = lax.axis_size("dp")
    place, me = lax.axis_index("dp"), lax.axis_index("fsdp")
    item, head = pl.program_id(0), pl.program_id(1)
    items, rows = prefix_all_ref.shape[0], prefix_ref.shape[1]

    def copy(at, k):
        return pltpu.make_async_remote_copy(
            src_ref=held.at[0, at],
            dst_ref=held.at[k, at],
            send_sem=send_sem.at[at, k],
            recv_sem=recv_sem.at[at, k],
            device_id=(lax.rem(place + k, copies), me),
            device_id_type=pl.DeviceIdType.MESH,
        )

    @pl.when((item == 0) & (head == 0))
    def _():
        for at in range(items):
            held[0, at, :rows] = prefix_all_ref[at, :, features:]
            held[0, at, rows:] = action_all_ref[at, :, features:]
        greet_copies()
        for at in range(items):
            for k in range(1, copies):
                copy(at, k).start()

    @pl.when(head == 0)
    def _():
        for k in range(1, copies):
            copy(item, k).wait_recv()

    queries = stacked((prefix_ref, action_ref))
    kv = jnp.concatenate([held[k, item] for k in range(copies)], axis=0)
    head_size = kv.shape[1] // 2
    probs = softmax_of(queries, kv[:, :head_size], bias_ref[0], scale).astype(LOW)
    mixed = multiply(probs, kv[:, head_size:]).astype(LOW)
    prefix_out[0] = mixed[:rows]
    action_out[0] = mixed[rows:]

    @pl.when((item == items - 1) & (head == pl.num_programs(1) - 1))
    def _():
        whole = pltpu.make_async_copy(held, kv_out, out_sem)
        whole.start()
        for at in range(items):
            for k in range(1, copies):
                copy(at, k).wait_send()
        whole.wait()


def mix_back_kernel(
    scale,
    prefix_ref,
    action_ref,
    prefix_grad_ref,
    action_grad_ref,
    bias_ref,
    kv_ref,
    prefix_out,
    action_out,
    kv_out,
    total,
    own,
    sent,
    arrived,
    send_sem,
    recv_sem,
):
    copies = lax.axis_size("dp")
    place, me = lax.axis_index("dp"), lax.axis_index("fsdp")
    item, head = pl.program_id(0), pl.program_id(1)
    items, heads = pl.num_programs(0), pl.num_programs(1)
    rows = prefix_ref.shape[1]
    step = rows + action_ref.shape[1]

    def copy(at, k):
        return pltpu.make_async_remote_copy(
            src_ref=sent.at[at, k - 1],
            dst_ref=arrived.at[at, k - 1],
            send_sem=send_sem.at[at, k],
            recv_sem=recv_sem.at[at, k],
            device_id=(lax.rem(place + copies - k, copies), me),
            device_id_type=pl.DeviceIdType.MESH,
        )

    @pl.when((item == 0) & (head == 0))
    def _():
        greet_copies()

    @pl.when(head == 0)
    def _():
        total[...] = jnp.zeros_like(total)

    queries = stacked((prefix_ref, action_ref))
    grads = stacked((prefix_grad_ref, action_grad_ref))
    kv = jnp.concatenate([kv_ref[k, 0] for k in range(copies)], axis=0)
    head_size = kv.shape[1] // 2
    keys, values = kv[:, :head_size], kv[:, head_size:]
    probs = softmax_of(queries, keys, bias_ref[0], scale)
    probs_grad = multiply_right(grads, values)
    delta = jnp.sum(probs * probs_grad, axis=-1, keepdims=True)
    score_grad = (probs * (probs_grad - delta)).astype(LOW)
    query_grad = (multiply(score_grad, keys) * scale).astype(LOW)
    prefix_out[0] = query_grad[:rows]
    action_out[0] = query_grad[rows:]
    total[:, :head_size] += multiply_left(score_grad, queries) * scale
    total[:, head_size:] += multiply_left(probs.astype(LOW), grads)

    @pl.when(head == heads - 1)
    def _():
        own[item] = total[:step]
        for k in range(1, copies):
            sent[item, k - 1] = total[k * step : (k + 1) * step].astype(LOW)
            copy(item, k).start()

    @pl.when((item == items - 1) & (head == heads - 1))
    def _():
        for at in range(kv_out.shape[0]):
            for k in range(1, copies):
                copy(at, k).wait_recv()
                copy(at, k).wait_send()
            summed = own[at]
            for k in range(1, copies):
                summed = summed + arrived[at, k - 1].astype(FULL)
            kv_out[at] = summed.astype(LOW)


def mix_call(scale, heads, prefix, action, bias, grads=None, kv=None):
    copies = lax.axis_size("dp")
    items, prefix_rows, columns = prefix.shape
    action_rows = action.shape[1]
    rows, length = prefix_rows + action_rows, bias.shape[2]
    head_size = columns // (heads + 2)
    features = heads * head_size
    per_head = [
        pl.BlockSpec((1, prefix_rows, head_size), lambda i, h: (i, 0, h)),
        pl.BlockSpec((1, action_rows, head_size), lambda i, h: (i, 0, h)),
    ]
    bias_spec = pl.BlockSpec((1, rows, length), lambda i, h: (i, 0, 0))
    shapes = [
        jax.ShapeDtypeStruct((items, prefix_rows, features), LOW),
        jax.ShapeDtypeStruct((items, action_rows, features), LOW),
    ]
    dma = pltpu.SemaphoreType.DMA
    sems = [dma((items, copies)), dma((items, copies))]
    block = (rows, 2 * head_size)
    if grads is None:
        return pl.pallas_call(
            functools.partial(mix_kernel, scale, features),
            out_shape=shapes + [jax.ShapeDtypeStruct((copies, items, *block), LOW)],
            grid=(items, heads),
            in_specs=per_head
            + [
                pl.BlockSpec(prefix.shape, lambda i, h: (0, 0, 0)),
                pl.BlockSpec(action.shape, lambda i, h: (0, 0, 0)),
                bias_spec,
            ],
            out_specs=per_head + [pl.BlockSpec(memory_space=pl.ANY)],
            scratch_shapes=[pltpu.VMEM((copies, items, *block), LOW), *sems, dma],
            compiler_params=pltpu.CompilerParams(
                collective_id=7, has_side_effects=True, vmem_limit_bytes=48 * MIB
            ),
            cost_estimate=SMALL,
            name="mix",
        )(prefix, action, prefix, action, bias)
    return pl.pallas_call(
        functools.partial(mix_back_kernel, scale),
        out_shape=shapes + [jax.ShapeDtypeStruct((items, *block), LOW)],
        grid=(items, heads),
        in_specs=per_head * 2
        + [bias_spec, pl.BlockSpec((copies, 1, *block), lambda i, h: (0, i, 0, 0))],
        out_specs=per_head + [pl.BlockSpec((items, *block), lambda i, h: (0, 0, 0))],
        scratch_shapes=[
            pltpu.VMEM((length, 2 * head_size), FULL),
            pltpu.VMEM((items, *block), FULL),
            pltpu.VMEM((items, copies - 1, *block), LOW),
            pltpu.VMEM((items, copies - 1, *block), LOW),
            *sems,
        ],
        compiler_params=pltpu.CompilerParams(
            collective_id=8, has_side_effects=True, vmem_limit_bytes=48 * MIB
        ),
        cost_estimate=SMALL,
        name="mix_back",
    )(prefix, action, *grads, bias, kv)


def body(
    prefix_in,
    action_in,
    valid_count,
    prefix_before,
    prefix_query,
    prefix_key,
    prefix_value,
    prefix_output,
    prefix_middle,
    prefix_gate,
    prefix_up,
    prefix_down,
    action_before,
    action_query,
    action_key,
    action_value,
    action_output,
    action_middle,
    action_gate,
    action_up,
    action_down,
    prefix_cotangent,
    action_cotangent,
):
    line = Line()
    shards = line.size
    copies = lax.axis_size("dp")
    items, prefix_rows, width = prefix_in.shape
    action_rows = action_in.shape[1]
    action_width = action_in.shape[2]
    head_size = prefix_key.shape[1]
    features = prefix_query.shape[1]
    heads = features // head_size
    columns = features + 2 * head_size
    prefix_length = prefix_rows * copies
    scale = head_size ** (-0.5)
    place = lax.axis_index("dp")
    prefix_pad, action_pad = rounded(prefix_rows), rounded(action_rows)
    prefix_tokens, action_tokens = items * prefix_pad, items * action_pad
    folded = action_tokens * action_width // width
    folded_pad = rounded(folded)

    def padded(prefix, action):
        prefix = jnp.pad(prefix, ((0, 0), (0, prefix_pad - prefix_rows), (0, 0)))
        action = jnp.pad(action, ((0, 0), (0, action_pad - action_rows), (0, 0)))
        return prefix.reshape(prefix_tokens, width), action.reshape(action_tokens, action_width)

    def trimmed(prefix, action):
        prefix = prefix.reshape(items, prefix_pad, width)[:, :prefix_rows]
        return prefix, action.reshape(items, action_pad, action_width)[:, :action_rows]

    def fold(action):
        rows = action.reshape(-1, folded, width)
        return jnp.pad(rows, ((0, 0), (0, folded_pad - folded), (0, 0)))

    def unfold(rows):
        return rows[:folded].reshape(action_tokens, action_width)

    def pack(prefix, action):
        return jnp.concatenate([prefix, fold(action)[0]], axis=0)

    def unpack(packed):
        return packed[:prefix_tokens], unfold(packed[prefix_tokens:])

    share, action_share = prefix_before.shape[0], action_before.shape[0]
    cuts = [0, share, 2 * share, 2 * share + action_share, 2 * share + 2 * action_share]
    gain_rows = rounded(-(-cuts[4] // 128))
    gains = jnp.concatenate([prefix_before, prefix_middle, action_before, action_middle])
    gains = jnp.pad(gains, (0, gain_rows * 128 - cuts[4])).reshape(gain_rows, 128)
    prefix_qkv, action_qkv, gains = gather_shards(
        0,
        jnp.concatenate([prefix_query, prefix_key, prefix_value], axis=1),
        jnp.concatenate([action_query, action_key, action_value], axis=1),
        gains,
    )
    gains = gains.reshape(shards, gain_rows * 128).astype(FULL)
    prefix_gain_in, prefix_gain, action_gain_in, action_gain = (
        gains[:, cuts[i] : cuts[i + 1]].reshape(-1) for i in range(4)
    )

    live = (place * action_rows + jnp.arange(action_rows))[None, :] < valid_count[:, None]
    prefix_back, action_back = padded(
        prefix_cotangent,
        jnp.where(live[:, :, None], action_cotangent, jnp.zeros_like(action_cotangent)),
    )
    backs = lax.all_gather(pack(prefix_back, action_back), "fsdp", axis=0, tiled=True)

    prefix_flat, action_flat = padded(prefix_in.astype(FULL), action_in.astype(FULL))
    prefix_hidden = normalize(prefix_flat, prefix_gain_in).astype(LOW)
    action_hidden = normalize(action_flat, action_gain_in).astype(LOW)
    prefix_all = multiply(prefix_hidden, prefix_qkv).astype(LOW)
    prefix_all = prefix_all.reshape(items, prefix_pad, columns)
    action_all = multiply(action_hidden, action_qkv).astype(LOW)
    action_all = action_all.reshape(items, action_pad, columns)
    far = copies * (prefix_rows + action_rows)

    def places(owner):
        prefix = jnp.arange(prefix_pad)
        action = jnp.arange(action_pad)
        return jnp.concatenate(
            [
                jnp.where(prefix < prefix_rows, owner * prefix_rows + prefix, far),
                jnp.where(
                    action < action_rows, prefix_length + owner * action_rows + action, far
                ),
            ]
        )

    query_place = places(place)
    key_place = jnp.concatenate([places((place + copies - k) % copies) for k in range(copies)])
    later = (query_place[:, None] >= prefix_length) & (key_place[None, :] <= query_place[:, None])
    allowed = (key_place[None, None, :] < prefix_length) | later[None] & (
        key_place[None, None, :] < prefix_length + valid_count[:, None, None]
    )
    bias = jnp.where(allowed, 0.0, NEGATIVE).astype(FULL)
    prefix_mixed, action_mixed, kv = mix_call(scale, heads, prefix_all, action_all, bias)
    backs, prefix_output, action_output, _ = lax.optimization_barrier(
        (backs, prefix_output, action_output, prefix_mixed)
    )
    prefix_o, action_o = gather_shards(4, prefix_output, action_output)

    prefix_mixed = prefix_mixed.reshape(prefix_tokens, features)
    action_mixed = action_mixed.reshape(action_tokens, features)
    prefix_mid = prefix_flat + multiply(prefix_mixed, prefix_o)
    action_mid = action_flat + multiply(action_mixed, action_o)

    hidden = pack(
        normalize(prefix_mid, prefix_gain).astype(LOW),
        normalize(action_mid, action_gain).astype(LOW),
    )
    inner, gate_grad, up_grad, all_rows, all_back, small = feed_all(
        prefix_tokens, hidden, backs, prefix_gate, prefix_up, prefix_down
    )
    action_rows_all, action_back_all = (
        small[i, :, :, :folded].reshape(shards * action_tokens, action_width) for i in range(2)
    )
    action_inner, pull = jax.vjp(
        activate, multiply(action_rows_all, action_gate), multiply(action_rows_all, action_up)
    )
    action_inner = action_inner.astype(LOW)
    action_gate_grad, action_up_grad = (
        v.astype(LOW) for v in pull(multiply_right(action_back_all, action_down))
    )

    down_grad = multiply_left(inner, all_back).astype(LOW)
    action_feed = tuple(
        v.astype(LOW)
        for v in (
            multiply_left(action_rows_all, action_gate_grad),
            multiply_left(action_rows_all, action_up_grad),
            multiply_left(action_inner, action_back_all),
        )
    )
    gate_weight_grad = multiply_left(all_rows, gate_grad).astype(LOW)
    gate_grad, up_grad, down_grad, gate_weight_grad = lax.optimization_barrier(
        (gate_grad, up_grad, down_grad, gate_weight_grad)
    )
    def halves(rows):
        return fold(rows.astype(LOW)).reshape(line.chips, 2, folded_pad, width)

    up_weight_grad = multiply_left(all_rows, up_grad).astype(LOW)
    gate_grad, up_grad, down_grad, gate_weight_grad, up_weight_grad, action_feed = (
        lax.optimization_barrier(
            (gate_grad, up_grad, down_grad, gate_weight_grad, up_weight_grad, action_feed)
        )
    )
    feed_sums = lax.psum((down_grad, gate_weight_grad, up_weight_grad, *action_feed), "dp")
    small = halves(
        multiply_right(action_gate_grad, action_gate) + multiply_right(action_up_grad, action_up)
    )
    feed_back = collect(
        2, prefix_tokens, True, (gate_grad, up_grad), (prefix_gate, prefix_up), small, width
    )
    feed_back, inner = lax.optimization_barrier((unpack(feed_back), inner))

    prefix_mid_grad, prefix_low, prefix_mixed_grad, prefix_middle_part = middle_back(
        feed_back[0], prefix_mid, prefix_back, prefix_gain, prefix_o
    )
    action_mid_grad, action_low, action_mixed_grad, action_middle_part = middle_back(
        feed_back[1], action_mid, action_back, action_gain, action_o
    )
    sent = line.pairs(9, prefix_mixed, prefix_low, action_mixed, action_low)
    output_sums = Relay(line, sent, lambda chip: chip)
    output_sums.advance(1)
    parts = part_chunks(
        prefix_tokens,
        lax.optimization_barrier((inner, sent))[0],
        prefix_down,
        halves(multiply(action_inner, action_down)),
    )
    sent = add_pairs(11, *parts)
    sent, mixed_grads = lax.optimization_barrier((sent, (prefix_mixed_grad, action_mixed_grad)))
    prefix_mixed_grad, action_mixed_grad = mixed_grads
    out_sums = Relay(line, sent, lambda chip: line.chip ^ chip)
    out_sums.advance(1)
    prefix_mixed_grad = output_sums.after(prefix_mixed_grad)
    output_sums.advance(2)
    mixed_grads = (
        prefix_mixed_grad.reshape(items, prefix_pad, features),
        action_mixed_grad.reshape(items, action_pad, features),
    )
    prefix_query_grad, action_query_grad, kv_grad = mix_call(
        scale, heads, prefix_all, action_all, bias, mixed_grads, kv
    )
    kv_grad = output_sums.after(out_sums.after(kv_grad))
    out_sums.advance(2)
    output_sums.advance(3)
    prefix_qkv_grad = jnp.concatenate([prefix_query_grad, kv_grad[:, :prefix_pad]], axis=2)
    action_qkv_grad = jnp.concatenate([action_query_grad, kv_grad[:, prefix_pad:]], axis=2)
    prefix_qkv_grad = prefix_qkv_grad.reshape(prefix_tokens, columns)
    action_qkv_grad = action_qkv_grad.reshape(action_tokens, columns)
    prefix_grad, prefix_before_part = entry_back(
        prefix_query_grad.reshape(prefix_tokens, features),
        kv_grad[:, :prefix_pad].reshape(prefix_tokens, 2 * head_size),
        prefix_flat,
        prefix_mid_grad,
        prefix_gain_in,
        prefix_qkv,
    )
    action_grad, action_before_part = entry_back(
        action_query_grad.reshape(action_tokens, features),
        kv_grad[:, prefix_pad:].reshape(action_tokens, 2 * head_size),
        action_flat,
        action_mid_grad,
        action_gain_in,
        action_qkv,
    )
    prefix_grad, action_grad = trimmed(prefix_grad, action_grad)

    gain_parts = jnp.concatenate(
        [
            part.reshape(shards, -1)
            for part in (
                prefix_before_part,
                prefix_middle_part,
                action_before_part,
                action_middle_part,
            )
        ],
        axis=1,
    )
    gain_rows = rounded(-(-cuts[4] // columns))
    gain_parts = jnp.pad(gain_parts, ((0, 0), (0, gain_rows * columns - cuts[4])))
    gain_parts = gain_parts.astype(LOW).reshape(shards, gain_rows, columns)
    sent = line.pairs(
        10, prefix_hidden, prefix_qkv_grad, action_hidden, action_qkv_grad, gain_parts
    )
    qkv_sums = Relay(line, out_sums.after(sent), lambda chip: chip)
    out_sums.advance(3)
    qkv_sums.advance(1)
    output_owned = output_sums.finish()
    qkv_sums.arrived, output_owned = out_sums.after((qkv_sums.arrived, output_owned))
    qkv_sums.advance(2)
    rows, output_rows = prefix_query.shape[0], prefix_output.shape[0]
    folded_rows = output_owned[output_rows:]
    folded_rows = jnp.concatenate(
        [folded_rows[:, i : i + action_width] for i in range(0, width, action_width)], axis=0
    )
    output_owned, action_output_owned = sum_copies(
        6, [output_owned[:output_rows].astype(LOW), folded_rows.astype(LOW)]
    )
    feed_sums, output_owned = qkv_sums.after((feed_sums, output_owned))
    qkv_sums.advance(3)
    sums = unpack(out_sums.finish())
    prefix_out, action_out = trimmed(
        (prefix_mid + sums[0]).astype(LOW), (action_mid + sums[1]).astype(LOW)
    )
    qkv_owned = qkv_sums.finish()
    gain_start = rows + action_query.shape[0]
    qkv_owned, action_qkv_owned, gain_owned = sum_copies(
        12,
        [
            qkv_owned[:rows].astype(LOW),
            qkv_owned[rows:gain_start].astype(LOW),
            qkv_owned[gain_start:].reshape(TILE * copies, -1).astype(LOW),
        ],
    )
    gain_owned = gain_owned.reshape(-1)
    return (
        prefix_out,
        action_out,
        prefix_grad,
        action_grad,
        gain_owned[cuts[0] : cuts[1]],
        qkv_owned[:rows, :features],
        qkv_owned[:rows, features : features + head_size],
        qkv_owned[:rows, features + head_size :],
        output_owned,
        gain_owned[cuts[1] : cuts[2]],
        widen(feed_sums[1]),
        widen(feed_sums[2]),
        widen(feed_sums[0]),
        gain_owned[cuts[2] : cuts[3]],
        action_qkv_owned[:, :features],
        action_qkv_owned[:, features : features + head_size],
        action_qkv_owned[:, features + head_size :],
        action_output_owned,
        gain_owned[cuts[3] : cuts[4]],
        *(widen(v) for v in feed_sums[3:]),
    )


def solution(mesh):
    tokens = P("fsdp", "dp", None)
    rows, columns, vector = P("fsdp", None), P(None, "fsdp"), P("fsdp")
    weights = (vector, rows, rows, rows, rows, vector, columns, columns, rows)
    return jax.shard_map(
        body,
        mesh=mesh,
        in_specs=(tokens, tokens, vector, *weights, *weights, tokens, tokens),
        out_specs=(tokens, tokens, tokens, tokens, *weights, *weights),
        check_vma=False,
    )
```

```python
import functools
import math

import jax
import jax.numpy as jnp
from jax import lax
from jax.experimental import pallas as pl
from jax.experimental.pallas import tpu as pltpu
from jax.sharding import PartitionSpec as P

EPS = 1e-06
NEGATIVE = -1e30
LOW = jnp.bfloat16
FULL = jnp.float32
TILE = 16
MIB = 1 << 20
SMALL = pl.CostEstimate(flops=1, bytes_accessed=1, transcendentals=0)


def normalize(rows, gain):
    return rows * lax.rsqrt(jnp.mean(rows * rows, axis=-1, keepdims=True) + EPS) * gain


def multiply(left, right):
    return jnp.dot(left, right, preferred_element_type=FULL)


def multiply_left(left, right):
    return lax.dot_general(
        left, right, (((0,), (0,)), ((), ())), preferred_element_type=FULL
    )


def multiply_right(left, right):
    return lax.dot_general(
        left, right, (((1,), (1,)), ((), ())), preferred_element_type=FULL
    )


def activate(gate, upper):
    return jax.nn.gelu(gate, approximate=True) * upper


class Line:
    def __init__(self):
        self.size = lax.axis_size("fsdp")
        self.chips = self.size // 2
        self.place = lax.axis_index("fsdp")
        self.chip = self.place // 2
        self.core = self.place % 2

    def move(self, value, chips, step):
        pairs = [
            (2 * chip + core, 2 * (chip + step) + core) for chip in chips for core in range(2)
        ]
        return lax.ppermute(value, "fsdp", pairs)

    def pairs(self, identity, *values):
        mine, other = (weight_shares(core, *values) for core in (self.core, 1 - self.core))
        return add_pairs(identity, mine, other)


class Relay:
    def __init__(self, line, summed, index):
        self.line, self.summed, self.index = line, summed, index
        self.taken, self.arrived = 0, []

    def advance(self, part, parts=3):
        line, count = self.line, self.line.chips
        last = -(-(count - 1) * part // parts)
        while self.taken < last:
            self.taken += 1
            step, arrived = self.taken, self.arrived
            self.arrived = []
            for i, side in enumerate((1, -1)):
                target = self.index(jnp.clip(line.chip + side * (count - step), 0, count - 1))
                if arrived:
                    payload = add_block(self.summed, target, [arrived[i]], LOW)
                else:
                    payload = lax.dynamic_index_in_dim(self.summed, target, 0, keepdims=False)
                chips = range(0, step) if side == 1 else range(count - step, count)
                self.arrived.append(line.move(payload, chips, side))

    def after(self, values):
        self.arrived, values = lax.optimization_barrier((self.arrived, values))
        return values

    def finish(self):
        self.advance(1, 1)
        return add_block(self.summed, self.index(self.line.chip), self.arrived, FULL)


def add_kernel(index_ref, value_ref, *refs):
    total = value_ref[0].astype(FULL)
    for ref in refs[:-1]:
        total = total + ref[...].astype(FULL)
    refs[-1][...] = total.astype(refs[-1].dtype)


def add_block(values, index, others, kind):
    shape = values.shape[1:]
    block = pl.BlockSpec(shape, lambda i, index: (0, 0))
    return pl.pallas_call(
        add_kernel,
        out_shape=jax.ShapeDtypeStruct(shape, kind),
        grid_spec=pltpu.PrefetchScalarGridSpec(
            num_scalar_prefetch=1,
            grid=(1,),
            in_specs=[pl.BlockSpec((1, *shape), lambda i, index: (index[0], 0, 0))]
            + [block] * len(others),
            out_specs=block,
        ),
        compiler_params=pltpu.CompilerParams(vmem_limit_bytes=40 * MIB),
        cost_estimate=SMALL,
        name="add_block",
    )(jnp.reshape(index, (1,)).astype(jnp.int32), values, *others)


def pair_kernel(mine_ref, other_ref, out_ref, landed, send_sem, recv_sem):
    place, me = lax.axis_index("dp"), lax.axis_index("fsdp")
    partner = (place, me + 1 - 2 * (me % 2))
    mesh = pl.DeviceIdType.MESH
    turn, count = pl.program_id(0), landed.shape[0]

    def copy(at):
        return pltpu.make_async_remote_copy(
            src_ref=other_ref.at[at],
            dst_ref=landed.at[at],
            send_sem=send_sem.at[at],
            recv_sem=recv_sem.at[at],
            device_id=partner,
            device_id_type=mesh,
        )

    @pl.when(turn == 0)
    def _():
        barrier = pltpu.get_barrier_semaphore()
        pl.semaphore_signal(barrier, inc=1, device_id=partner, device_id_type=mesh)
        pl.semaphore_wait(barrier, 1)
        for at in range(count):
            copy(at).start()

    copy(turn).wait_recv()
    out_ref[0] = (mine_ref[0].astype(FULL) + landed[turn].astype(FULL)).astype(LOW)

    @pl.when(turn == count - 1)
    def _():
        for at in range(count):
            copy(at).wait_send()


def add_pairs(identity, mine, other):
    count, shape = mine.shape[0], mine.shape[1:]
    block = pl.BlockSpec((1, *shape), lambda i: (i, 0, 0))
    dma = pltpu.SemaphoreType.DMA
    return pl.pallas_call(
        pair_kernel,
        out_shape=jax.ShapeDtypeStruct(mine.shape, LOW),
        grid=(count,),
        in_specs=[block, pl.BlockSpec(memory_space=pl.ANY)],
        out_specs=block,
        scratch_shapes=[pltpu.VMEM(mine.shape, LOW), dma((count,)), dma((count,))],
        compiler_params=pltpu.CompilerParams(
            collective_id=identity, has_side_effects=True, vmem_limit_bytes=40 * MIB
        ),
        cost_estimate=SMALL,
        name="add_pairs",
    )(mine, other)


def rounded(count, unit=TILE):
    return -(-count // unit) * unit


class Gather:
    def __init__(self, shares, shards, wholes, sems):
        self.shares, self.shards, self.wholes = shares, shards, wholes
        self.local_sem, self.pair_send, self.pair_recv = sems[:3]
        self.line_send, self.line_recv, self.copy_send, self.copy_recv = sems[3:7]
        self.core_send, self.core_recv = sems[7:]
        self.copies, self.place = lax.axis_size("dp"), lax.axis_index("dp")
        self.chips, self.me = lax.axis_size("fsdp") // 2, lax.axis_index("fsdp")
        self.chip, self.core = self.me // 2, self.me % 2
        self.partner = 2 * self.chip + 1 - self.core

    @staticmethod
    def scratch(count):
        dma = pltpu.SemaphoreType.DMA
        copies, chips = lax.axis_size("dp"), lax.axis_size("fsdp") // 2
        return (
            [dma((count,))] * 3 + [dma((count, 2, chips))] * 2 + [dma((count, 2, chips, copies))] * 4
        )

    def greet(self):
        mesh = pl.DeviceIdType.MESH
        place, me, chip = self.place, self.me, self.chip
        barrier = pltpu.get_barrier_semaphore()
        pl.semaphore_signal(barrier, inc=1, device_id=(place, self.partner), device_id_type=mesh)
        for k in range(1, self.copies):
            peer = lax.rem(place + k, self.copies)
            pl.semaphore_signal(barrier, inc=1, device_id=(peer, me), device_id_type=mesh)

        @pl.when(chip > 0)
        def _():
            pl.semaphore_signal(barrier, inc=1, device_id=(place, me - 2), device_id_type=mesh)

        @pl.when(chip < self.chips - 1)
        def _():
            pl.semaphore_signal(barrier, inc=1, device_id=(place, me + 2), device_id_type=mesh)

        neighbours = jnp.minimum(chip, 1) + jnp.minimum(self.chips - 1 - chip, 1)
        pl.semaphore_wait(barrier, self.copies + neighbours)

    def rows(self, a, owner, share):
        whole = self.shards[a].shape[0]
        part = whole // self.shares[a]
        return pl.ds(pl.multiple_of(owner * whole + share * part, TILE), part)

    def remote(self, source, target, send, recv, device):
        return pltpu.make_async_remote_copy(
            src_ref=source,
            dst_ref=target,
            send_sem=send,
            recv_sem=recv,
            device_id=device,
            device_id_type=pl.DeviceIdType.MESH,
        )

    def my_share(self, a):
        return self.place if self.shares[a] > 1 else 0

    def peers(self, a):
        return range(1, self.copies) if self.shares[a] > 1 else range(0)

    def owner_of(self, side, step):
        return self.me - 2 * step if side == 0 else self.me + 2 * step

    def sends(self, side):
        return self.chip < self.chips - 1 if side == 0 else self.chip > 0

    def has(self, side, step):
        return self.chip >= step if side == 0 else self.chip + step <= self.chips - 1

    def line_copy(self, a, side, step):
        where = self.rows(a, self.owner_of(side, step), self.my_share(a))
        target = self.me + 2 if side == 0 else self.me - 2
        return self.remote(
            self.wholes[a].at[where],
            self.wholes[a].at[where],
            self.line_send.at[a, side, step],
            self.line_recv.at[a, side, step],
            (self.place, target),
        )

    def first_copy(self, a, side):
        part = self.shards[a].shape[0] // self.shares[a]
        target = self.me + 2 if side == 0 else self.me - 2
        return self.remote(
            self.shards[a].at[pl.ds(pl.multiple_of(self.my_share(a) * part, TILE), part)],
            self.wholes[a].at[self.rows(a, self.me, self.my_share(a))],
            self.line_send.at[a, side, 0],
            self.line_recv.at[a, side, 0],
            (self.place, target),
        )

    def peer_copy(self, a, side, step, k):
        where = self.rows(a, self.owner_of(side, step), self.place)
        return self.remote(
            self.wholes[a].at[where],
            self.wholes[a].at[where],
            self.copy_send.at[a, side, step, k],
            self.copy_recv.at[a, side, step, k],
            (lax.rem(self.place + k, self.copies), self.me),
        )

    def core_copy(self, a, side, step, k):
        share = lax.rem(self.place + self.copies - k, self.copies) if self.shares[a] > 1 else 0
        where = self.rows(a, self.owner_of(side, step), share)
        return self.remote(
            self.wholes[a].at[where],
            self.wholes[a].at[where],
            self.core_send.at[a, side, step, k],
            self.core_recv.at[a, side, step, k],
            (self.place, self.partner),
        )

    def rows_all(self, a):
        whole = self.shards[a].shape[0]
        return pl.ds(pl.multiple_of(self.me * whole, TILE), whole)

    def pair_copy(self, a):
        return self.remote(
            self.shards[a],
            self.wholes[a].at[self.rows_all(a)],
            self.pair_send.at[a],
            self.pair_recv.at[a],
            (self.place, self.partner),
        )

    def local_copy(self, a):
        return pltpu.make_async_copy(
            self.shards[a], self.wholes[a].at[self.rows_all(a)], self.local_sem.at[a]
        )

    def start(self):
        for a in range(len(self.shards)):
            for side in range(2):

                @pl.when(self.sends(side))
                def _(a=a, side=side):
                    self.first_copy(a, side).start()

        for a in range(len(self.shards)):
            self.pair_copy(a).start()
            self.local_copy(a).start()

    def hand_over(self, a, side, step):
        for k in self.peers(a):
            self.peer_copy(a, side, step, k).wait_recv()
            self.core_copy(a, side, step, k).start()

    def advance(self, step):
        for a in range(len(self.shards)):
            for side in range(2):

                @pl.when(self.has(side, step))
                def _(a=a, side=side):
                    self.line_copy(a, side, step - 1).wait_recv()

                    @pl.when(self.sends(side))
                    def _():
                        self.line_copy(a, side, step).start()

                    for k in self.peers(a):
                        self.peer_copy(a, side, step, k).start()
                    self.core_copy(a, side, step, 0).start()

        for a in range(len(self.shards)):
            for side in range(2):

                @pl.when((step > 1) & self.has(side, step - 1))
                def _(a=a, side=side):
                    self.hand_over(a, side, step - 1)

    def finish(self):
        last = self.chips - 1
        for a in range(len(self.shards)):
            for side in range(2):

                @pl.when(self.has(side, last))
                def _(a=a, side=side):
                    self.hand_over(a, side, last)

        def settle(step, _):
            for a in range(len(self.shards)):
                for side in range(2):

                    @pl.when(self.has(side, step))
                    def _(a=a, side=side):
                        @pl.when(self.sends(side))
                        def _():
                            self.line_copy(a, side, step).wait_send()

                        for k in self.peers(a):
                            self.peer_copy(a, side, step, k).wait_send()
                            self.core_copy(a, side, step, k).wait_send()
                            self.core_copy(a, side, step, k).wait_recv()
                        self.core_copy(a, side, step, 0).wait_send()
                        self.core_copy(a, side, step, 0).wait_recv()

            return 0

        lax.fori_loop(1, self.chips, settle, 0)
        for a in range(len(self.shards)):
            for side in range(2):

                @pl.when(self.sends(side))
                def _(a=a, side=side):
                    self.first_copy(a, side).wait_send()

            self.pair_copy(a).wait_send()
            self.pair_copy(a).wait_recv()
            self.local_copy(a).wait()


def shares_of(shards):
    copies = lax.axis_size("dp")
    return [copies if shard.shape[0] % (TILE * copies) == 0 else 1 for shard in shards]


def whole_shapes(shards):
    size = lax.axis_size("fsdp")
    return [jax.ShapeDtypeStruct((size * s.shape[0], *s.shape[1:]), s.dtype) for s in shards]


def gather_kernel(shares, *refs):
    count = len(shares)
    gather = Gather(shares, refs[:count], refs[count : 2 * count], refs[2 * count :])
    gather.greet()
    gather.start()

    def advance(step, _):
        gather.advance(step)
        return 0

    lax.fori_loop(1, gather.chips, advance, 0)
    gather.finish()


def gather_shards(identity, *shards):
    count = len(shards)
    anywhere = pl.BlockSpec(memory_space=pl.ANY)
    return pl.pallas_call(
        functools.partial(gather_kernel, shares_of(shards)),
        out_shape=whole_shapes(shards),
        in_specs=[anywhere] * count,
        out_specs=[anywhere] * count,
        scratch_shapes=Gather.scratch(count),
        compiler_params=pltpu.CompilerParams(collective_id=identity, has_side_effects=True),
        cost_estimate=SMALL,
        name="gather_shards",
    )(*shards)


def across(number, other):
    total, bit = 0, 1
    while bit < lax.axis_size("fsdp") // 2:
        total = total + bit * ((number // bit % 2 + other // bit % 2) % 2)
        bit *= 2
    return total


def greet(place, me, chip, chips):
    mesh = pl.DeviceIdType.MESH
    barrier = pltpu.get_barrier_semaphore()
    partner = 2 * chip + 1 - me % 2
    pl.semaphore_signal(barrier, inc=1, device_id=(place, partner), device_id_type=mesh)

    @pl.when(chip > 0)
    def _():
        pl.semaphore_signal(barrier, inc=1, device_id=(place, me - 2), device_id_type=mesh)

    @pl.when(chip < chips - 1)
    def _():
        pl.semaphore_signal(barrier, inc=1, device_id=(place, me + 2), device_id_type=mesh)

    neighbours = jnp.minimum(chip, 1) + jnp.minimum(chips - 1 - chip, 1)
    pl.semaphore_wait(barrier, 1 + neighbours)


def feed_kernel(
    valid,
    hidden_ref,
    backs_ref,
    gate_ref,
    up_ref,
    down_ref,
    inner_ref,
    gate_grad_ref,
    up_grad_ref,
    rows_ref,
    back_ref,
    small_ref,
    land,
    held,
    line_send,
    line_recv,
    core_send,
    core_recv,
    own_sem,
    back_sem,
    out_sem,
):
    mesh = pl.DeviceIdType.MESH
    place, me = lax.axis_index("dp"), lax.axis_index("fsdp")
    chips = lax.axis_size("fsdp") // 2
    chip, core = me // 2, me % 2
    block = hidden_ref.shape[0]
    position, tile = pl.program_id(0), pl.program_id(1)
    tiles = pl.num_programs(1)
    source = across(chip, position)
    owners = (2 * source + core, 2 * source + 1 - core)
    slot = lax.rem(position, 2)

    def sends(side):
        return chip < chips - 1 if side == 0 else chip > 0

    def has(side, step):
        return chip >= step if side == 0 else chip + step <= chips - 1

    def line_copy(side, step):
        owner = me - 2 * step if side == 0 else me + 2 * step
        target = me + 2 if side == 0 else me - 2
        return pltpu.make_async_remote_copy(
            src_ref=land.at[owner],
            dst_ref=land.at[owner],
            send_sem=line_send.at[side, step],
            recv_sem=line_recv.at[side, step],
            device_id=(place, target),
            device_id_type=mesh,
        )

    def line_arrival(side, step):
        owner = me - 2 * step if side == 0 else me + 2 * step
        return pltpu.make_async_remote_copy(
            src_ref=land.at[owner],
            dst_ref=land.at[owner],
            send_sem=line_send.at[side, step - 1],
            recv_sem=line_recv.at[side, step - 1],
            device_id=(place, me + 2 if side == 0 else me - 2),
            device_id_type=mesh,
        )

    def core_copy(owner_chip):
        owner = 2 * owner_chip + core
        return pltpu.make_async_remote_copy(
            src_ref=land.at[owner],
            dst_ref=land.at[owner],
            send_sem=core_send.at[owner_chip],
            recv_sem=core_recv.at[owner_chip],
            device_id=(place, 2 * chip + 1 - core),
            device_id_type=mesh,
        )

    def back_copies(at):
        origin = across(chip, at)
        to = lax.rem(at, 2)
        return [
            pltpu.make_async_copy(
                backs_ref.at[pl.ds(pl.multiple_of(owner * block, TILE), block)],
                held.at[to, half],
                back_sem.at[to, half],
            )
            for half, owner in enumerate((2 * origin + core, 2 * origin + 1 - core))
        ]

    def out_copies():
        copies = []
        for half in range(2):
            where = pl.ds(pl.multiple_of((2 * position + half) * valid, TILE), valid)
            rows, back = land.at[owners[half]], held.at[slot, half]
            for source_ref, target, small in ((rows, rows_ref, 0), (back, back_ref, 1)):
                copies.append((source_ref.at[pl.ds(0, valid)], target.at[where]))
                copies.append(
                    (
                        source_ref.at[pl.ds(valid, block - valid)],
                        small_ref.at[small, position, half],
                    )
                )
        return [
            pltpu.make_async_copy(source_ref, target, out_sem.at[i])
            for i, (source_ref, target) in enumerate(copies)
        ]

    @pl.when((position == 0) & (tile == 0))
    def _():
        for copy in back_copies(0):
            copy.start()
        own = pltpu.make_async_copy(hidden_ref, land.at[me], own_sem)
        own.start()
        greet(place, me, chip, chips)
        own.wait()
        for side in range(2):

            @pl.when(sends(side))
            def _(side=side):
                line_copy(side, 0).start()

        core_copy(chip).start()

    @pl.when(tile == 0)
    def _():
        for side in range(2):

            @pl.when((position > 0) & has(side, position))
            def _(side=side):
                line_arrival(side, position).wait_recv()

                @pl.when(sends(side))
                def _():
                    line_copy(side, position).start()

                core_copy(chip - position if side == 0 else chip + position).start()

        core_copy(source).wait_recv()
        for copy in back_copies(position):
            copy.wait()
        for copy in out_copies():
            copy.start()

        @pl.when(position < chips - 1)
        def _():
            for copy in back_copies(position + 1):
                copy.start()

    root = math.sqrt(2.0 / math.pi)
    for half in range(2):
        where = slice(half * valid, (half + 1) * valid)
        rows = land[owners[half], :valid]
        back = held[slot, half, :valid]
        gate = multiply(rows, gate_ref[...])
        upper = multiply(rows, up_ref[...])
        inner_grad = multiply_right(back, down_ref[...])
        square = gate * gate
        bent = jnp.tanh(root * gate * (1.0 + 0.044715 * square))
        half_up = 0.5 + 0.5 * bent
        active = gate * half_up
        slope = half_up + (0.5 * root) * gate * (1.0 - bent * bent) * (1.0 + 0.134145 * square)
        inner_ref[where] = (active * upper).astype(LOW)
        gate_grad_ref[where] = (inner_grad * upper * slope).astype(LOW)
        up_grad_ref[where] = (inner_grad * active).astype(LOW)

    @pl.when(tile == tiles - 1)
    def _():
        for copy in out_copies():
            copy.wait()

    @pl.when((tile == tiles - 1) & (position == chips - 1))
    def _():
        for side in range(2):

            @pl.when(sends(side))
            def _(side=side):
                line_copy(side, 0).wait_send()

        for owner in range(chips):
            core_copy(owner).wait_send()

        def finish(step, _):
            for side in range(2):

                @pl.when(sends(side) & has(side, step))
                def _(side=side):
                    line_copy(side, step).wait_send()

            return 0

        lax.fori_loop(1, chips, finish, 0)


def feed_all(valid, hidden, backs, gate, up, down):
    block, width = hidden.shape
    size = lax.axis_size("fsdp")
    chips = size // 2
    units = gate.shape[1]
    tile = math.gcd(units, 512)
    column = pl.BlockSpec((width, tile), lambda p, j: (0, j))
    anywhere = pl.BlockSpec(memory_space=pl.ANY)
    total = chips * 2 * valid
    dma = pltpu.SemaphoreType.DMA
    return pl.pallas_call(
        functools.partial(feed_kernel, valid),
        out_shape=[jax.ShapeDtypeStruct((total, units), LOW)] * 3
        + [jax.ShapeDtypeStruct((total, width), LOW)] * 2
        + [jax.ShapeDtypeStruct((2, chips, 2, block - valid, width), LOW)],
        grid=(chips, units // tile),
        in_specs=[anywhere, anywhere, column, column]
        + [pl.BlockSpec((tile, width), lambda p, j: (j, 0))],
        out_specs=[pl.BlockSpec((2 * valid, tile), lambda p, j: (p, j))] * 3 + [anywhere] * 3,
        scratch_shapes=[
            pltpu.VMEM((size, block, width), LOW),
            pltpu.VMEM((2, 2, block, width), LOW),
            dma((2, chips)),
            dma((2, chips)),
            dma((chips,)),
            dma((chips,)),
            dma,
            dma((2, 2)),
            dma((8,)),
        ],
        compiler_params=pltpu.CompilerParams(
            collective_id=1, has_side_effects=True, vmem_limit_bytes=58 * MIB
        ),
        cost_estimate=SMALL,
        name="feed_all",
    )(hidden, backs, gate, up, down)


def collect_kernel(valid, transposed, count, width, *refs):
    grads, weights = refs[:count], refs[count : 2 * count]
    small_ref, total_ref = refs[2 * count : 2 * count + 2]
    mine, other, pair, arrive = refs[2 * count + 2 : 2 * count + 6]
    line_send, line_recv, core_send, core_recv = refs[2 * count + 6 :]
    mesh = pl.DeviceIdType.MESH
    place, me = lax.axis_index("dp"), lax.axis_index("fsdp")
    chips = lax.axis_size("fsdp") // 2
    chip, core = me // 2, me % 2
    turn, tile = pl.program_id(0), pl.program_id(1)
    tiles = pl.num_programs(1)
    span = small_ref.shape[-1]
    target = across(chip, chips - 1 - turn)
    slot = lax.rem(turn, 2)
    columns = pl.ds(pl.multiple_of(tile * span, 128), span)

    def core_copy(at_turn, at_tile):
        where = pl.ds(pl.multiple_of(at_tile * span, 128), span)
        owner = across(chip, chips - 1 - at_turn)
        return pltpu.make_async_remote_copy(
            src_ref=other.at[lax.rem(at_turn, 2), :, where],
            dst_ref=pair.at[owner, :, where],
            send_sem=core_send.at[lax.rem(at_turn, 2), at_tile],
            recv_sem=core_recv.at[owner, at_tile],
            device_id=(place, 2 * chip + 1 - core),
            device_id_type=mesh,
        )

    def valid_at(side, step):
        return chip <= step - 1 if side == 0 else chip >= chips - step

    def fed(side):
        return chip > 0 if side == 0 else chip < chips - 1

    def owner_at(side, step):
        return chip + chips - step if side == 0 else chip - chips + step

    def line_copy(side, step):
        return pltpu.make_async_remote_copy(
            src_ref=mine.at[owner_at(side, step)],
            dst_ref=arrive.at[side, step - 1],
            send_sem=line_send.at[side, step - 1],
            recv_sem=line_recv.at[side, step - 1],
            device_id=(place, me + 2 if side == 0 else me - 2),
            device_id_type=mesh,
        )

    def line_arrival(side, step):
        return pltpu.make_async_remote_copy(
            src_ref=mine.at[chip],
            dst_ref=arrive.at[side, step - 1],
            send_sem=line_send.at[side, step - 1],
            recv_sem=line_recv.at[side, step - 1],
            device_id=(place, me + 2 if side == 0 else me - 2),
            device_id_type=mesh,
        )

    @pl.when((turn == 0) & (tile == 0))
    def _():
        greet(place, me, chip, chips)

    @pl.when((turn > 0) & (tile == 0))
    def _():
        done = across(chip, chips - turn)

        def take(at_tile, _):
            core_copy(turn - 1, at_tile).wait_recv()
            return 0

        lax.fori_loop(0, tiles, take, 0)
        mine[done] = (mine[done].astype(FULL) + pair[done].astype(FULL)).astype(LOW)
        for side in range(2):

            @pl.when(valid_at(side, turn))
            def _(side=side):
                owner = owner_at(side, turn)

                @pl.when((turn > 1) & fed(side))
                def _():
                    line_arrival(side, turn - 1).wait_recv()
                    mine[owner] = (
                        mine[owner].astype(FULL) + arrive[side, turn - 2].astype(FULL)
                    ).astype(LOW)

                line_copy(side, turn).start()

    @pl.when(turn > 1)
    def _():
        core_copy(turn - 2, tile).wait_send()

    for half in range(2):
        where = slice(half * valid, (half + 1) * valid)
        part = None
        for grad, weight in zip(grads, weights):
            product = (multiply_right if transposed else multiply)(grad[where], weight[...])
            part = product if part is None else part + product
        if half == 0:
            mine[target, :valid, columns] = part.astype(LOW)
            mine[target, valid:, columns] = small_ref[0, 0]
        else:
            other[slot, :valid, columns] = part.astype(LOW)
            other[slot, valid:, columns] = small_ref[0, 1]
    core_copy(turn, tile).start()

    @pl.when((turn == chips - 1) & (tile == tiles - 1))
    def _():
        def take(at_tile, _):
            core_copy(turn, at_tile).wait_recv()
            core_copy(turn, at_tile).wait_send()

            @pl.when(turn > 0)
            def _():
                core_copy(turn - 1, at_tile).wait_send()

            return 0

        lax.fori_loop(0, tiles, take, 0)
        total_ref[...] = mine[chip].astype(FULL) + pair[chip].astype(FULL)
        for side in range(2):

            @pl.when(fed(side))
            def _(side=side):
                line_arrival(side, chips - 1).wait_recv()
                total_ref[...] += arrive[side, chips - 2].astype(FULL)

        def finish(step, _):
            for side in range(2):

                @pl.when(valid_at(side, step))
                def _(side=side):
                    line_copy(side, step).wait_send()

            return 0

        lax.fori_loop(1, chips, finish, 0)


def collect(identity, valid, transposed, grads, weights, small, width):
    chips = lax.axis_size("fsdp") // 2
    units = grads[0].shape[1]
    extra = small.shape[2]
    block = valid + extra
    tile = math.gcd(width, 256)
    count = len(grads)
    rows = pl.BlockSpec((2 * valid, units), lambda t, j: (chips - 1 - t, 0))
    if transposed:
        weight = pl.BlockSpec((tile, units), lambda t, j: (j, 0))
    else:
        weight = pl.BlockSpec((units, tile), lambda t, j: (0, j))
    dma = pltpu.SemaphoreType.DMA
    return pl.pallas_call(
        functools.partial(collect_kernel, valid, transposed, count, width),
        out_shape=jax.ShapeDtypeStruct((block, width), FULL),
        grid=(chips, width // tile),
        in_specs=[rows] * count
        + [weight] * count
        + [pl.BlockSpec((1, 2, extra, tile), lambda t, j: (chips - 1 - t, 0, 0, j))],
        out_specs=pl.BlockSpec((block, width), lambda t, j: (0, 0)),
        scratch_shapes=[
            pltpu.VMEM((chips, block, width), LOW),
            pltpu.VMEM((2, block, width), LOW),
            pltpu.VMEM((chips, block, width), LOW),
            pltpu.VMEM((2, chips - 1, block, width), LOW),
            dma((2, chips - 1)),
            dma((2, chips - 1)),
            dma((2, width // tile)),
            dma((chips, width // tile)),
        ],
        compiler_params=pltpu.CompilerParams(
            collective_id=identity, has_side_effects=True, vmem_limit_bytes=62 * MIB
        ),
        cost_estimate=SMALL,
        name="collect",
    )(*grads, *weights, small)


def part_kernel(valid, inner_ref, down_ref, small_ref, mine_ref, other_ref):
    for half, out in enumerate((mine_ref, other_ref)):
        where = slice(half * valid, (half + 1) * valid)
        out[0, :valid] = multiply(inner_ref[where], down_ref[...]).astype(LOW)
        out[0, valid:] = small_ref[0, half]


def part_chunks(valid, inner, down, small):
    chips, _, extra, width = small.shape
    units = inner.shape[1]
    tile = math.gcd(width, 512)
    out = pl.BlockSpec((1, valid + extra, tile), lambda p, j: (p, 0, j))
    return pl.pallas_call(
        functools.partial(part_kernel, valid),
        out_shape=[jax.ShapeDtypeStruct((chips, valid + extra, width), LOW)] * 2,
        grid=(chips, width // tile),
        in_specs=[
            pl.BlockSpec((2 * valid, units), lambda p, j: (p, 0)),
            pl.BlockSpec((units, tile), lambda p, j: (0, j)),
            pl.BlockSpec((1, 2, extra, tile), lambda p, j: (p, 0, 0, j)),
        ],
        out_specs=[out] * 2,
        compiler_params=pltpu.CompilerParams(vmem_limit_bytes=48 * MIB),
        cost_estimate=SMALL,
        name="part_chunks",
    )(inner, down, small)


def norm_back(rows, gain, grad):
    factor = lax.rsqrt(jnp.mean(rows * rows, axis=-1, keepdims=True) + EPS)
    scaled = gain * grad
    inner = jnp.mean(rows * scaled, axis=-1, keepdims=True)
    rows_grad = factor * scaled - (factor * factor * factor * inner) * rows
    return rows_grad, jnp.sum(grad * rows * factor, axis=0, keepdims=True)


def middle_kernel(grad_ref, rows_ref, back_ref, gain_ref, weight_ref, total_ref, low_ref, mixed_ref, part_ref):
    @pl.when(pl.program_id(0) == 0)
    def _():
        rows_grad, part_ref[...] = norm_back(rows_ref[...], gain_ref[...], grad_ref[...])
        total = back_ref[...].astype(FULL) + rows_grad
        total_ref[...] = total
        low_ref[...] = total.astype(LOW)

    mixed_ref[...] = multiply_right(low_ref[...], weight_ref[...]).astype(LOW)


def middle_back(grad, rows, back, gain, weight):
    count, width = rows.shape
    features = weight.shape[0]
    tile = math.gcd(features, 512)
    whole = pl.BlockSpec((count, width), lambda j: (0, 0))
    return pl.pallas_call(
        middle_kernel,
        out_shape=[
            jax.ShapeDtypeStruct((count, width), FULL),
            jax.ShapeDtypeStruct((count, width), LOW),
            jax.ShapeDtypeStruct((count, features), LOW),
            jax.ShapeDtypeStruct((1, width), FULL),
        ],
        grid=(features // tile,),
        in_specs=[whole, whole, whole, pl.BlockSpec((1, width), lambda j: (0, 0))]
        + [pl.BlockSpec((tile, width), lambda j: (j, 0))],
        out_specs=[whole, whole, pl.BlockSpec((count, tile), lambda j: (0, j))]
        + [pl.BlockSpec((1, width), lambda j: (0, 0))],
        compiler_params=pltpu.CompilerParams(vmem_limit_bytes=56 * MIB),
        cost_estimate=SMALL,
        name="middle_back",
    )(grad, rows, back, gain.reshape(1, width), weight)


def entry_kernel(query_ref, kv_ref, rows_ref, total_ref, gain_ref, weight_ref, out_ref, part_ref, held):
    tile = weight_ref.shape[0]
    where = pl.ds(pl.multiple_of(pl.program_id(0) * tile, 128), tile)
    features = query_ref.shape[1]
    held[:, where] = multiply_right(query_ref[...], weight_ref[:, :features]) + multiply_right(
        kv_ref[...], weight_ref[:, features:]
    )

    @pl.when(pl.program_id(0) == pl.num_programs(0) - 1)
    def _():
        rows_grad, part_ref[...] = norm_back(rows_ref[...], gain_ref[...], held[...])
        out_ref[...] = total_ref[...] + rows_grad


def entry_back(query_grad, kv_grad, rows, total, gain, weight):
    count, width = rows.shape
    tile = math.gcd(width, 512)
    fixed = lambda j: (0, 0)
    whole = pl.BlockSpec((count, width), fixed)
    return pl.pallas_call(
        entry_kernel,
        out_shape=[
            jax.ShapeDtypeStruct((count, width), FULL),
            jax.ShapeDtypeStruct((1, width), FULL),
        ],
        grid=(width // tile,),
        in_specs=[
            pl.BlockSpec(query_grad.shape, fixed),
            pl.BlockSpec(kv_grad.shape, fixed),
            whole,
            whole,
            pl.BlockSpec((1, width), fixed),
            pl.BlockSpec((tile, weight.shape[1]), lambda j: (j, 0)),
        ],
        out_specs=[whole, pl.BlockSpec((1, width), fixed)],
        scratch_shapes=[pltpu.VMEM((count, width), FULL)],
        compiler_params=pltpu.CompilerParams(vmem_limit_bytes=56 * MIB),
        cost_estimate=SMALL,
        name="entry_back",
    )(query_grad, kv_grad, rows, total, gain.reshape(1, width), weight)


class CopySum:
    def __init__(self, split, values, totals, arrived, whole, sems):
        self.split, self.values, self.totals = split, values, totals
        self.arrived, self.whole = arrived, whole
        self.part_send, self.part_recv, self.whole_send, self.whole_recv = sems
        self.copies = lax.axis_size("dp")
        self.place, self.me = lax.axis_index("dp"), lax.axis_index("fsdp")

    @staticmethod
    def split_of(shapes):
        return [shape[0] % (TILE * lax.axis_size("dp")) == 0 for shape in shapes]

    @staticmethod
    def scratch(shapes):
        copies = lax.axis_size("dp")
        arrived, whole = [], []
        for (rows, columns), parts in zip(shapes, CopySum.split_of(shapes)):
            arrived.append((copies - 1, rows // copies, columns) if parts else (copies, rows, columns))
            whole.append((rows, columns) if parts else (TILE, 128))
        return [pltpu.VMEM(shape, LOW) for shape in arrived + whole]

    def rows(self, a, owner):
        part = self.values[a].shape[0] // self.copies
        return pl.ds(pl.multiple_of(owner * part, TILE), part)

    def part_copy(self, a, k):
        peer = lax.rem(self.place + k, self.copies)
        value, arrived = self.values[a], self.arrived[a]
        return pltpu.make_async_remote_copy(
            src_ref=value.at[self.rows(a, peer)] if self.split[a] else value,
            dst_ref=arrived.at[k - 1] if self.split[a] else arrived.at[self.place],
            send_sem=self.part_send.at[a, k],
            recv_sem=self.part_recv.at[a, k],
            device_id=(peer, self.me),
            device_id_type=pl.DeviceIdType.MESH,
        )

    def whole_copy(self, a, k):
        where = self.rows(a, self.place)
        return pltpu.make_async_remote_copy(
            src_ref=self.whole[a].at[where],
            dst_ref=self.whole[a].at[where],
            send_sem=self.whole_send.at[a, k],
            recv_sem=self.whole_recv.at[a, k],
            device_id=(lax.rem(self.place + k, self.copies), self.me),
            device_id_type=pl.DeviceIdType.MESH,
        )

    def send(self, a):
        for k in range(1, self.copies):
            self.part_copy(a, k).start()

    def reduce(self, a):
        value, arrived = self.values[a], self.arrived[a]
        if not self.split[a]:
            arrived[self.place] = value[...]
        for k in range(1, self.copies):
            self.part_copy(a, k).wait_recv()
        if self.split[a]:
            total = value[self.rows(a, self.place)].astype(FULL)
            for k in range(1, self.copies):
                total = total + arrived[k - 1].astype(FULL)
            self.whole[a][self.rows(a, self.place)] = total.astype(LOW)
            for k in range(1, self.copies):
                self.whole_copy(a, k).start()
        else:
            total = arrived[0].astype(FULL)
            for k in range(1, self.copies):
                total = total + arrived[k].astype(FULL)
            self.totals[a][...] = total

    def finish(self, a):
        for k in range(1, self.copies):
            self.part_copy(a, k).wait_send()
            if self.split[a]:
                self.whole_copy(a, k).wait_send()
                self.whole_copy(a, k).wait_recv()
        if self.split[a]:
            self.totals[a][...] = self.whole[a][...].astype(FULL)


def tail_kernel(split, *refs):
    count = len(split)
    given = count - 3
    inputs, refs = refs[:given], refs[given:]
    summed_ref, left_ref, right_ref = refs[:3]
    totals, all_ref, refs = refs[3 : 3 + count], refs[3 + count], refs[4 + count :]
    arrived, whole, refs = refs[:count], refs[count : 2 * count], refs[2 * count :]
    held, arrive, total, action, weights, gains, right_all = refs[:7]
    load_sem, right_sem, line_send, line_recv = refs[7:11]
    sums = CopySum(split, (*inputs, action, weights, gains), totals, arrived, whole, refs[11:15])
    gather = Gather([1], [right_ref], [all_ref], refs[15:])
    mesh = pl.DeviceIdType.MESH
    place, me = lax.axis_index("dp"), lax.axis_index("fsdp")
    chips = lax.axis_size("fsdp") // 2
    chip = me // 2

    load = pltpu.make_async_copy(summed_ref, held, load_sem)
    load.start()
    gather.greet()
    gather.start()
    load.wait()

    def valid_at(side, step):
        return chip <= step - 1 if side == 0 else chip >= chips - step

    def fed(side):
        return chip > 0 if side == 0 else chip < chips - 1

    def line_copy(side, step, owner):
        return pltpu.make_async_remote_copy(
            src_ref=held.at[owner],
            dst_ref=arrive.at[side, step - 1],
            send_sem=line_send.at[side, step - 1],
            recv_sem=line_recv.at[side, step - 1],
            device_id=(place, me + 2 if side == 0 else me - 2),
            device_id_type=mesh,
        )

    for step in range(1, chips):
        for side in range(2):

            @pl.when(valid_at(side, step))
            def _(step=step, side=side):
                owner = chip + chips - step if side == 0 else chip - chips + step
                if step > 1:

                    @pl.when(fed(side))
                    def _():
                        line_copy(side, step - 1, chip).wait_recv()
                        held[owner] = (
                            held[owner].astype(FULL) + arrive[side, step - 2].astype(FULL)
                        ).astype(LOW)

                line_copy(side, step, owner).start()

        gather.advance(step)
        if step == 1:
            for a in range(given):
                sums.send(a)
        if step == min(2, chips - 1):
            for a in range(given):
                sums.reduce(a)
    gather.finish()
    fetch = pltpu.make_async_copy(all_ref, right_all, right_sem)
    fetch.start()
    fetch.wait()
    action[...] = multiply_left(left_ref[...], right_all[...]).astype(LOW)
    sums.send(given)
    total[...] = held[chip].astype(FULL)
    for side in range(2):

        @pl.when(fed(side))
        def _(side=side):
            line_copy(side, chips - 1, chip).wait_recv()
            total[...] += arrive[side, chips - 2].astype(FULL)

    rows = weights.shape[0]
    weights[...] = total[:rows].astype(LOW)
    gains[...] = total[rows:].astype(LOW)
    for a in range(given + 1, count):
        sums.send(a)
    for a in range(given):
        sums.finish(a)
    for a in range(given, count):
        sums.reduce(a)
    for step in range(1, chips):
        for side in range(2):

            @pl.when(valid_at(side, step))
            def _(step=step, side=side):
                line_copy(side, step, chip).wait_send()

    for a in range(given, count):
        sums.finish(a)


def tail_sums(values, summed, rows, left, right):
    chips, block = summed.shape[0], summed.shape[1:]
    own = [(left.shape[1], right.shape[1]), (rows, block[1]), (block[0] - rows, block[1])]
    shapes = [value.shape for value in values] + own
    count = len(shapes)
    dma = pltpu.SemaphoreType.DMA
    copies = lax.axis_size("dp")
    inside = pl.BlockSpec(memory_space=pltpu.VMEM)
    anywhere = pl.BlockSpec(memory_space=pl.ANY)
    outs = pl.pallas_call(
        functools.partial(tail_kernel, CopySum.split_of(shapes)),
        out_shape=[jax.ShapeDtypeStruct(shape, FULL) for shape in shapes] + whole_shapes([right]),
        in_specs=[inside] * len(values) + [anywhere, inside, anywhere],
        out_specs=[inside] * count + [anywhere],
        scratch_shapes=CopySum.scratch(shapes)
        + [
            pltpu.VMEM((chips, *block), LOW),
            pltpu.VMEM((2, chips - 1, *block), LOW),
            pltpu.VMEM(block, FULL),
            *(pltpu.VMEM(shape, LOW) for shape in own),
            pltpu.VMEM((2 * chips * right.shape[0], right.shape[1]), LOW),
            dma,
            dma,
            dma((2, chips - 1)),
            dma((2, chips - 1)),
        ]
        + [dma((count, copies))] * 4
        + Gather.scratch(1),
        compiler_params=pltpu.CompilerParams(
            collective_id=6, has_side_effects=True, vmem_limit_bytes=58 * MIB
        ),
        cost_estimate=pl.CostEstimate(
            flops=30_000_000_000, bytes_accessed=1, transcendentals=0
        ),
        name="tail_sums",
    )(*values, summed, left, right)
    return outs[:count]


def widen_kernel(*refs):
    count = len(refs) - 1
    for k, ref in enumerate(refs[:-1]):

        @pl.when(pl.program_id(0) == k)
        def _(ref=ref):
            refs[-1][...] = ref[...].astype(FULL)


def widen(*values):
    count, (rows, columns) = len(values), values[0].shape
    tile = math.gcd(rows, 256)
    return pl.pallas_call(
        widen_kernel,
        out_shape=jax.ShapeDtypeStruct((count * rows, columns), FULL),
        grid=(count, rows // tile),
        in_specs=[pl.BlockSpec((tile, columns), lambda k, i: (i, 0))] * count,
        out_specs=pl.BlockSpec((tile, columns), lambda k, i: (k * (rows // tile) + i, 0)),
        compiler_params=pltpu.CompilerParams(vmem_limit_bytes=32 * MIB),
        cost_estimate=SMALL,
        name="widen",
    )(*values)


def share_kernel(core_ref, left_ref, right_ref, *refs):
    rows = left_ref.shape[1]
    refs[-1][0, :rows] = multiply_left(left_ref[...], right_ref[...]).astype(LOW)
    if len(refs) > 1:
        refs[-1][0, rows:] = refs[0][0]


def weight_shares(core, left, right, gains=None):
    size = lax.axis_size("fsdp")
    chips = size // 2
    count, rows = left.shape[0], left.shape[1] // size
    width, total, extra = right.shape[1], rows, []
    if gains is not None:
        total += gains.shape[1]
        extra = [pl.BlockSpec((1, *gains.shape[1:]), lambda c, core: (2 * c + core[0], 0, 0))]
    return pl.pallas_call(
        share_kernel,
        out_shape=jax.ShapeDtypeStruct((chips, total, width), LOW),
        grid_spec=pltpu.PrefetchScalarGridSpec(
            num_scalar_prefetch=1,
            grid=(chips,),
            in_specs=[
                pl.BlockSpec((count, rows), lambda c, core: (0, 2 * c + core[0])),
                pl.BlockSpec((count, width), lambda c, core: (0, 0)),
            ]
            + extra,
            out_specs=pl.BlockSpec((1, total, width), lambda c, core: (c, 0, 0)),
        ),
        compiler_params=pltpu.CompilerParams(vmem_limit_bytes=48 * MIB),
        cost_estimate=SMALL,
        name="weight_shares",
    )(
        jnp.reshape(core, (1,)).astype(jnp.int32),
        left,
        right,
        *([] if gains is None else [gains]),
    )


def stacked(refs, columns=slice(None)):
    return jnp.concatenate([ref[0, :, columns] for ref in refs], axis=0)


def softmax_of(queries, keys, bias, scale):
    scores = multiply_right(queries, keys) * scale + bias
    raised = jnp.exp(scores - jnp.max(scores, axis=-1, keepdims=True))
    return raised / jnp.sum(raised, axis=-1, keepdims=True)


def mix_kernel(scale, features, shares, *refs):
    count = len(shares)
    prefix_ref, action_ref, prefix_all_ref, action_all_ref, bias_ref = refs[:5]
    shards, refs = refs[5 : 5 + count], refs[5 + count :]
    prefix_out, action_out, kv_out = refs[:3]
    wholes, refs = refs[3 : 3 + count], refs[3 + count :]
    held, send_sem, recv_sem, out_sem = refs[:4]
    gather = Gather(shares, shards, wholes, refs[4:])
    copies = lax.axis_size("dp")
    place, me = lax.axis_index("dp"), lax.axis_index("fsdp")
    item, head = pl.program_id(0), pl.program_id(1)
    items, rows = prefix_all_ref.shape[0], prefix_ref.shape[1]
    heads = pl.num_programs(1)
    turn = item * heads + head

    def copy(at, k):
        return pltpu.make_async_remote_copy(
            src_ref=held.at[0, at],
            dst_ref=held.at[k, at],
            send_sem=send_sem.at[at, k],
            recv_sem=recv_sem.at[at, k],
            device_id=(lax.rem(place + k, copies), me),
            device_id_type=pl.DeviceIdType.MESH,
        )

    @pl.when((item == 0) & (head == 0))
    def _():
        for at in range(items):
            held[0, at, :rows] = prefix_all_ref[at, :, features:]
            held[0, at, rows:] = action_all_ref[at, :, features:]
        gather.greet()
        for at in range(items):
            for k in range(1, copies):
                copy(at, k).start()
        gather.start()

    @pl.when(head == 0)
    def _():
        for k in range(1, copies):
            copy(item, k).wait_recv()

    every = 2 if gather.chips <= items * features // kv_out.shape[3] else 1

    @pl.when((turn > 0) & (lax.rem(turn, every) == 0) & (turn < every * gather.chips))
    def _():
        gather.advance(turn // every)

    queries = stacked((prefix_ref, action_ref))
    kv = jnp.concatenate([held[k, item] for k in range(copies)], axis=0)
    head_size = kv.shape[1] // 2
    probs = softmax_of(queries, kv[:, :head_size], bias_ref[0], scale).astype(LOW)
    mixed = multiply(probs, kv[:, head_size:]).astype(LOW)
    prefix_out[0] = mixed[:rows]
    action_out[0] = mixed[rows:]

    @pl.when((item == items - 1) & (head == pl.num_programs(1) - 1))
    def _():
        whole = pltpu.make_async_copy(held, kv_out, out_sem)
        whole.start()
        for at in range(items):
            for k in range(1, copies):
                copy(at, k).wait_send()
        whole.wait()
        gather.finish()


def mix_back_kernel(scale, shares, *refs):
    count = len(shares)
    prefix_ref, action_ref, prefix_grad_ref, action_grad_ref, bias_ref, kv_ref = refs[:6]
    shards, refs = refs[6 : 6 + count], refs[6 + count :]
    prefix_out, action_out, kv_out = refs[:3]
    wholes, refs = refs[3 : 3 + count], refs[3 + count :]
    total, own, sent, arrived, send_sem, recv_sem = refs[:6]
    gather = Gather(shares, shards, wholes, refs[6:])
    copies = lax.axis_size("dp")
    place, me = lax.axis_index("dp"), lax.axis_index("fsdp")
    item, head = pl.program_id(0), pl.program_id(1)
    items, heads = pl.num_programs(0), pl.num_programs(1)
    rows = prefix_ref.shape[1]
    step = rows + action_ref.shape[1]
    turn = item * heads + head

    def copy(at, k):
        return pltpu.make_async_remote_copy(
            src_ref=sent.at[at, k - 1],
            dst_ref=arrived.at[at, k - 1],
            send_sem=send_sem.at[at, k],
            recv_sem=recv_sem.at[at, k],
            device_id=(lax.rem(place + copies - k, copies), me),
            device_id_type=pl.DeviceIdType.MESH,
        )

    @pl.when(turn == 0)
    def _():
        gather.greet()
        gather.start()

    @pl.when((turn > 0) & (turn < gather.chips))
    def _():
        gather.advance(turn)

    @pl.when(head == 0)
    def _():
        total[...] = jnp.zeros_like(total)

    queries = stacked((prefix_ref, action_ref))
    grads = stacked((prefix_grad_ref, action_grad_ref))
    kv = jnp.concatenate([kv_ref[k, 0] for k in range(copies)], axis=0)
    head_size = kv.shape[1] // 2
    keys, values = kv[:, :head_size], kv[:, head_size:]
    probs = softmax_of(queries, keys, bias_ref[0], scale)
    probs_grad = multiply_right(grads, values)
    delta = jnp.sum(probs * probs_grad, axis=-1, keepdims=True)
    score_grad = (probs * (probs_grad - delta)).astype(LOW)
    query_grad = (multiply(score_grad, keys) * scale).astype(LOW)
    prefix_out[0] = query_grad[:rows]
    action_out[0] = query_grad[rows:]
    total[:, :head_size] += multiply_left(score_grad, queries) * scale
    total[:, head_size:] += multiply_left(probs.astype(LOW), grads)

    @pl.when(head == heads - 1)
    def _():
        own[item] = total[:step]
        for k in range(1, copies):
            sent[item, k - 1] = total[k * step : (k + 1) * step].astype(LOW)
            copy(item, k).start()

    @pl.when((item == items - 1) & (head == heads - 1))
    def _():
        for at in range(kv_out.shape[0]):
            for k in range(1, copies):
                copy(at, k).wait_recv()
                copy(at, k).wait_send()
            summed = own[at]
            for k in range(1, copies):
                summed = summed + arrived[at, k - 1].astype(FULL)
            kv_out[at] = summed.astype(LOW)
        gather.finish()


def mix_call(scale, heads, prefix, action, bias, grads=None, kv=None, shards=()):
    copies = lax.axis_size("dp")
    items, prefix_rows, columns = prefix.shape
    action_rows = action.shape[1]
    rows, length = prefix_rows + action_rows, bias.shape[2]
    head_size = columns // (heads + 2)
    features = heads * head_size
    per_head = [
        pl.BlockSpec((1, prefix_rows, head_size), lambda i, h: (i, 0, h)),
        pl.BlockSpec((1, action_rows, head_size), lambda i, h: (i, 0, h)),
    ]
    bias_spec = pl.BlockSpec((1, rows, length), lambda i, h: (i, 0, 0))
    shapes = [
        jax.ShapeDtypeStruct((items, prefix_rows, features), LOW),
        jax.ShapeDtypeStruct((items, action_rows, features), LOW),
    ]
    dma = pltpu.SemaphoreType.DMA
    sems = [dma((items, copies)), dma((items, copies))]
    block = (rows, 2 * head_size)
    if grads is None:
        return pl.pallas_call(
            functools.partial(mix_kernel, scale, features, shares_of(shards)),
            out_shape=shapes
            + [jax.ShapeDtypeStruct((copies, items, *block), LOW)]
            + whole_shapes(shards),
            grid=(items, heads),
            in_specs=per_head
            + [
                pl.BlockSpec(prefix.shape, lambda i, h: (0, 0, 0)),
                pl.BlockSpec(action.shape, lambda i, h: (0, 0, 0)),
                bias_spec,
            ]
            + [pl.BlockSpec(memory_space=pl.ANY)] * len(shards),
            out_specs=per_head + [pl.BlockSpec(memory_space=pl.ANY)] * (1 + len(shards)),
            scratch_shapes=[pltpu.VMEM((copies, items, *block), LOW), *sems, dma]
            + Gather.scratch(len(shards)),
            compiler_params=pltpu.CompilerParams(
                collective_id=7, has_side_effects=True, vmem_limit_bytes=48 * MIB
            ),
            cost_estimate=SMALL,
            name="mix",
        )(prefix, action, prefix, action, bias, *shards)
    return pl.pallas_call(
        functools.partial(mix_back_kernel, scale, shares_of(shards)),
        out_shape=shapes + [jax.ShapeDtypeStruct((items, *block), LOW)] + whole_shapes(shards),
        grid=(items, heads),
        in_specs=per_head * 2
        + [bias_spec, pl.BlockSpec((copies, 1, *block), lambda i, h: (0, i, 0, 0))]
        + [pl.BlockSpec(memory_space=pl.ANY)] * len(shards),
        out_specs=per_head
        + [pl.BlockSpec((items, *block), lambda i, h: (0, 0, 0))]
        + [pl.BlockSpec(memory_space=pl.ANY)] * len(shards),
        scratch_shapes=[
            pltpu.VMEM((length, 2 * head_size), FULL),
            pltpu.VMEM((items, *block), FULL),
            pltpu.VMEM((items, copies - 1, *block), LOW),
            pltpu.VMEM((items, copies - 1, *block), LOW),
            *sems,
            *Gather.scratch(len(shards)),
        ],
        compiler_params=pltpu.CompilerParams(
            collective_id=8, has_side_effects=True, vmem_limit_bytes=48 * MIB
        ),
        cost_estimate=SMALL,
        name="mix_back",
    )(prefix, action, *grads, bias, kv, *shards)


def body(
    prefix_in,
    action_in,
    valid_count,
    prefix_before,
    prefix_query,
    prefix_key,
    prefix_value,
    prefix_output,
    prefix_middle,
    prefix_gate,
    prefix_up,
    prefix_down,
    action_before,
    action_query,
    action_key,
    action_value,
    action_output,
    action_middle,
    action_gate,
    action_up,
    action_down,
    prefix_cotangent,
    action_cotangent,
):
    line = Line()
    shards = line.size
    copies = lax.axis_size("dp")
    items, prefix_rows, width = prefix_in.shape
    action_rows = action_in.shape[1]
    action_width = action_in.shape[2]
    head_size = prefix_key.shape[1]
    features = prefix_query.shape[1]
    heads = features // head_size
    columns = features + 2 * head_size
    prefix_length = prefix_rows * copies
    scale = head_size ** (-0.5)
    place = lax.axis_index("dp")
    prefix_pad, action_pad = rounded(prefix_rows), rounded(action_rows)
    prefix_tokens, action_tokens = items * prefix_pad, items * action_pad
    folded = action_tokens * action_width // width
    folded_pad = rounded(folded)

    def padded(prefix, action):
        prefix = jnp.pad(prefix, ((0, 0), (0, prefix_pad - prefix_rows), (0, 0)))
        action = jnp.pad(action, ((0, 0), (0, action_pad - action_rows), (0, 0)))
        return prefix.reshape(prefix_tokens, width), action.reshape(action_tokens, action_width)

    def trimmed(prefix, action):
        prefix = prefix.reshape(items, prefix_pad, width)[:, :prefix_rows]
        return prefix, action.reshape(items, action_pad, action_width)[:, :action_rows]

    def fold(action):
        rows = action.reshape(-1, folded, width)
        return jnp.pad(rows, ((0, 0), (0, folded_pad - folded), (0, 0)))

    def unfold(rows):
        return rows[:folded].reshape(action_tokens, action_width)

    def pack(prefix, action):
        return jnp.concatenate([prefix, fold(action)[0]], axis=0)

    def unpack(packed):
        return packed[:prefix_tokens], unfold(packed[prefix_tokens:])

    share, action_share = prefix_before.shape[0], action_before.shape[0]
    cuts = [0, share, 2 * share, 2 * share + action_share, 2 * share + 2 * action_share]
    gain_rows = rounded(-(-cuts[4] // 128))
    gains = jnp.concatenate([prefix_before, prefix_middle, action_before, action_middle])
    gains = jnp.pad(gains, (0, gain_rows * 128 - cuts[4])).reshape(gain_rows, 128)
    prefix_qkv, action_qkv, gains = gather_shards(
        0,
        jnp.concatenate([prefix_query, prefix_key, prefix_value], axis=1),
        jnp.concatenate([action_query, action_key, action_value], axis=1),
        gains,
    )
    gains = gains.reshape(shards, gain_rows * 128).astype(FULL)
    prefix_gain_in, prefix_gain, action_gain_in, action_gain = (
        gains[:, cuts[i] : cuts[i + 1]].reshape(-1) for i in range(4)
    )

    live = (place * action_rows + jnp.arange(action_rows))[None, :] < valid_count[:, None]
    prefix_back, action_back = padded(
        prefix_cotangent,
        jnp.where(live[:, :, None], action_cotangent, jnp.zeros_like(action_cotangent)),
    )
    backs = lax.all_gather(pack(prefix_back, action_back), "fsdp", axis=0, tiled=True)

    prefix_flat, action_flat = padded(prefix_in.astype(FULL), action_in.astype(FULL))
    prefix_hidden = normalize(prefix_flat, prefix_gain_in).astype(LOW)
    action_hidden = normalize(action_flat, action_gain_in).astype(LOW)
    prefix_all = multiply(prefix_hidden, prefix_qkv).astype(LOW)
    prefix_all = prefix_all.reshape(items, prefix_pad, columns)
    action_all = multiply(action_hidden, action_qkv).astype(LOW)
    action_all = action_all.reshape(items, action_pad, columns)
    far = copies * (prefix_rows + action_rows)

    def places(owner):
        prefix = jnp.arange(prefix_pad)
        action = jnp.arange(action_pad)
        return jnp.concatenate(
            [
                jnp.where(prefix < prefix_rows, owner * prefix_rows + prefix, far),
                jnp.where(
                    action < action_rows, prefix_length + owner * action_rows + action, far
                ),
            ]
        )

    query_place = places(place)
    key_place = jnp.concatenate([places((place + copies - k) % copies) for k in range(copies)])
    later = (query_place[:, None] >= prefix_length) & (key_place[None, :] <= query_place[:, None])
    allowed = (key_place[None, None, :] < prefix_length) | later[None] & (
        key_place[None, None, :] < prefix_length + valid_count[:, None, None]
    )
    bias = jnp.where(allowed, 0.0, NEGATIVE).astype(FULL)
    prefix_mixed, action_mixed, kv, prefix_o, action_o = mix_call(
        scale, heads, prefix_all, action_all, bias, shards=(prefix_output, action_output)
    )
    backs, prefix_mixed = lax.optimization_barrier((backs, prefix_mixed))
    action_mixed = action_mixed.reshape(action_tokens, features)
    prefix_mixed = prefix_mixed.reshape(prefix_tokens, features)
    prefix_mid = prefix_flat + multiply(prefix_mixed, prefix_o)
    action_mid = action_flat + multiply(action_mixed, action_o)

    hidden = pack(
        normalize(prefix_mid, prefix_gain).astype(LOW),
        normalize(action_mid, action_gain).astype(LOW),
    )
    inner, gate_grad, up_grad, all_rows, all_back, small = feed_all(
        prefix_tokens, hidden, backs, prefix_gate, prefix_up, prefix_down
    )
    action_rows_all, action_back_all = (
        small[i, :, :, :folded].reshape(shards * action_tokens, action_width) for i in range(2)
    )
    action_inner, pull = jax.vjp(
        activate, multiply(action_rows_all, action_gate), multiply(action_rows_all, action_up)
    )
    action_inner = action_inner.astype(LOW)
    action_gate_grad, action_up_grad = (
        v.astype(LOW) for v in pull(multiply_right(action_back_all, action_down))
    )

    down_grad = multiply_left(inner, all_back).astype(LOW)
    action_feed = tuple(
        v.astype(LOW)
        for v in (
            multiply_left(action_rows_all, action_gate_grad),
            multiply_left(action_rows_all, action_up_grad),
            multiply_left(action_inner, action_back_all),
        )
    )
    gate_weight_grad = multiply_left(all_rows, gate_grad).astype(LOW)
    gate_grad, up_grad, down_grad, gate_weight_grad = lax.optimization_barrier(
        (gate_grad, up_grad, down_grad, gate_weight_grad)
    )
    def halves(rows):
        return fold(rows.astype(LOW)).reshape(line.chips, 2, folded_pad, width)

    up_weight_grad = multiply_left(all_rows, up_grad).astype(LOW)
    gate_grad, up_grad, down_grad, gate_weight_grad, up_weight_grad, action_feed = (
        lax.optimization_barrier(
            (gate_grad, up_grad, down_grad, gate_weight_grad, up_weight_grad, action_feed)
        )
    )
    feed_sums = lax.psum((down_grad, gate_weight_grad, up_weight_grad, *action_feed), "dp")
    parts = part_chunks(
        prefix_tokens,
        lax.optimization_barrier((inner, up_weight_grad))[0],
        prefix_down,
        halves(multiply(action_inner, action_down)),
    )
    sent, gate_grad = lax.optimization_barrier((add_pairs(11, *parts), gate_grad))
    out_sums = Relay(line, sent, lambda chip: line.chip ^ chip)
    out_sums.advance(1)
    small = halves(
        multiply_right(action_gate_grad, action_gate) + multiply_right(action_up_grad, action_up)
    )
    feed_back = collect(
        2, prefix_tokens, True, (gate_grad, up_grad), (prefix_gate, prefix_up), small, width
    )
    feed_back = out_sums.after(feed_back)
    out_sums.advance(2)

    prefix_mid_grad, prefix_low, prefix_mixed_grad, prefix_middle_part = middle_back(
        feed_back, prefix_mid, prefix_back, prefix_gain, prefix_o
    )
    action_mid_grad, action_low, action_mixed_grad, action_middle_part = middle_back(
        unfold(feed_back[prefix_tokens:]), action_mid, action_back, action_gain, action_o
    )
    sent = line.pairs(9, prefix_mixed, prefix_low)
    output_sums = Relay(line, sent, lambda chip: chip)
    output_sums.advance(1)
    mixed_grads = (
        prefix_mixed_grad.reshape(items, prefix_pad, features),
        action_mixed_grad.reshape(items, action_pad, features),
    )
    tokens_all = jnp.concatenate([action_hidden, action_mixed, action_low], axis=1)
    prefix_query_grad, action_query_grad, kv_grad, tokens_all = mix_call(
        scale, heads, prefix_all, action_all, bias, mixed_grads, kv, (tokens_all,)
    )
    kv_grad = output_sums.after(out_sums.after(kv_grad))
    output_sums.advance(2)
    prefix_qkv_grad = jnp.concatenate([prefix_query_grad, kv_grad[:, :prefix_pad]], axis=2)
    action_qkv_grad = jnp.concatenate([action_query_grad, kv_grad[:, prefix_pad:]], axis=2)
    prefix_qkv_grad = prefix_qkv_grad.reshape(prefix_tokens, columns)
    action_qkv_grad = action_qkv_grad.reshape(action_tokens, columns)
    prefix_grad, prefix_before_part = entry_back(
        prefix_query_grad.reshape(prefix_tokens, features),
        kv_grad[:, :prefix_pad].reshape(prefix_tokens, 2 * head_size),
        prefix_flat,
        prefix_mid_grad,
        prefix_gain_in,
        prefix_qkv,
    )
    action_grad, action_before_part = entry_back(
        action_query_grad.reshape(action_tokens, features),
        kv_grad[:, prefix_pad:].reshape(action_tokens, 2 * head_size),
        action_flat,
        action_mid_grad,
        action_gain_in,
        action_qkv,
    )
    prefix_grad, action_grad = trimmed(prefix_grad, action_grad)

    gain_parts = jnp.concatenate(
        [
            part.reshape(shards, -1)
            for part in (
                prefix_before_part,
                prefix_middle_part,
                action_before_part,
                action_middle_part,
            )
        ],
        axis=1,
    )
    gain_rows = rounded(-(-cuts[4] // columns))
    gain_parts = jnp.pad(gain_parts, ((0, 0), (0, gain_rows * columns - cuts[4])))
    gain_parts = gain_parts.astype(LOW).reshape(shards, gain_rows, columns)
    gain_parts = output_sums.after(gain_parts)
    output_sums.advance(3)
    sent = line.pairs(10, prefix_hidden, prefix_qkv_grad, gain_parts)
    edges = [0]
    for part in (action_width, features, action_width):
        edges.append(edges[-1] + part)
    hidden_all, mixed_all, low_all = (
        tokens_all[:, start:stop] for start, stop in zip(edges, edges[1:])
    )
    rows = action_query.shape[0]
    hidden_slice = lax.dynamic_slice_in_dim(hidden_all, line.place * rows, rows, 1)
    rows = action_output.shape[0]
    action_output_owned = multiply_left(
        lax.dynamic_slice_in_dim(mixed_all, line.place * rows, rows, 1), low_all
    )
    output_owned, action_output_owned, action_qkv_owned, qkv_owned, gain_owned = tail_sums(
        [output_sums.finish().astype(LOW), action_output_owned.astype(LOW)],
        sent,
        prefix_query.shape[0],
        hidden_slice,
        action_qkv_grad,
    )
    feed_sums, output_owned, sent = lax.optimization_barrier((feed_sums, output_owned, sent))
    out_sums.advance(3)
    out_sums.arrived, output_owned = lax.optimization_barrier((out_sums.arrived, output_owned))
    feed_sums = [widen(value) for value in feed_sums]
    sums = unpack(out_sums.finish())
    prefix_out, action_out = trimmed(
        (prefix_mid + sums[0]).astype(LOW), (action_mid + sums[1]).astype(LOW)
    )
    gain_owned = gain_owned.reshape(-1)
    return (
        prefix_out,
        action_out,
        prefix_grad,
        action_grad,
        gain_owned[cuts[0] : cuts[1]],
        qkv_owned[:rows, :features],
        qkv_owned[:rows, features : features + head_size],
        qkv_owned[:rows, features + head_size :],
        output_owned,
        gain_owned[cuts[1] : cuts[2]],
        feed_sums[1],
        feed_sums[2],
        feed_sums[0],
        gain_owned[cuts[2] : cuts[3]],
        action_qkv_owned[:, :features],
        action_qkv_owned[:, features : features + head_size],
        action_qkv_owned[:, features + head_size :],
        action_output_owned,
        gain_owned[cuts[3] : cuts[4]],
        *feed_sums[3:],
    )


def solution(mesh):
    tokens = P("fsdp", "dp", None)
    rows, columns, vector = P("fsdp", None), P(None, "fsdp"), P("fsdp")
    weights = (vector, rows, rows, rows, rows, vector, columns, columns, rows)
    return jax.shard_map(
        body,
        mesh=mesh,
        in_specs=(tokens, tokens, vector, *weights, *weights, tokens, tokens),
        out_specs=(tokens, tokens, tokens, tokens, *weights, *weights),
        check_vma=False,
    )
```

```python
import functools
import math

import jax
import jax.numpy as jnp
from jax import lax
from jax.experimental import pallas as pl
from jax.experimental.pallas import tpu as pltpu
from jax.sharding import PartitionSpec as P

EPS = 1e-06
NEGATIVE = -1e30
LOW = jnp.bfloat16
FULL = jnp.float32
TILE = 16
MIB = 1 << 20
SMALL = pl.CostEstimate(flops=1, bytes_accessed=1, transcendentals=0)


def normalize(rows, gain):
    return rows * lax.rsqrt(jnp.mean(rows * rows, axis=-1, keepdims=True) + EPS) * gain


def multiply(left, right):
    return jnp.dot(left, right, preferred_element_type=FULL)


def multiply_left(left, right):
    return lax.dot_general(
        left, right, (((0,), (0,)), ((), ())), preferred_element_type=FULL
    )


def multiply_right(left, right):
    return lax.dot_general(
        left, right, (((1,), (1,)), ((), ())), preferred_element_type=FULL
    )


def activate(gate, upper):
    return jax.nn.gelu(gate, approximate=True) * upper


class Line:
    def __init__(self):
        self.size = lax.axis_size("fsdp")
        self.chips = self.size // 2
        self.place = lax.axis_index("fsdp")
        self.chip = self.place // 2
        self.core = self.place % 2

    def move(self, value, chips, step):
        pairs = [
            (2 * chip + core, 2 * (chip + step) + core) for chip in chips for core in range(2)
        ]
        return lax.ppermute(value, "fsdp", pairs)

    def pairs(self, identity, *values):
        mine, other = (weight_shares(core, *values) for core in (self.core, 1 - self.core))
        return add_pairs(identity, mine, other)


class Relay:
    def __init__(self, line, summed, index):
        self.line, self.summed, self.index = line, summed, index
        self.taken, self.arrived = 0, []

    def advance(self, part, parts=3):
        line, count = self.line, self.line.chips
        last = -(-(count - 1) * part // parts)
        while self.taken < last:
            self.taken += 1
            step, arrived = self.taken, self.arrived
            self.arrived = []
            for i, side in enumerate((1, -1)):
                target = self.index(jnp.clip(line.chip + side * (count - step), 0, count - 1))
                if arrived:
                    payload = add_block(self.summed, target, [arrived[i]], LOW)
                else:
                    payload = lax.dynamic_index_in_dim(self.summed, target, 0, keepdims=False)
                chips = range(0, step) if side == 1 else range(count - step, count)
                self.arrived.append(line.move(payload, chips, side))

    def after(self, values):
        self.arrived, values = lax.optimization_barrier((self.arrived, values))
        return values

    def finish(self):
        self.advance(1, 1)
        return add_block(self.summed, self.index(self.line.chip), self.arrived, FULL)


def add_kernel(index_ref, value_ref, *refs):
    total = value_ref[0].astype(FULL)
    for ref in refs[:-1]:
        total = total + ref[...].astype(FULL)
    refs[-1][...] = total.astype(refs[-1].dtype)


def add_block(values, index, others, kind):
    shape = values.shape[1:]
    block = pl.BlockSpec(shape, lambda i, index: (0, 0))
    return pl.pallas_call(
        add_kernel,
        out_shape=jax.ShapeDtypeStruct(shape, kind),
        grid_spec=pltpu.PrefetchScalarGridSpec(
            num_scalar_prefetch=1,
            grid=(1,),
            in_specs=[pl.BlockSpec((1, *shape), lambda i, index: (index[0], 0, 0))]
            + [block] * len(others),
            out_specs=block,
        ),
        compiler_params=pltpu.CompilerParams(vmem_limit_bytes=40 * MIB),
        cost_estimate=SMALL,
        name="add_block",
    )(jnp.reshape(index, (1,)).astype(jnp.int32), values, *others)


def pair_kernel(mine_ref, other_ref, out_ref, landed, send_sem, recv_sem):
    place, me = lax.axis_index("dp"), lax.axis_index("fsdp")
    partner = (place, me + 1 - 2 * (me % 2))
    mesh = pl.DeviceIdType.MESH
    turn, count = pl.program_id(0), landed.shape[0]

    def copy(at):
        return pltpu.make_async_remote_copy(
            src_ref=other_ref.at[at],
            dst_ref=landed.at[at],
            send_sem=send_sem.at[at],
            recv_sem=recv_sem.at[at],
            device_id=partner,
            device_id_type=mesh,
        )

    @pl.when(turn == 0)
    def _():
        barrier = pltpu.get_barrier_semaphore()
        pl.semaphore_signal(barrier, inc=1, device_id=partner, device_id_type=mesh)
        pl.semaphore_wait(barrier, 1)
        for at in range(count):
            copy(at).start()

    copy(turn).wait_recv()
    out_ref[0] = (mine_ref[0].astype(FULL) + landed[turn].astype(FULL)).astype(LOW)

    @pl.when(turn == count - 1)
    def _():
        for at in range(count):
            copy(at).wait_send()


def add_pairs(identity, mine, other):
    count, shape = mine.shape[0], mine.shape[1:]
    block = pl.BlockSpec((1, *shape), lambda i: (i, 0, 0))
    dma = pltpu.SemaphoreType.DMA
    return pl.pallas_call(
        pair_kernel,
        out_shape=jax.ShapeDtypeStruct(mine.shape, LOW),
        grid=(count,),
        in_specs=[block, pl.BlockSpec(memory_space=pl.ANY)],
        out_specs=block,
        scratch_shapes=[pltpu.VMEM(mine.shape, LOW), dma((count,)), dma((count,))],
        compiler_params=pltpu.CompilerParams(
            collective_id=identity, has_side_effects=True, vmem_limit_bytes=40 * MIB
        ),
        cost_estimate=SMALL,
        name="add_pairs",
    )(mine, other)


def rounded(count, unit=TILE):
    return -(-count // unit) * unit


class Gather:
    def __init__(self, shares, shards, wholes, sems):
        self.shares, self.shards, self.wholes = shares, shards, wholes
        self.local_sem, self.pair_send, self.pair_recv = sems[:3]
        self.line_send, self.line_recv, self.copy_send, self.copy_recv = sems[3:7]
        self.core_send, self.core_recv = sems[7:]
        self.copies, self.place = lax.axis_size("dp"), lax.axis_index("dp")
        self.chips, self.me = lax.axis_size("fsdp") // 2, lax.axis_index("fsdp")
        self.chip, self.core = self.me // 2, self.me % 2
        self.partner = 2 * self.chip + 1 - self.core

    @staticmethod
    def scratch(count):
        dma = pltpu.SemaphoreType.DMA
        copies, chips = lax.axis_size("dp"), lax.axis_size("fsdp") // 2
        return (
            [dma((count,))] * 3 + [dma((count, 2, chips))] * 2 + [dma((count, 2, chips, copies))] * 4
        )

    def greet(self):
        mesh = pl.DeviceIdType.MESH
        place, me, chip = self.place, self.me, self.chip
        barrier = pltpu.get_barrier_semaphore()
        pl.semaphore_signal(barrier, inc=1, device_id=(place, self.partner), device_id_type=mesh)
        for k in range(1, self.copies):
            peer = lax.rem(place + k, self.copies)
            pl.semaphore_signal(barrier, inc=1, device_id=(peer, me), device_id_type=mesh)

        @pl.when(chip > 0)
        def _():
            pl.semaphore_signal(barrier, inc=1, device_id=(place, me - 2), device_id_type=mesh)

        @pl.when(chip < self.chips - 1)
        def _():
            pl.semaphore_signal(barrier, inc=1, device_id=(place, me + 2), device_id_type=mesh)

        neighbours = jnp.minimum(chip, 1) + jnp.minimum(self.chips - 1 - chip, 1)
        pl.semaphore_wait(barrier, self.copies + neighbours)

    def rows(self, a, owner, share):
        whole = self.shards[a].shape[0]
        part = whole // self.shares[a]
        return pl.ds(pl.multiple_of(owner * whole + share * part, TILE), part)

    def remote(self, source, target, send, recv, device):
        return pltpu.make_async_remote_copy(
            src_ref=source,
            dst_ref=target,
            send_sem=send,
            recv_sem=recv,
            device_id=device,
            device_id_type=pl.DeviceIdType.MESH,
        )

    def my_share(self, a):
        return self.place if self.shares[a] > 1 else 0

    def peers(self, a):
        return range(1, self.copies) if self.shares[a] > 1 else range(0)

    def owner_of(self, side, step):
        return self.me - 2 * step if side == 0 else self.me + 2 * step

    def sends(self, side):
        return self.chip < self.chips - 1 if side == 0 else self.chip > 0

    def has(self, side, step):
        return self.chip >= step if side == 0 else self.chip + step <= self.chips - 1

    def line_copy(self, a, side, step):
        where = self.rows(a, self.owner_of(side, step), self.my_share(a))
        target = self.me + 2 if side == 0 else self.me - 2
        return self.remote(
            self.wholes[a].at[where],
            self.wholes[a].at[where],
            self.line_send.at[a, side, step],
            self.line_recv.at[a, side, step],
            (self.place, target),
        )

    def first_copy(self, a, side):
        part = self.shards[a].shape[0] // self.shares[a]
        target = self.me + 2 if side == 0 else self.me - 2
        return self.remote(
            self.shards[a].at[pl.ds(pl.multiple_of(self.my_share(a) * part, TILE), part)],
            self.wholes[a].at[self.rows(a, self.me, self.my_share(a))],
            self.line_send.at[a, side, 0],
            self.line_recv.at[a, side, 0],
            (self.place, target),
        )

    def peer_copy(self, a, side, step, k):
        where = self.rows(a, self.owner_of(side, step), self.place)
        return self.remote(
            self.wholes[a].at[where],
            self.wholes[a].at[where],
            self.copy_send.at[a, side, step, k],
            self.copy_recv.at[a, side, step, k],
            (lax.rem(self.place + k, self.copies), self.me),
        )

    def core_copy(self, a, side, step, k):
        share = lax.rem(self.place + self.copies - k, self.copies) if self.shares[a] > 1 else 0
        where = self.rows(a, self.owner_of(side, step), share)
        return self.remote(
            self.wholes[a].at[where],
            self.wholes[a].at[where],
            self.core_send.at[a, side, step, k],
            self.core_recv.at[a, side, step, k],
            (self.place, self.partner),
        )

    def rows_all(self, a):
        whole = self.shards[a].shape[0]
        return pl.ds(pl.multiple_of(self.me * whole, TILE), whole)

    def pair_copy(self, a):
        return self.remote(
            self.shards[a],
            self.wholes[a].at[self.rows_all(a)],
            self.pair_send.at[a],
            self.pair_recv.at[a],
            (self.place, self.partner),
        )

    def local_copy(self, a):
        return pltpu.make_async_copy(
            self.shards[a], self.wholes[a].at[self.rows_all(a)], self.local_sem.at[a]
        )

    def start(self):
        for a in range(len(self.shards)):
            for side in range(2):

                @pl.when(self.sends(side))
                def _(a=a, side=side):
                    self.first_copy(a, side).start()

        for a in range(len(self.shards)):
            self.pair_copy(a).start()
            self.local_copy(a).start()

    def hand_over(self, a, side, step):
        for k in self.peers(a):
            self.peer_copy(a, side, step, k).wait_recv()
            self.core_copy(a, side, step, k).start()

    def advance(self, step):
        for a in range(len(self.shards)):
            for side in range(2):

                @pl.when(self.has(side, step))
                def _(a=a, side=side):
                    self.line_copy(a, side, step - 1).wait_recv()

                    @pl.when(self.sends(side))
                    def _():
                        self.line_copy(a, side, step).start()

                    for k in self.peers(a):
                        self.peer_copy(a, side, step, k).start()
                    self.core_copy(a, side, step, 0).start()

        for a in range(len(self.shards)):
            for side in range(2):

                @pl.when((step > 1) & self.has(side, step - 1))
                def _(a=a, side=side):
                    self.hand_over(a, side, step - 1)

    def finish(self):
        last = self.chips - 1
        for a in range(len(self.shards)):
            for side in range(2):

                @pl.when(self.has(side, last))
                def _(a=a, side=side):
                    self.hand_over(a, side, last)

        def settle(step, _):
            for a in range(len(self.shards)):
                for side in range(2):

                    @pl.when(self.has(side, step))
                    def _(a=a, side=side):
                        @pl.when(self.sends(side))
                        def _():
                            self.line_copy(a, side, step).wait_send()

                        for k in self.peers(a):
                            self.peer_copy(a, side, step, k).wait_send()
                            self.core_copy(a, side, step, k).wait_send()
                            self.core_copy(a, side, step, k).wait_recv()
                        self.core_copy(a, side, step, 0).wait_send()
                        self.core_copy(a, side, step, 0).wait_recv()

            return 0

        lax.fori_loop(1, self.chips, settle, 0)
        for a in range(len(self.shards)):
            for side in range(2):

                @pl.when(self.sends(side))
                def _(a=a, side=side):
                    self.first_copy(a, side).wait_send()

            self.pair_copy(a).wait_send()
            self.pair_copy(a).wait_recv()
            self.local_copy(a).wait()


def shares_of(shards):
    copies = lax.axis_size("dp")
    return [copies if shard.shape[0] % (TILE * copies) == 0 else 1 for shard in shards]


def whole_shapes(shards):
    size = lax.axis_size("fsdp")
    return [jax.ShapeDtypeStruct((size * s.shape[0], *s.shape[1:]), s.dtype) for s in shards]


def gather_kernel(shares, *refs):
    count = len(shares)
    gather = Gather(shares, refs[:count], refs[count : 2 * count], refs[2 * count :])
    gather.greet()
    gather.start()

    def advance(step, _):
        gather.advance(step)
        return 0

    lax.fori_loop(1, gather.chips, advance, 0)
    gather.finish()


def gather_shards(identity, *shards):
    count = len(shards)
    anywhere = pl.BlockSpec(memory_space=pl.ANY)
    return pl.pallas_call(
        functools.partial(gather_kernel, shares_of(shards)),
        out_shape=whole_shapes(shards),
        in_specs=[anywhere] * count,
        out_specs=[anywhere] * count,
        scratch_shapes=Gather.scratch(count),
        compiler_params=pltpu.CompilerParams(collective_id=identity, has_side_effects=True),
        cost_estimate=SMALL,
        name="gather_shards",
    )(*shards)


def across(number, other):
    total, bit = 0, 1
    while bit < lax.axis_size("fsdp") // 2:
        total = total + bit * ((number // bit % 2 + other // bit % 2) % 2)
        bit *= 2
    return total


def greet(place, me, chip, chips):
    mesh = pl.DeviceIdType.MESH
    barrier = pltpu.get_barrier_semaphore()
    partner = 2 * chip + 1 - me % 2
    pl.semaphore_signal(barrier, inc=1, device_id=(place, partner), device_id_type=mesh)

    @pl.when(chip > 0)
    def _():
        pl.semaphore_signal(barrier, inc=1, device_id=(place, me - 2), device_id_type=mesh)

    @pl.when(chip < chips - 1)
    def _():
        pl.semaphore_signal(barrier, inc=1, device_id=(place, me + 2), device_id_type=mesh)

    neighbours = jnp.minimum(chip, 1) + jnp.minimum(chips - 1 - chip, 1)
    pl.semaphore_wait(barrier, 1 + neighbours)


def feed_kernel(
    valid,
    hidden_ref,
    backs_ref,
    gate_ref,
    up_ref,
    down_ref,
    inner_ref,
    gate_grad_ref,
    up_grad_ref,
    rows_ref,
    back_ref,
    small_ref,
    land,
    held,
    line_send,
    line_recv,
    core_send,
    core_recv,
    own_sem,
    back_sem,
    out_sem,
):
    mesh = pl.DeviceIdType.MESH
    place, me = lax.axis_index("dp"), lax.axis_index("fsdp")
    chips = lax.axis_size("fsdp") // 2
    chip, core = me // 2, me % 2
    block = hidden_ref.shape[0]
    position, tile = pl.program_id(0), pl.program_id(1)
    tiles = pl.num_programs(1)
    source = across(chip, position)
    owners = (2 * source + core, 2 * source + 1 - core)
    slot = lax.rem(position, 2)

    def sends(side):
        return chip < chips - 1 if side == 0 else chip > 0

    def has(side, step):
        return chip >= step if side == 0 else chip + step <= chips - 1

    def line_copy(side, step):
        owner = me - 2 * step if side == 0 else me + 2 * step
        target = me + 2 if side == 0 else me - 2
        return pltpu.make_async_remote_copy(
            src_ref=land.at[owner],
            dst_ref=land.at[owner],
            send_sem=line_send.at[side, step],
            recv_sem=line_recv.at[side, step],
            device_id=(place, target),
            device_id_type=mesh,
        )

    def line_arrival(side, step):
        owner = me - 2 * step if side == 0 else me + 2 * step
        return pltpu.make_async_remote_copy(
            src_ref=land.at[owner],
            dst_ref=land.at[owner],
            send_sem=line_send.at[side, step - 1],
            recv_sem=line_recv.at[side, step - 1],
            device_id=(place, me + 2 if side == 0 else me - 2),
            device_id_type=mesh,
        )

    def core_copy(owner_chip):
        owner = 2 * owner_chip + core
        return pltpu.make_async_remote_copy(
            src_ref=land.at[owner],
            dst_ref=land.at[owner],
            send_sem=core_send.at[owner_chip],
            recv_sem=core_recv.at[owner_chip],
            device_id=(place, 2 * chip + 1 - core),
            device_id_type=mesh,
        )

    def back_copies(at):
        origin = across(chip, at)
        to = lax.rem(at, 2)
        return [
            pltpu.make_async_copy(
                backs_ref.at[pl.ds(pl.multiple_of(owner * block, TILE), block)],
                held.at[to, half],
                back_sem.at[to, half],
            )
            for half, owner in enumerate((2 * origin + core, 2 * origin + 1 - core))
        ]

    def out_copies():
        copies = []
        for half in range(2):
            where = pl.ds(pl.multiple_of((2 * position + half) * valid, TILE), valid)
            rows, back = land.at[owners[half]], held.at[slot, half]
            for source_ref, target, small in ((rows, rows_ref, 0), (back, back_ref, 1)):
                copies.append((source_ref.at[pl.ds(0, valid)], target.at[where]))
                copies.append(
                    (
                        source_ref.at[pl.ds(valid, block - valid)],
                        small_ref.at[small, position, half],
                    )
                )
        return [
            pltpu.make_async_copy(source_ref, target, out_sem.at[i])
            for i, (source_ref, target) in enumerate(copies)
        ]

    @pl.when((position == 0) & (tile == 0))
    def _():
        for copy in back_copies(0):
            copy.start()
        own = pltpu.make_async_copy(hidden_ref, land.at[me], own_sem)
        own.start()
        greet(place, me, chip, chips)
        own.wait()
        for side in range(2):

            @pl.when(sends(side))
            def _(side=side):
                line_copy(side, 0).start()

        core_copy(chip).start()

    @pl.when(tile == 0)
    def _():
        for side in range(2):

            @pl.when((position > 0) & has(side, position))
            def _(side=side):
                line_arrival(side, position).wait_recv()

                @pl.when(sends(side))
                def _():
                    line_copy(side, position).start()

                core_copy(chip - position if side == 0 else chip + position).start()

        core_copy(source).wait_recv()
        for copy in back_copies(position):
            copy.wait()
        for copy in out_copies():
            copy.start()

        @pl.when(position < chips - 1)
        def _():
            for copy in back_copies(position + 1):
                copy.start()

    root = math.sqrt(2.0 / math.pi)
    for half in range(2):
        where = slice(half * valid, (half + 1) * valid)
        rows = land[owners[half], :valid]
        back = held[slot, half, :valid]
        gate = multiply(rows, gate_ref[...])
        upper = multiply(rows, up_ref[...])
        inner_grad = multiply_right(back, down_ref[...])
        square = gate * gate
        bent = jnp.tanh(root * gate * (1.0 + 0.044715 * square))
        half_up = 0.5 + 0.5 * bent
        active = gate * half_up
        slope = half_up + (0.5 * root) * gate * (1.0 - bent * bent) * (1.0 + 0.134145 * square)
        inner_ref[where] = (active * upper).astype(LOW)
        gate_grad_ref[where] = (inner_grad * upper * slope).astype(LOW)
        up_grad_ref[where] = (inner_grad * active).astype(LOW)

    @pl.when(tile == tiles - 1)
    def _():
        for copy in out_copies():
            copy.wait()

    @pl.when((tile == tiles - 1) & (position == chips - 1))
    def _():
        for side in range(2):

            @pl.when(sends(side))
            def _(side=side):
                line_copy(side, 0).wait_send()

        for owner in range(chips):
            core_copy(owner).wait_send()

        def finish(step, _):
            for side in range(2):

                @pl.when(sends(side) & has(side, step))
                def _(side=side):
                    line_copy(side, step).wait_send()

            return 0

        lax.fori_loop(1, chips, finish, 0)


def feed_all(valid, hidden, backs, gate, up, down):
    block, width = hidden.shape
    size = lax.axis_size("fsdp")
    chips = size // 2
    units = gate.shape[1]
    tile = math.gcd(units, 512)
    column = pl.BlockSpec((width, tile), lambda p, j: (0, j))
    anywhere = pl.BlockSpec(memory_space=pl.ANY)
    total = chips * 2 * valid
    dma = pltpu.SemaphoreType.DMA
    return pl.pallas_call(
        functools.partial(feed_kernel, valid),
        out_shape=[jax.ShapeDtypeStruct((total, units), LOW)] * 3
        + [jax.ShapeDtypeStruct((total, width), LOW)] * 2
        + [jax.ShapeDtypeStruct((2, chips, 2, block - valid, width), LOW)],
        grid=(chips, units // tile),
        in_specs=[anywhere, anywhere, column, column]
        + [pl.BlockSpec((tile, width), lambda p, j: (j, 0))],
        out_specs=[pl.BlockSpec((2 * valid, tile), lambda p, j: (p, j))] * 3 + [anywhere] * 3,
        scratch_shapes=[
            pltpu.VMEM((size, block, width), LOW),
            pltpu.VMEM((2, 2, block, width), LOW),
            dma((2, chips)),
            dma((2, chips)),
            dma((chips,)),
            dma((chips,)),
            dma,
            dma((2, 2)),
            dma((8,)),
        ],
        compiler_params=pltpu.CompilerParams(
            collective_id=1, has_side_effects=True, vmem_limit_bytes=58 * MIB
        ),
        cost_estimate=SMALL,
        name="feed_all",
    )(hidden, backs, gate, up, down)


def collect_kernel(valid, transposed, count, width, *refs):
    grads, weights = refs[:count], refs[count : 2 * count]
    small_ref, total_ref = refs[2 * count : 2 * count + 2]
    mine, other, pair, arrive = refs[2 * count + 2 : 2 * count + 6]
    line_send, line_recv, core_send, core_recv = refs[2 * count + 6 :]
    mesh = pl.DeviceIdType.MESH
    place, me = lax.axis_index("dp"), lax.axis_index("fsdp")
    chips = lax.axis_size("fsdp") // 2
    chip, core = me // 2, me % 2
    turn, tile = pl.program_id(0), pl.program_id(1)
    tiles = pl.num_programs(1)
    span = small_ref.shape[-1]
    target = across(chip, chips - 1 - turn)
    slot = lax.rem(turn, 2)
    columns = pl.ds(pl.multiple_of(tile * span, 128), span)

    def core_copy(at_turn, at_tile):
        where = pl.ds(pl.multiple_of(at_tile * span, 128), span)
        owner = across(chip, chips - 1 - at_turn)
        return pltpu.make_async_remote_copy(
            src_ref=other.at[lax.rem(at_turn, 2), :, where],
            dst_ref=pair.at[owner, :, where],
            send_sem=core_send.at[lax.rem(at_turn, 2), at_tile],
            recv_sem=core_recv.at[owner, at_tile],
            device_id=(place, 2 * chip + 1 - core),
            device_id_type=mesh,
        )

    def valid_at(side, step):
        return chip <= step - 1 if side == 0 else chip >= chips - step

    def fed(side):
        return chip > 0 if side == 0 else chip < chips - 1

    def owner_at(side, step):
        return chip + chips - step if side == 0 else chip - chips + step

    def line_copy(side, step):
        return pltpu.make_async_remote_copy(
            src_ref=mine.at[owner_at(side, step)],
            dst_ref=arrive.at[side, step - 1],
            send_sem=line_send.at[side, step - 1],
            recv_sem=line_recv.at[side, step - 1],
            device_id=(place, me + 2 if side == 0 else me - 2),
            device_id_type=mesh,
        )

    def line_arrival(side, step):
        return pltpu.make_async_remote_copy(
            src_ref=mine.at[chip],
            dst_ref=arrive.at[side, step - 1],
            send_sem=line_send.at[side, step - 1],
            recv_sem=line_recv.at[side, step - 1],
            device_id=(place, me + 2 if side == 0 else me - 2),
            device_id_type=mesh,
        )

    @pl.when((turn == 0) & (tile == 0))
    def _():
        greet(place, me, chip, chips)

    @pl.when((turn > 0) & (tile == 0))
    def _():
        done = across(chip, chips - turn)

        def take(at_tile, _):
            core_copy(turn - 1, at_tile).wait_recv()
            return 0

        lax.fori_loop(0, tiles, take, 0)
        mine[done] = (mine[done].astype(FULL) + pair[done].astype(FULL)).astype(LOW)
        for side in range(2):

            @pl.when(valid_at(side, turn))
            def _(side=side):
                owner = owner_at(side, turn)

                @pl.when((turn > 1) & fed(side))
                def _():
                    line_arrival(side, turn - 1).wait_recv()
                    mine[owner] = (
                        mine[owner].astype(FULL) + arrive[side, turn - 2].astype(FULL)
                    ).astype(LOW)

                line_copy(side, turn).start()

    @pl.when(turn > 1)
    def _():
        core_copy(turn - 2, tile).wait_send()

    for half in range(2):
        where = slice(half * valid, (half + 1) * valid)
        part = None
        for grad, weight in zip(grads, weights):
            product = (multiply_right if transposed else multiply)(grad[where], weight[...])
            part = product if part is None else part + product
        if half == 0:
            mine[target, :valid, columns] = part.astype(LOW)
            mine[target, valid:, columns] = small_ref[0, 0]
        else:
            other[slot, :valid, columns] = part.astype(LOW)
            other[slot, valid:, columns] = small_ref[0, 1]
    core_copy(turn, tile).start()

    @pl.when((turn == chips - 1) & (tile == tiles - 1))
    def _():
        def take(at_tile, _):
            core_copy(turn, at_tile).wait_recv()
            core_copy(turn, at_tile).wait_send()

            @pl.when(turn > 0)
            def _():
                core_copy(turn - 1, at_tile).wait_send()

            return 0

        lax.fori_loop(0, tiles, take, 0)
        total_ref[...] = mine[chip].astype(FULL) + pair[chip].astype(FULL)
        for side in range(2):

            @pl.when(fed(side))
            def _(side=side):
                line_arrival(side, chips - 1).wait_recv()
                total_ref[...] += arrive[side, chips - 2].astype(FULL)

        def finish(step, _):
            for side in range(2):

                @pl.when(valid_at(side, step))
                def _(side=side):
                    line_copy(side, step).wait_send()

            return 0

        lax.fori_loop(1, chips, finish, 0)


def collect(identity, valid, transposed, grads, weights, small, width):
    chips = lax.axis_size("fsdp") // 2
    units = grads[0].shape[1]
    extra = small.shape[2]
    block = valid + extra
    tile = math.gcd(width, 256)
    count = len(grads)
    rows = pl.BlockSpec((2 * valid, units), lambda t, j: (chips - 1 - t, 0))
    if transposed:
        weight = pl.BlockSpec((tile, units), lambda t, j: (j, 0))
    else:
        weight = pl.BlockSpec((units, tile), lambda t, j: (0, j))
    dma = pltpu.SemaphoreType.DMA
    return pl.pallas_call(
        functools.partial(collect_kernel, valid, transposed, count, width),
        out_shape=jax.ShapeDtypeStruct((block, width), FULL),
        grid=(chips, width // tile),
        in_specs=[rows] * count
        + [weight] * count
        + [pl.BlockSpec((1, 2, extra, tile), lambda t, j: (chips - 1 - t, 0, 0, j))],
        out_specs=pl.BlockSpec((block, width), lambda t, j: (0, 0)),
        scratch_shapes=[
            pltpu.VMEM((chips, block, width), LOW),
            pltpu.VMEM((2, block, width), LOW),
            pltpu.VMEM((chips, block, width), LOW),
            pltpu.VMEM((2, chips - 1, block, width), LOW),
            dma((2, chips - 1)),
            dma((2, chips - 1)),
            dma((2, width // tile)),
            dma((chips, width // tile)),
        ],
        compiler_params=pltpu.CompilerParams(
            collective_id=identity, has_side_effects=True, vmem_limit_bytes=62 * MIB
        ),
        cost_estimate=SMALL,
        name="collect",
    )(*grads, *weights, small)


def part_kernel(
    valid, inner_ref, down_ref, small_ref, out_ref, mine, other, pair, core_send, core_recv, out_sem
):
    place, me = lax.axis_index("dp"), lax.axis_index("fsdp")
    partner = (place, me + 1 - 2 * (me % 2))
    mesh = pl.DeviceIdType.MESH
    turn, tile = pl.program_id(0), pl.program_id(1)
    turns, tiles = pl.num_programs(0), pl.num_programs(1)
    span = small_ref.shape[-1]
    slot = lax.rem(turn, 2)
    columns = pl.ds(pl.multiple_of(tile * span, 128), span)

    def core_copy(at_turn, at_tile):
        where = pl.ds(pl.multiple_of(at_tile * span, 128), span)
        return pltpu.make_async_remote_copy(
            src_ref=other.at[lax.rem(at_turn, 2), :, where],
            dst_ref=pair.at[at_turn, :, where],
            send_sem=core_send.at[lax.rem(at_turn, 2), at_tile],
            recv_sem=core_recv.at[at_turn, at_tile],
            device_id=partner,
            device_id_type=mesh,
        )

    def out_copy(at_turn):
        return pltpu.make_async_copy(mine.at[at_turn], out_ref.at[at_turn], out_sem.at[at_turn])

    def settle(at_turn):
        def take(at_tile, _):
            core_copy(at_turn, at_tile).wait_recv()
            return 0

        lax.fori_loop(0, tiles, take, 0)
        mine[at_turn] = (mine[at_turn].astype(FULL) + pair[at_turn].astype(FULL)).astype(LOW)
        out_copy(at_turn).start()

    @pl.when((turn == 0) & (tile == 0))
    def _():
        barrier = pltpu.get_barrier_semaphore()
        pl.semaphore_signal(barrier, inc=1, device_id=partner, device_id_type=mesh)
        pl.semaphore_wait(barrier, 1)

    @pl.when((turn > 0) & (tile == 0))
    def _():
        settle(turn - 1)

    @pl.when(turn > 1)
    def _():
        core_copy(turn - 2, tile).wait_send()

    for half in range(2):
        where = slice(half * valid, (half + 1) * valid)
        part = multiply(inner_ref[where], down_ref[...]).astype(LOW)
        if half == 0:
            mine[turn, :valid, columns] = part
            mine[turn, valid:, columns] = small_ref[0, 0]
        else:
            other[slot, :valid, columns] = part
            other[slot, valid:, columns] = small_ref[0, 1]
    core_copy(turn, tile).start()

    @pl.when((turn == turns - 1) & (tile == tiles - 1))
    def _():
        settle(turn)

        def take(at_tile, _):
            core_copy(turn, at_tile).wait_send()

            @pl.when(turn > 0)
            def _():
                core_copy(turn - 1, at_tile).wait_send()

            return 0

        lax.fori_loop(0, tiles, take, 0)
        for at_turn in range(mine.shape[0]):
            out_copy(at_turn).wait()


def part_chunks(valid, inner, down, small):
    chips, _, extra, width = small.shape
    units = inner.shape[1]
    tile = math.gcd(width, 512)
    block = (valid + extra, width)
    dma = pltpu.SemaphoreType.DMA
    return pl.pallas_call(
        functools.partial(part_kernel, valid),
        out_shape=jax.ShapeDtypeStruct((chips, *block), LOW),
        grid=(chips, width // tile),
        in_specs=[
            pl.BlockSpec((2 * valid, units), lambda p, j: (p, 0)),
            pl.BlockSpec((units, tile), lambda p, j: (0, j)),
            pl.BlockSpec((1, 2, extra, tile), lambda p, j: (p, 0, 0, j)),
        ],
        out_specs=pl.BlockSpec(memory_space=pl.ANY),
        scratch_shapes=[
            pltpu.VMEM((chips, *block), LOW),
            pltpu.VMEM((2, *block), LOW),
            pltpu.VMEM((chips, *block), LOW),
            dma((2, width // tile)),
            dma((chips, width // tile)),
            dma((chips,)),
        ],
        compiler_params=pltpu.CompilerParams(
            collective_id=11, has_side_effects=True, vmem_limit_bytes=52 * MIB
        ),
        cost_estimate=SMALL,
        name="part_chunks",
    )(inner, down, small)


def norm_back(rows, gain, grad):
    factor = lax.rsqrt(jnp.mean(rows * rows, axis=-1, keepdims=True) + EPS)
    scaled = gain * grad
    inner = jnp.mean(rows * scaled, axis=-1, keepdims=True)
    rows_grad = factor * scaled - (factor * factor * factor * inner) * rows
    return rows_grad, jnp.sum(grad * rows * factor, axis=0, keepdims=True)


def middle_kernel(grad_ref, rows_ref, back_ref, gain_ref, weight_ref, total_ref, low_ref, mixed_ref, part_ref):
    @pl.when(pl.program_id(0) == 0)
    def _():
        rows_grad, part_ref[...] = norm_back(rows_ref[...], gain_ref[...], grad_ref[...])
        total = back_ref[...].astype(FULL) + rows_grad
        total_ref[...] = total
        low_ref[...] = total.astype(LOW)

    mixed_ref[...] = multiply_right(low_ref[...], weight_ref[...]).astype(LOW)


def middle_back(grad, rows, back, gain, weight):
    count, width = rows.shape
    features = weight.shape[0]
    tile = math.gcd(features, 512)
    whole = pl.BlockSpec((count, width), lambda j: (0, 0))
    return pl.pallas_call(
        middle_kernel,
        out_shape=[
            jax.ShapeDtypeStruct((count, width), FULL),
            jax.ShapeDtypeStruct((count, width), LOW),
            jax.ShapeDtypeStruct((count, features), LOW),
            jax.ShapeDtypeStruct((1, width), FULL),
        ],
        grid=(features // tile,),
        in_specs=[whole, whole, whole, pl.BlockSpec((1, width), lambda j: (0, 0))]
        + [pl.BlockSpec((tile, width), lambda j: (j, 0))],
        out_specs=[whole, whole, pl.BlockSpec((count, tile), lambda j: (0, j))]
        + [pl.BlockSpec((1, width), lambda j: (0, 0))],
        compiler_params=pltpu.CompilerParams(vmem_limit_bytes=56 * MIB),
        cost_estimate=SMALL,
        name="middle_back",
    )(grad, rows, back, gain.reshape(1, width), weight)


def entry_kernel(query_ref, kv_ref, rows_ref, total_ref, gain_ref, weight_ref, out_ref, part_ref, held):
    tile = weight_ref.shape[0]
    where = pl.ds(pl.multiple_of(pl.program_id(0) * tile, 128), tile)
    features = query_ref.shape[1]
    held[:, where] = multiply_right(query_ref[...], weight_ref[:, :features]) + multiply_right(
        kv_ref[...], weight_ref[:, features:]
    )

    @pl.when(pl.program_id(0) == pl.num_programs(0) - 1)
    def _():
        rows_grad, part_ref[...] = norm_back(rows_ref[...].astype(FULL), gain_ref[...], held[...])
        out_ref[...] = total_ref[...] + rows_grad


def entry_back(query_grad, kv_grad, rows, total, gain, weight):
    count, width = rows.shape
    tile = math.gcd(width, 512)
    fixed = lambda j: (0, 0)
    whole = pl.BlockSpec((count, width), fixed)
    return pl.pallas_call(
        entry_kernel,
        out_shape=[
            jax.ShapeDtypeStruct((count, width), FULL),
            jax.ShapeDtypeStruct((1, width), FULL),
        ],
        grid=(width // tile,),
        in_specs=[
            pl.BlockSpec(query_grad.shape, fixed),
            pl.BlockSpec(kv_grad.shape, fixed),
            whole,
            whole,
            pl.BlockSpec((1, width), fixed),
            pl.BlockSpec((tile, weight.shape[1]), lambda j: (j, 0)),
        ],
        out_specs=[whole, pl.BlockSpec((1, width), fixed)],
        scratch_shapes=[pltpu.VMEM((count, width), FULL)],
        compiler_params=pltpu.CompilerParams(vmem_limit_bytes=56 * MIB),
        cost_estimate=SMALL,
        name="entry_back",
    )(query_grad, kv_grad, rows, total, gain.reshape(1, width), weight)


class CopySum:
    def __init__(self, split, values, totals, arrived, whole, sems):
        self.split, self.values, self.totals = split, values, totals
        self.arrived, self.whole = arrived, whole
        self.part_send, self.part_recv, self.whole_send, self.whole_recv = sems
        self.copies = lax.axis_size("dp")
        self.place, self.me = lax.axis_index("dp"), lax.axis_index("fsdp")

    @staticmethod
    def split_of(shapes):
        return [shape[0] % (TILE * lax.axis_size("dp")) == 0 for shape in shapes]

    @staticmethod
    def scratch(shapes):
        copies = lax.axis_size("dp")
        arrived, whole = [], []
        for (rows, columns), parts in zip(shapes, CopySum.split_of(shapes)):
            arrived.append((copies - 1, rows // copies, columns) if parts else (copies, rows, columns))
            whole.append((rows, columns) if parts else (TILE, 128))
        return [pltpu.VMEM(shape, LOW) for shape in arrived + whole]

    def rows(self, a, owner):
        part = self.values[a].shape[0] // self.copies
        return pl.ds(pl.multiple_of(owner * part, TILE), part)

    def part_copy(self, a, k):
        peer = lax.rem(self.place + k, self.copies)
        value, arrived = self.values[a], self.arrived[a]
        return pltpu.make_async_remote_copy(
            src_ref=value.at[self.rows(a, peer)] if self.split[a] else value,
            dst_ref=arrived.at[k - 1] if self.split[a] else arrived.at[self.place],
            send_sem=self.part_send.at[a, k],
            recv_sem=self.part_recv.at[a, k],
            device_id=(peer, self.me),
            device_id_type=pl.DeviceIdType.MESH,
        )

    def whole_copy(self, a, k):
        where = self.rows(a, self.place)
        return pltpu.make_async_remote_copy(
            src_ref=self.whole[a].at[where],
            dst_ref=self.whole[a].at[where],
            send_sem=self.whole_send.at[a, k],
            recv_sem=self.whole_recv.at[a, k],
            device_id=(lax.rem(self.place + k, self.copies), self.me),
            device_id_type=pl.DeviceIdType.MESH,
        )

    def send(self, a):
        for k in range(1, self.copies):
            self.part_copy(a, k).start()

    def reduce(self, a):
        value, arrived = self.values[a], self.arrived[a]
        if not self.split[a]:
            arrived[self.place] = value[...]
        for k in range(1, self.copies):
            self.part_copy(a, k).wait_recv()
        if self.split[a]:
            total = value[self.rows(a, self.place)].astype(FULL)
            for k in range(1, self.copies):
                total = total + arrived[k - 1].astype(FULL)
            self.whole[a][self.rows(a, self.place)] = total.astype(LOW)
            for k in range(1, self.copies):
                self.whole_copy(a, k).start()
        else:
            total = arrived[0].astype(FULL)
            for k in range(1, self.copies):
                total = total + arrived[k].astype(FULL)
            self.totals[a][...] = total

    def finish(self, a):
        for k in range(1, self.copies):
            self.part_copy(a, k).wait_send()
            if self.split[a]:
                self.whole_copy(a, k).wait_send()
                self.whole_copy(a, k).wait_recv()
        if self.split[a]:
            self.totals[a][...] = self.whole[a][...].astype(FULL)


def tail_kernel(split, *refs):
    count = len(split)
    given = count - 3
    inputs, refs = refs[:given], refs[given:]
    summed_ref, left_ref, right_ref = refs[:3]
    totals, all_ref, refs = refs[3 : 3 + count], refs[3 + count], refs[4 + count :]
    arrived, whole, refs = refs[:count], refs[count : 2 * count], refs[2 * count :]
    held, arrive, total, action, weights, gains, right_all = refs[:7]
    load_sem, right_sem, line_send, line_recv = refs[7:11]
    sums = CopySum(split, (*inputs, action, weights, gains), totals, arrived, whole, refs[11:15])
    gather = Gather([1], [right_ref], [all_ref], refs[15:])
    mesh = pl.DeviceIdType.MESH
    place, me = lax.axis_index("dp"), lax.axis_index("fsdp")
    chips = lax.axis_size("fsdp") // 2
    chip = me // 2

    load = pltpu.make_async_copy(summed_ref, held, load_sem)
    load.start()
    gather.greet()
    gather.start()
    load.wait()

    def valid_at(side, step):
        return chip <= step - 1 if side == 0 else chip >= chips - step

    def fed(side):
        return chip > 0 if side == 0 else chip < chips - 1

    def line_copy(side, step, owner):
        return pltpu.make_async_remote_copy(
            src_ref=held.at[owner],
            dst_ref=arrive.at[side, step - 1],
            send_sem=line_send.at[side, step - 1],
            recv_sem=line_recv.at[side, step - 1],
            device_id=(place, me + 2 if side == 0 else me - 2),
            device_id_type=mesh,
        )

    for step in range(1, chips):
        for side in range(2):

            @pl.when(valid_at(side, step))
            def _(step=step, side=side):
                owner = chip + chips - step if side == 0 else chip - chips + step
                if step > 1:

                    @pl.when(fed(side))
                    def _():
                        line_copy(side, step - 1, chip).wait_recv()
                        held[owner] = (
                            held[owner].astype(FULL) + arrive[side, step - 2].astype(FULL)
                        ).astype(LOW)

                line_copy(side, step, owner).start()

        gather.advance(step)
        if step == 1:
            for a in range(given):
                sums.send(a)
        if step == min(2, chips - 1):
            for a in range(given):
                sums.reduce(a)
    gather.finish()
    fetch = pltpu.make_async_copy(all_ref, right_all, right_sem)
    fetch.start()
    fetch.wait()
    action[...] = multiply_left(left_ref[...], right_all[...]).astype(LOW)
    sums.send(given)
    total[...] = held[chip].astype(FULL)
    for side in range(2):

        @pl.when(fed(side))
        def _(side=side):
            line_copy(side, chips - 1, chip).wait_recv()
            total[...] += arrive[side, chips - 2].astype(FULL)

    rows = weights.shape[0]
    weights[...] = total[:rows].astype(LOW)
    gains[...] = total[rows:].astype(LOW)
    for a in range(given + 1, count):
        sums.send(a)
    for a in range(given):
        sums.finish(a)
    for a in range(given, count):
        sums.reduce(a)
    for step in range(1, chips):
        for side in range(2):

            @pl.when(valid_at(side, step))
            def _(step=step, side=side):
                line_copy(side, step, chip).wait_send()

    for a in range(given, count):
        sums.finish(a)


def tail_sums(values, summed, rows, left, right):
    chips, block = summed.shape[0], summed.shape[1:]
    own = [(left.shape[1], right.shape[1]), (rows, block[1]), (block[0] - rows, block[1])]
    shapes = [value.shape for value in values] + own
    count = len(shapes)
    dma = pltpu.SemaphoreType.DMA
    copies = lax.axis_size("dp")
    inside = pl.BlockSpec(memory_space=pltpu.VMEM)
    anywhere = pl.BlockSpec(memory_space=pl.ANY)
    outs = pl.pallas_call(
        functools.partial(tail_kernel, CopySum.split_of(shapes)),
        out_shape=[jax.ShapeDtypeStruct(shape, FULL) for shape in shapes] + whole_shapes([right]),
        in_specs=[inside] * len(values) + [anywhere, inside, anywhere],
        out_specs=[inside] * count + [anywhere],
        scratch_shapes=CopySum.scratch(shapes)
        + [
            pltpu.VMEM((chips, *block), LOW),
            pltpu.VMEM((2, chips - 1, *block), LOW),
            pltpu.VMEM(block, FULL),
            *(pltpu.VMEM(shape, LOW) for shape in own),
            pltpu.VMEM((2 * chips * right.shape[0], right.shape[1]), LOW),
            dma,
            dma,
            dma((2, chips - 1)),
            dma((2, chips - 1)),
        ]
        + [dma((count, copies))] * 4
        + Gather.scratch(1),
        compiler_params=pltpu.CompilerParams(
            collective_id=6, has_side_effects=True, vmem_limit_bytes=58 * MIB
        ),
        cost_estimate=pl.CostEstimate(
            flops=30_000_000_000, bytes_accessed=1, transcendentals=0
        ),
        name="tail_sums",
    )(*values, summed, left, right)
    return outs[:count]


def widen_kernel(*refs):
    count = len(refs) - 1
    for k, ref in enumerate(refs[:-1]):

        @pl.when(pl.program_id(0) == k)
        def _(ref=ref):
            refs[-1][...] = ref[...].astype(FULL)


def widen(*values):
    count, (rows, columns) = len(values), values[0].shape
    tile = math.gcd(rows, 256)
    return pl.pallas_call(
        widen_kernel,
        out_shape=jax.ShapeDtypeStruct((count * rows, columns), FULL),
        grid=(count, rows // tile),
        in_specs=[pl.BlockSpec((tile, columns), lambda k, i: (i, 0))] * count,
        out_specs=pl.BlockSpec((tile, columns), lambda k, i: (k * (rows // tile) + i, 0)),
        compiler_params=pltpu.CompilerParams(vmem_limit_bytes=32 * MIB),
        cost_estimate=SMALL,
        name="widen",
    )(*values)


def share_kernel(core_ref, left_ref, right_ref, *refs):
    rows = left_ref.shape[1]
    refs[-1][0, :rows] = multiply_left(left_ref[...], right_ref[...]).astype(LOW)
    if len(refs) > 1:
        refs[-1][0, rows:] = refs[0][0]


def weight_shares(core, left, right, gains=None):
    size = lax.axis_size("fsdp")
    chips = size // 2
    count, rows = left.shape[0], left.shape[1] // size
    width, total, extra = right.shape[1], rows, []
    if gains is not None:
        total += gains.shape[1]
        extra = [pl.BlockSpec((1, *gains.shape[1:]), lambda c, core: (2 * c + core[0], 0, 0))]
    return pl.pallas_call(
        share_kernel,
        out_shape=jax.ShapeDtypeStruct((chips, total, width), LOW),
        grid_spec=pltpu.PrefetchScalarGridSpec(
            num_scalar_prefetch=1,
            grid=(chips,),
            in_specs=[
                pl.BlockSpec((count, rows), lambda c, core: (0, 2 * c + core[0])),
                pl.BlockSpec((count, width), lambda c, core: (0, 0)),
            ]
            + extra,
            out_specs=pl.BlockSpec((1, total, width), lambda c, core: (c, 0, 0)),
        ),
        compiler_params=pltpu.CompilerParams(vmem_limit_bytes=48 * MIB),
        cost_estimate=SMALL,
        name="weight_shares",
    )(
        jnp.reshape(core, (1,)).astype(jnp.int32),
        left,
        right,
        *([] if gains is None else [gains]),
    )


def entry_forward_kernel(rows_ref, gain_ref, weight_ref, hidden_ref, out_ref):
    @pl.when(pl.program_id(0) == 0)
    def _():
        hidden_ref[...] = normalize(rows_ref[...].astype(FULL), gain_ref[...]).astype(LOW)

    out_ref[...] = multiply(hidden_ref[...], weight_ref[...]).astype(LOW)


def entry_forward(rows, gain, weight):
    count, width = rows.shape
    columns = weight.shape[1]
    tile = math.gcd(columns, 512)
    whole = pl.BlockSpec((count, width), lambda j: (0, 0))
    return pl.pallas_call(
        entry_forward_kernel,
        out_shape=[
            jax.ShapeDtypeStruct((count, width), LOW),
            jax.ShapeDtypeStruct((count, columns), LOW),
        ],
        grid=(columns // tile,),
        in_specs=[
            whole,
            pl.BlockSpec((1, width), lambda j: (0, 0)),
            pl.BlockSpec((width, tile), lambda j: (0, j)),
        ],
        out_specs=[whole, pl.BlockSpec((count, tile), lambda j: (0, j))],
        compiler_params=pltpu.CompilerParams(vmem_limit_bytes=48 * MIB),
        cost_estimate=SMALL,
        name="entry_forward",
    )(rows, gain.reshape(1, width), weight)


def middle_forward_kernel(mixed_ref, rows_ref, gain_ref, weight_ref, *refs):
    mid_ref, hidden_ref = refs[-2:]
    tile = weight_ref.shape[1]
    where = pl.ds(pl.multiple_of(pl.program_id(0) * tile, 128), tile)
    mid_ref[:, where] = rows_ref[:, where].astype(FULL) + multiply(mixed_ref[...], weight_ref[...])

    @pl.when(pl.program_id(0) == pl.num_programs(0) - 1)
    def _():
        count = mid_ref.shape[0]
        hidden_ref[:count] = normalize(mid_ref[...], gain_ref[...]).astype(LOW)
        if len(refs) > 2:
            hidden_ref[count:] = refs[0][...]


def middle_forward(mixed, rows, gain, weight, below=None):
    count, width = rows.shape
    features = mixed.shape[1]
    tile = math.gcd(width, 512)
    fixed = lambda j: (0, 0)
    extra = [] if below is None else [below]
    total = count + sum(value.shape[0] for value in extra)
    return pl.pallas_call(
        middle_forward_kernel,
        out_shape=[
            jax.ShapeDtypeStruct((count, width), FULL),
            jax.ShapeDtypeStruct((total, width), LOW),
        ],
        grid=(width // tile,),
        in_specs=[
            pl.BlockSpec((count, features), fixed),
            pl.BlockSpec((count, width), fixed),
            pl.BlockSpec((1, width), fixed),
            pl.BlockSpec((features, tile), lambda j: (0, j)),
        ]
        + [pl.BlockSpec(value.shape, fixed) for value in extra],
        out_specs=[pl.BlockSpec((count, width), fixed), pl.BlockSpec((total, width), fixed)],
        compiler_params=pltpu.CompilerParams(vmem_limit_bytes=48 * MIB),
        cost_estimate=SMALL,
        name="middle_forward",
    )(mixed, rows, gain.reshape(1, width), weight, *extra)


def stacked(refs, columns=slice(None)):
    return jnp.concatenate([ref[0, :, columns] for ref in refs], axis=0)


def softmax_of(queries, keys, bias, scale):
    scores = multiply_right(queries, keys) * scale + bias
    raised = jnp.exp(scores - jnp.max(scores, axis=-1, keepdims=True))
    return raised / jnp.sum(raised, axis=-1, keepdims=True)


def mix_kernel(scale, features, shares, *refs):
    count = len(shares)
    prefix_ref, action_ref, prefix_all_ref, action_all_ref, bias_ref = refs[:5]
    shards, refs = refs[5 : 5 + count], refs[5 + count :]
    prefix_out, action_out, kv_out = refs[:3]
    wholes, refs = refs[3 : 3 + count], refs[3 + count :]
    held, send_sem, recv_sem, out_sem = refs[:4]
    gather = Gather(shares, shards, wholes, refs[4:])
    copies = lax.axis_size("dp")
    place, me = lax.axis_index("dp"), lax.axis_index("fsdp")
    item, head = pl.program_id(0), pl.program_id(1)
    items, rows = prefix_all_ref.shape[0], prefix_ref.shape[1]
    heads = pl.num_programs(1)
    turn = item * heads + head

    def copy(at, k):
        return pltpu.make_async_remote_copy(
            src_ref=held.at[0, at],
            dst_ref=held.at[k, at],
            send_sem=send_sem.at[at, k],
            recv_sem=recv_sem.at[at, k],
            device_id=(lax.rem(place + k, copies), me),
            device_id_type=pl.DeviceIdType.MESH,
        )

    @pl.when((item == 0) & (head == 0))
    def _():
        for at in range(items):
            held[0, at, :rows] = prefix_all_ref[at, :, features:]
            held[0, at, rows:] = action_all_ref[at, :, features:]
        gather.greet()
        for at in range(items):
            for k in range(1, copies):
                copy(at, k).start()
        gather.start()

    @pl.when(head == 0)
    def _():
        for k in range(1, copies):
            copy(item, k).wait_recv()

    every = 2 if gather.chips <= items * features // kv_out.shape[3] else 1

    @pl.when((turn > 0) & (lax.rem(turn, every) == 0) & (turn < every * gather.chips))
    def _():
        gather.advance(turn // every)

    queries = stacked((prefix_ref, action_ref))
    kv = jnp.concatenate([held[k, item] for k in range(copies)], axis=0)
    head_size = kv.shape[1] // 2
    probs = softmax_of(queries, kv[:, :head_size], bias_ref[0], scale).astype(LOW)
    mixed = multiply(probs, kv[:, head_size:]).astype(LOW)
    prefix_out[0] = mixed[:rows]
    action_out[0] = mixed[rows:]

    @pl.when((item == items - 1) & (head == pl.num_programs(1) - 1))
    def _():
        whole = pltpu.make_async_copy(held, kv_out, out_sem)
        whole.start()
        for at in range(items):
            for k in range(1, copies):
                copy(at, k).wait_send()
        whole.wait()
        gather.finish()


def mix_back_kernel(scale, shares, *refs):
    count = len(shares)
    prefix_ref, action_ref, prefix_grad_ref, action_grad_ref, bias_ref, kv_ref = refs[:6]
    shards, refs = refs[6 : 6 + count], refs[6 + count :]
    prefix_out, action_out, kv_out = refs[:3]
    wholes, refs = refs[3 : 3 + count], refs[3 + count :]
    total, own, sent, arrived, send_sem, recv_sem = refs[:6]
    gather = Gather(shares, shards, wholes, refs[6:])
    copies = lax.axis_size("dp")
    place, me = lax.axis_index("dp"), lax.axis_index("fsdp")
    item, head = pl.program_id(0), pl.program_id(1)
    items, heads = pl.num_programs(0), pl.num_programs(1)
    rows = prefix_ref.shape[1]
    step = rows + action_ref.shape[1]
    turn = item * heads + head

    def copy(at, k):
        return pltpu.make_async_remote_copy(
            src_ref=sent.at[at, k - 1],
            dst_ref=arrived.at[at, k - 1],
            send_sem=send_sem.at[at, k],
            recv_sem=recv_sem.at[at, k],
            device_id=(lax.rem(place + copies - k, copies), me),
            device_id_type=pl.DeviceIdType.MESH,
        )

    @pl.when(turn == 0)
    def _():
        gather.greet()
        gather.start()

    @pl.when((turn > 0) & (turn < gather.chips))
    def _():
        gather.advance(turn)

    @pl.when(head == 0)
    def _():
        total[...] = jnp.zeros_like(total)

    queries = stacked((prefix_ref, action_ref))
    grads = stacked((prefix_grad_ref, action_grad_ref))
    kv = jnp.concatenate([kv_ref[k, 0] for k in range(copies)], axis=0)
    head_size = kv.shape[1] // 2
    keys, values = kv[:, :head_size], kv[:, head_size:]
    probs = softmax_of(queries, keys, bias_ref[0], scale)
    probs_grad = multiply_right(grads, values)
    delta = jnp.sum(probs * probs_grad, axis=-1, keepdims=True)
    score_grad = (probs * (probs_grad - delta)).astype(LOW)
    query_grad = (multiply(score_grad, keys) * scale).astype(LOW)
    prefix_out[0] = query_grad[:rows]
    action_out[0] = query_grad[rows:]
    total[:, :head_size] += multiply_left(score_grad, queries) * scale
    total[:, head_size:] += multiply_left(probs.astype(LOW), grads)

    @pl.when(head == heads - 1)
    def _():
        own[item] = total[:step]
        for k in range(1, copies):
            sent[item, k - 1] = total[k * step : (k + 1) * step].astype(LOW)
            copy(item, k).start()

    @pl.when((item == items - 1) & (head == heads - 1))
    def _():
        for at in range(kv_out.shape[0]):
            for k in range(1, copies):
                copy(at, k).wait_recv()
                copy(at, k).wait_send()
            summed = own[at]
            for k in range(1, copies):
                summed = summed + arrived[at, k - 1].astype(FULL)
            kv_out[at] = summed.astype(LOW)
        gather.finish()


def mix_call(scale, heads, prefix, action, bias, grads=None, kv=None, shards=()):
    copies = lax.axis_size("dp")
    items, prefix_rows, columns = prefix.shape
    action_rows = action.shape[1]
    rows, length = prefix_rows + action_rows, bias.shape[2]
    head_size = columns // (heads + 2)
    features = heads * head_size
    per_head = [
        pl.BlockSpec((1, prefix_rows, head_size), lambda i, h: (i, 0, h)),
        pl.BlockSpec((1, action_rows, head_size), lambda i, h: (i, 0, h)),
    ]
    bias_spec = pl.BlockSpec((1, rows, length), lambda i, h: (i, 0, 0))
    shapes = [
        jax.ShapeDtypeStruct((items, prefix_rows, features), LOW),
        jax.ShapeDtypeStruct((items, action_rows, features), LOW),
    ]
    dma = pltpu.SemaphoreType.DMA
    sems = [dma((items, copies)), dma((items, copies))]
    block = (rows, 2 * head_size)
    if grads is None:
        return pl.pallas_call(
            functools.partial(mix_kernel, scale, features, shares_of(shards)),
            out_shape=shapes
            + [jax.ShapeDtypeStruct((copies, items, *block), LOW)]
            + whole_shapes(shards),
            grid=(items, heads),
            in_specs=per_head
            + [
                pl.BlockSpec(prefix.shape, lambda i, h: (0, 0, 0)),
                pl.BlockSpec(action.shape, lambda i, h: (0, 0, 0)),
                bias_spec,
            ]
            + [pl.BlockSpec(memory_space=pl.ANY)] * len(shards),
            out_specs=per_head + [pl.BlockSpec(memory_space=pl.ANY)] * (1 + len(shards)),
            scratch_shapes=[pltpu.VMEM((copies, items, *block), LOW), *sems, dma]
            + Gather.scratch(len(shards)),
            compiler_params=pltpu.CompilerParams(
                collective_id=7, has_side_effects=True, vmem_limit_bytes=48 * MIB
            ),
            cost_estimate=SMALL,
            name="mix",
        )(prefix, action, prefix, action, bias, *shards)
    return pl.pallas_call(
        functools.partial(mix_back_kernel, scale, shares_of(shards)),
        out_shape=shapes + [jax.ShapeDtypeStruct((items, *block), LOW)] + whole_shapes(shards),
        grid=(items, heads),
        in_specs=per_head * 2
        + [bias_spec, pl.BlockSpec((copies, 1, *block), lambda i, h: (0, i, 0, 0))]
        + [pl.BlockSpec(memory_space=pl.ANY)] * len(shards),
        out_specs=per_head
        + [pl.BlockSpec((items, *block), lambda i, h: (0, 0, 0))]
        + [pl.BlockSpec(memory_space=pl.ANY)] * len(shards),
        scratch_shapes=[
            pltpu.VMEM((length, 2 * head_size), FULL),
            pltpu.VMEM((items, *block), FULL),
            pltpu.VMEM((items, copies - 1, *block), LOW),
            pltpu.VMEM((items, copies - 1, *block), LOW),
            *sems,
            *Gather.scratch(len(shards)),
        ],
        compiler_params=pltpu.CompilerParams(
            collective_id=8, has_side_effects=True, vmem_limit_bytes=48 * MIB
        ),
        cost_estimate=SMALL,
        name="mix_back",
    )(prefix, action, *grads, bias, kv, *shards)


def body(
    prefix_in,
    action_in,
    valid_count,
    prefix_before,
    prefix_query,
    prefix_key,
    prefix_value,
    prefix_output,
    prefix_middle,
    prefix_gate,
    prefix_up,
    prefix_down,
    action_before,
    action_query,
    action_key,
    action_value,
    action_output,
    action_middle,
    action_gate,
    action_up,
    action_down,
    prefix_cotangent,
    action_cotangent,
):
    line = Line()
    shards = line.size
    copies = lax.axis_size("dp")
    items, prefix_rows, width = prefix_in.shape
    action_rows = action_in.shape[1]
    action_width = action_in.shape[2]
    head_size = prefix_key.shape[1]
    features = prefix_query.shape[1]
    heads = features // head_size
    columns = features + 2 * head_size
    prefix_length = prefix_rows * copies
    scale = head_size ** (-0.5)
    place = lax.axis_index("dp")
    prefix_pad, action_pad = rounded(prefix_rows), rounded(action_rows)
    prefix_tokens, action_tokens = items * prefix_pad, items * action_pad
    folded = action_tokens * action_width // width
    folded_pad = rounded(folded)

    def padded(prefix, action):
        prefix = jnp.pad(prefix, ((0, 0), (0, prefix_pad - prefix_rows), (0, 0)))
        action = jnp.pad(action, ((0, 0), (0, action_pad - action_rows), (0, 0)))
        return prefix.reshape(prefix_tokens, width), action.reshape(action_tokens, action_width)

    def trimmed(prefix, action):
        prefix = prefix.reshape(items, prefix_pad, width)[:, :prefix_rows]
        return prefix, action.reshape(items, action_pad, action_width)[:, :action_rows]

    def fold(action):
        rows = action.reshape(-1, folded, width)
        return jnp.pad(rows, ((0, 0), (0, folded_pad - folded), (0, 0)))

    def unfold(rows):
        return rows[:folded].reshape(action_tokens, action_width)

    def pack(prefix, action):
        return jnp.concatenate([prefix, fold(action)[0]], axis=0)

    def unpack(packed):
        return packed[:prefix_tokens], unfold(packed[prefix_tokens:])

    share, action_share = prefix_before.shape[0], action_before.shape[0]
    cuts = [0, share, 2 * share, 2 * share + action_share, 2 * share + 2 * action_share]
    gain_rows = rounded(-(-cuts[4] // 128))
    gains = jnp.concatenate([prefix_before, prefix_middle, action_before, action_middle])
    gains = jnp.pad(gains, (0, gain_rows * 128 - cuts[4])).reshape(gain_rows, 128)
    prefix_qkv, action_qkv, gains = gather_shards(
        0,
        jnp.concatenate([prefix_query, prefix_key, prefix_value], axis=1),
        jnp.concatenate([action_query, action_key, action_value], axis=1),
        gains,
    )
    gains = gains.reshape(shards, gain_rows * 128).astype(FULL)
    prefix_gain_in, prefix_gain, action_gain_in, action_gain = (
        gains[:, cuts[i] : cuts[i + 1]].reshape(-1) for i in range(4)
    )

    live = (place * action_rows + jnp.arange(action_rows))[None, :] < valid_count[:, None]
    prefix_back, action_back = padded(
        prefix_cotangent,
        jnp.where(live[:, :, None], action_cotangent, jnp.zeros_like(action_cotangent)),
    )
    backs = lax.all_gather(pack(prefix_back, action_back), "fsdp", axis=0, tiled=True)

    prefix_flat, action_flat = padded(prefix_in, action_in)
    prefix_hidden, prefix_all = entry_forward(prefix_flat, prefix_gain_in, prefix_qkv)
    prefix_all = prefix_all.reshape(items, prefix_pad, columns)
    action_hidden, action_all = entry_forward(action_flat, action_gain_in, action_qkv)
    action_all = action_all.reshape(items, action_pad, columns)
    far = copies * (prefix_rows + action_rows)

    def places(owner):
        prefix = jnp.arange(prefix_pad)
        action = jnp.arange(action_pad)
        return jnp.concatenate(
            [
                jnp.where(prefix < prefix_rows, owner * prefix_rows + prefix, far),
                jnp.where(
                    action < action_rows, prefix_length + owner * action_rows + action, far
                ),
            ]
        )

    query_place = places(place)
    key_place = jnp.concatenate([places((place + copies - k) % copies) for k in range(copies)])
    later = (query_place[:, None] >= prefix_length) & (key_place[None, :] <= query_place[:, None])
    allowed = (key_place[None, None, :] < prefix_length) | later[None] & (
        key_place[None, None, :] < prefix_length + valid_count[:, None, None]
    )
    bias = jnp.where(allowed, 0.0, NEGATIVE).astype(FULL)
    prefix_mixed, action_mixed, kv, prefix_o, action_o = mix_call(
        scale, heads, prefix_all, action_all, bias, shards=(prefix_output, action_output)
    )
    backs, prefix_mixed = lax.optimization_barrier((backs, prefix_mixed))
    action_mixed = action_mixed.reshape(action_tokens, features)
    prefix_mixed = prefix_mixed.reshape(prefix_tokens, features)
    action_mid, action_ffn = middle_forward(action_mixed, action_flat, action_gain, action_o)
    prefix_mid, hidden = middle_forward(
        prefix_mixed, prefix_flat, prefix_gain, prefix_o, fold(action_ffn)[0]
    )
    inner, gate_grad, up_grad, all_rows, all_back, small = feed_all(
        prefix_tokens, hidden, backs, prefix_gate, prefix_up, prefix_down
    )
    action_rows_all, action_back_all = (
        small[i, :, :, :folded].reshape(shards * action_tokens, action_width) for i in range(2)
    )
    action_inner, pull = jax.vjp(
        activate, multiply(action_rows_all, action_gate), multiply(action_rows_all, action_up)
    )
    action_inner = action_inner.astype(LOW)
    action_gate_grad, action_up_grad = (
        v.astype(LOW) for v in pull(multiply_right(action_back_all, action_down))
    )

    down_grad = multiply_left(inner, all_back).astype(LOW)
    action_feed = tuple(
        v.astype(LOW)
        for v in (
            multiply_left(action_rows_all, action_gate_grad),
            multiply_left(action_rows_all, action_up_grad),
            multiply_left(action_inner, action_back_all),
        )
    )
    gate_weight_grad = multiply_left(all_rows, gate_grad).astype(LOW)
    gate_grad, up_grad, down_grad, gate_weight_grad = lax.optimization_barrier(
        (gate_grad, up_grad, down_grad, gate_weight_grad)
    )
    def halves(rows):
        return fold(rows.astype(LOW)).reshape(line.chips, 2, folded_pad, width)

    up_weight_grad = multiply_left(all_rows, up_grad).astype(LOW)
    gate_grad, up_grad, down_grad, gate_weight_grad, up_weight_grad, action_feed = (
        lax.optimization_barrier(
            (gate_grad, up_grad, down_grad, gate_weight_grad, up_weight_grad, action_feed)
        )
    )
    feed_sums = lax.psum((down_grad, gate_weight_grad, up_weight_grad, *action_feed), "dp")
    parts = part_chunks(
        prefix_tokens,
        lax.optimization_barrier((inner, up_weight_grad))[0],
        prefix_down,
        halves(multiply(action_inner, action_down)),
    )
    sent, gate_grad = lax.optimization_barrier((parts, gate_grad))
    out_sums = Relay(line, sent, lambda chip: line.chip ^ chip)
    out_sums.advance(1)
    small = halves(
        multiply_right(action_gate_grad, action_gate) + multiply_right(action_up_grad, action_up)
    )
    feed_back = collect(
        2, prefix_tokens, True, (gate_grad, up_grad), (prefix_gate, prefix_up), small, width
    )
    feed_back = out_sums.after(feed_back)
    out_sums.advance(2)

    prefix_mid_grad, prefix_low, prefix_mixed_grad, prefix_middle_part = middle_back(
        feed_back, prefix_mid, prefix_back, prefix_gain, prefix_o
    )
    action_mid_grad, action_low, action_mixed_grad, action_middle_part = middle_back(
        unfold(feed_back[prefix_tokens:]), action_mid, action_back, action_gain, action_o
    )
    sent = line.pairs(9, prefix_mixed, prefix_low)
    output_sums = Relay(line, sent, lambda chip: chip)
    output_sums.advance(1)
    mixed_grads = (
        prefix_mixed_grad.reshape(items, prefix_pad, features),
        action_mixed_grad.reshape(items, action_pad, features),
    )
    tokens_all = jnp.concatenate([action_hidden, action_mixed, action_low], axis=1)
    prefix_query_grad, action_query_grad, kv_grad, tokens_all = mix_call(
        scale, heads, prefix_all, action_all, bias, mixed_grads, kv, (tokens_all,)
    )
    kv_grad = output_sums.after(out_sums.after(kv_grad))
    output_sums.advance(2)
    prefix_qkv_grad = jnp.concatenate([prefix_query_grad, kv_grad[:, :prefix_pad]], axis=2)
    action_qkv_grad = jnp.concatenate([action_query_grad, kv_grad[:, prefix_pad:]], axis=2)
    prefix_qkv_grad = prefix_qkv_grad.reshape(prefix_tokens, columns)
    action_qkv_grad = action_qkv_grad.reshape(action_tokens, columns)
    prefix_grad, prefix_before_part = entry_back(
        prefix_query_grad.reshape(prefix_tokens, features),
        kv_grad[:, :prefix_pad].reshape(prefix_tokens, 2 * head_size),
        prefix_flat,
        prefix_mid_grad,
        prefix_gain_in,
        prefix_qkv,
    )
    action_grad, action_before_part = entry_back(
        action_query_grad.reshape(action_tokens, features),
        kv_grad[:, prefix_pad:].reshape(action_tokens, 2 * head_size),
        action_flat,
        action_mid_grad,
        action_gain_in,
        action_qkv,
    )
    prefix_grad, action_grad = trimmed(prefix_grad, action_grad)

    gain_parts = jnp.concatenate(
        [
            part.reshape(shards, -1)
            for part in (
                prefix_before_part,
                prefix_middle_part,
                action_before_part,
                action_middle_part,
            )
        ],
        axis=1,
    )
    gain_rows = rounded(-(-cuts[4] // columns))
    gain_parts = jnp.pad(gain_parts, ((0, 0), (0, gain_rows * columns - cuts[4])))
    gain_parts = gain_parts.astype(LOW).reshape(shards, gain_rows, columns)
    gain_parts = output_sums.after(gain_parts)
    output_sums.advance(3)
    sent = line.pairs(10, prefix_hidden, prefix_qkv_grad, gain_parts)
    edges = [0]
    for part in (action_width, features, action_width):
        edges.append(edges[-1] + part)
    hidden_all, mixed_all, low_all = (
        tokens_all[:, start:stop] for start, stop in zip(edges, edges[1:])
    )
    rows = action_query.shape[0]
    hidden_slice = lax.dynamic_slice_in_dim(hidden_all, line.place * rows, rows, 1)
    rows = action_output.shape[0]
    action_output_owned = multiply_left(
        lax.dynamic_slice_in_dim(mixed_all, line.place * rows, rows, 1), low_all
    )
    output_owned, action_output_owned, action_qkv_owned, qkv_owned, gain_owned = tail_sums(
        [output_sums.finish().astype(LOW), action_output_owned.astype(LOW)],
        sent,
        prefix_query.shape[0],
        hidden_slice,
        action_qkv_grad,
    )
    feed_sums, output_owned, sent = lax.optimization_barrier((feed_sums, output_owned, sent))
    out_sums.advance(3)
    out_sums.arrived, output_owned = lax.optimization_barrier((out_sums.arrived, output_owned))
    feed_sums = [widen(value) for value in feed_sums]
    sums = unpack(out_sums.finish())
    prefix_out, action_out = trimmed(
        (prefix_mid + sums[0]).astype(LOW), (action_mid + sums[1]).astype(LOW)
    )
    gain_owned = gain_owned.reshape(-1)
    return (
        prefix_out,
        action_out,
        prefix_grad,
        action_grad,
        gain_owned[cuts[0] : cuts[1]],
        qkv_owned[:rows, :features],
        qkv_owned[:rows, features : features + head_size],
        qkv_owned[:rows, features + head_size :],
        output_owned,
        gain_owned[cuts[1] : cuts[2]],
        feed_sums[1],
        feed_sums[2],
        feed_sums[0],
        gain_owned[cuts[2] : cuts[3]],
        action_qkv_owned[:, :features],
        action_qkv_owned[:, features : features + head_size],
        action_qkv_owned[:, features + head_size :],
        action_output_owned,
        gain_owned[cuts[3] : cuts[4]],
        *feed_sums[3:],
    )


def solution(mesh):
    tokens = P("fsdp", "dp", None)
    rows, columns, vector = P("fsdp", None), P(None, "fsdp"), P("fsdp")
    weights = (vector, rows, rows, rows, rows, vector, columns, columns, rows)
    return jax.shard_map(
        body,
        mesh=mesh,
        in_specs=(tokens, tokens, vector, *weights, *weights, tokens, tokens),
        out_specs=(tokens, tokens, tokens, tokens, *weights, *weights),
        check_vma=False,
    )
```

```python
import functools
import math

import jax
import jax.numpy as jnp
from jax import lax
from jax.experimental import pallas as pl
from jax.experimental.pallas import tpu as pltpu
from jax.sharding import PartitionSpec as P

EPS = 1e-06
NEGATIVE = -1e30
LOW = jnp.bfloat16
FULL = jnp.float32
TILE = 16
MIB = 1 << 20
SMALL = pl.CostEstimate(flops=1, bytes_accessed=1, transcendentals=0)


def normalize(rows, gain):
    return rows * lax.rsqrt(jnp.mean(rows * rows, axis=-1, keepdims=True) + EPS) * gain


def multiply(left, right):
    return jnp.dot(left, right, preferred_element_type=FULL)


def multiply_left(left, right):
    return lax.dot_general(
        left, right, (((0,), (0,)), ((), ())), preferred_element_type=FULL
    )


def multiply_right(left, right):
    return lax.dot_general(
        left, right, (((1,), (1,)), ((), ())), preferred_element_type=FULL
    )


def activate(gate, upper):
    return jax.nn.gelu(gate, approximate=True) * upper


class Line:
    def __init__(self):
        self.size = lax.axis_size("fsdp")
        self.chips = self.size // 2
        self.place = lax.axis_index("fsdp")
        self.chip = self.place // 2
        self.core = self.place % 2

    def move(self, value, chips, step):
        pairs = [
            (2 * chip + core, 2 * (chip + step) + core) for chip in chips for core in range(2)
        ]
        return lax.ppermute(value, "fsdp", pairs)

    def pairs(self, identity, *values):
        mine, other = (weight_shares(core, *values) for core in (self.core, 1 - self.core))
        return add_pairs(identity, mine, other)


class Relay:
    def __init__(self, line, summed, index):
        self.line, self.summed, self.index = line, summed, index
        self.taken, self.arrived = 0, []

    def advance(self, part, parts=3):
        line, count = self.line, self.line.chips
        last = -(-(count - 1) * part // parts)
        while self.taken < last:
            self.taken += 1
            step, arrived = self.taken, self.arrived
            self.arrived = []
            for i, side in enumerate((1, -1)):
                target = self.index(jnp.clip(line.chip + side * (count - step), 0, count - 1))
                if arrived:
                    payload = add_block(self.summed, target, [arrived[i]], LOW)
                else:
                    payload = lax.dynamic_index_in_dim(self.summed, target, 0, keepdims=False)
                chips = range(0, step) if side == 1 else range(count - step, count)
                self.arrived.append(line.move(payload, chips, side))

    def after(self, values):
        self.arrived, values = lax.optimization_barrier((self.arrived, values))
        return values

    def finish(self):
        self.advance(1, 1)
        return add_block(self.summed, self.index(self.line.chip), self.arrived, FULL)


def add_kernel(index_ref, value_ref, *refs):
    total = value_ref[0].astype(FULL)
    for ref in refs[:-1]:
        total = total + ref[...].astype(FULL)
    refs[-1][...] = total.astype(refs[-1].dtype)


def add_block(values, index, others, kind):
    shape = values.shape[1:]
    block = pl.BlockSpec(shape, lambda i, index: (0, 0))
    return pl.pallas_call(
        add_kernel,
        out_shape=jax.ShapeDtypeStruct(shape, kind),
        grid_spec=pltpu.PrefetchScalarGridSpec(
            num_scalar_prefetch=1,
            grid=(1,),
            in_specs=[pl.BlockSpec((1, *shape), lambda i, index: (index[0], 0, 0))]
            + [block] * len(others),
            out_specs=block,
        ),
        compiler_params=pltpu.CompilerParams(vmem_limit_bytes=40 * MIB),
        cost_estimate=SMALL,
        name="add_block",
    )(jnp.reshape(index, (1,)).astype(jnp.int32), values, *others)


def pair_kernel(mine_ref, other_ref, out_ref, landed, send_sem, recv_sem):
    place, me = lax.axis_index("dp"), lax.axis_index("fsdp")
    partner = (place, me + 1 - 2 * (me % 2))
    mesh = pl.DeviceIdType.MESH
    turn, count = pl.program_id(0), landed.shape[0]

    def copy(at):
        return pltpu.make_async_remote_copy(
            src_ref=other_ref.at[at],
            dst_ref=landed.at[at],
            send_sem=send_sem.at[at],
            recv_sem=recv_sem.at[at],
            device_id=partner,
            device_id_type=mesh,
        )

    @pl.when(turn == 0)
    def _():
        barrier = pltpu.get_barrier_semaphore()
        pl.semaphore_signal(barrier, inc=1, device_id=partner, device_id_type=mesh)
        pl.semaphore_wait(barrier, 1)
        for at in range(count):
            copy(at).start()

    copy(turn).wait_recv()
    out_ref[0] = (mine_ref[0].astype(FULL) + landed[turn].astype(FULL)).astype(LOW)

    @pl.when(turn == count - 1)
    def _():
        for at in range(count):
            copy(at).wait_send()


def add_pairs(identity, mine, other):
    count, shape = mine.shape[0], mine.shape[1:]
    block = pl.BlockSpec((1, *shape), lambda i: (i, 0, 0))
    dma = pltpu.SemaphoreType.DMA
    return pl.pallas_call(
        pair_kernel,
        out_shape=jax.ShapeDtypeStruct(mine.shape, LOW),
        grid=(count,),
        in_specs=[block, pl.BlockSpec(memory_space=pl.ANY)],
        out_specs=block,
        scratch_shapes=[pltpu.VMEM(mine.shape, LOW), dma((count,)), dma((count,))],
        compiler_params=pltpu.CompilerParams(
            collective_id=identity, has_side_effects=True, vmem_limit_bytes=40 * MIB
        ),
        cost_estimate=SMALL,
        name="add_pairs",
    )(mine, other)


def rounded(count, unit=TILE):
    return -(-count // unit) * unit


class Gather:
    def __init__(self, shares, shards, wholes, sems):
        self.shares, self.shards, self.wholes = shares, shards, wholes
        self.local_sem, self.pair_send, self.pair_recv = sems[:3]
        self.line_send, self.line_recv, self.copy_send, self.copy_recv = sems[3:7]
        self.core_send, self.core_recv = sems[7:]
        self.copies, self.place = lax.axis_size("dp"), lax.axis_index("dp")
        self.chips, self.me = lax.axis_size("fsdp") // 2, lax.axis_index("fsdp")
        self.chip, self.core = self.me // 2, self.me % 2
        self.partner = 2 * self.chip + 1 - self.core

    @staticmethod
    def scratch(count):
        dma = pltpu.SemaphoreType.DMA
        copies, chips = lax.axis_size("dp"), lax.axis_size("fsdp") // 2
        return (
            [dma((count,))] * 3 + [dma((count, 2, chips))] * 2 + [dma((count, 2, chips, copies))] * 4
        )

    def greet(self):
        mesh = pl.DeviceIdType.MESH
        place, me, chip = self.place, self.me, self.chip
        barrier = pltpu.get_barrier_semaphore()
        pl.semaphore_signal(barrier, inc=1, device_id=(place, self.partner), device_id_type=mesh)
        for k in range(1, self.copies):
            peer = lax.rem(place + k, self.copies)
            pl.semaphore_signal(barrier, inc=1, device_id=(peer, me), device_id_type=mesh)

        @pl.when(chip > 0)
        def _():
            pl.semaphore_signal(barrier, inc=1, device_id=(place, me - 2), device_id_type=mesh)

        @pl.when(chip < self.chips - 1)
        def _():
            pl.semaphore_signal(barrier, inc=1, device_id=(place, me + 2), device_id_type=mesh)

        neighbours = jnp.minimum(chip, 1) + jnp.minimum(self.chips - 1 - chip, 1)
        pl.semaphore_wait(barrier, self.copies + neighbours)

    def rows(self, a, owner, share):
        whole = self.shards[a].shape[0]
        part = whole // self.shares[a]
        return pl.ds(pl.multiple_of(owner * whole + share * part, TILE), part)

    def remote(self, source, target, send, recv, device):
        return pltpu.make_async_remote_copy(
            src_ref=source,
            dst_ref=target,
            send_sem=send,
            recv_sem=recv,
            device_id=device,
            device_id_type=pl.DeviceIdType.MESH,
        )

    def my_share(self, a):
        return self.place if self.shares[a] > 1 else 0

    def peers(self, a):
        return range(1, self.copies) if self.shares[a] > 1 else range(0)

    def owner_of(self, side, step):
        return self.me - 2 * step if side == 0 else self.me + 2 * step

    def sends(self, side):
        return self.chip < self.chips - 1 if side == 0 else self.chip > 0

    def has(self, side, step):
        return self.chip >= step if side == 0 else self.chip + step <= self.chips - 1

    def line_copy(self, a, side, step):
        where = self.rows(a, self.owner_of(side, step), self.my_share(a))
        target = self.me + 2 if side == 0 else self.me - 2
        return self.remote(
            self.wholes[a].at[where],
            self.wholes[a].at[where],
            self.line_send.at[a, side, step],
            self.line_recv.at[a, side, step],
            (self.place, target),
        )

    def first_copy(self, a, side):
        part = self.shards[a].shape[0] // self.shares[a]
        target = self.me + 2 if side == 0 else self.me - 2
        return self.remote(
            self.shards[a].at[pl.ds(pl.multiple_of(self.my_share(a) * part, TILE), part)],
            self.wholes[a].at[self.rows(a, self.me, self.my_share(a))],
            self.line_send.at[a, side, 0],
            self.line_recv.at[a, side, 0],
            (self.place, target),
        )

    def peer_copy(self, a, side, step, k):
        where = self.rows(a, self.owner_of(side, step), self.place)
        return self.remote(
            self.wholes[a].at[where],
            self.wholes[a].at[where],
            self.copy_send.at[a, side, step, k],
            self.copy_recv.at[a, side, step, k],
            (lax.rem(self.place + k, self.copies), self.me),
        )

    def core_copy(self, a, side, step, k):
        share = lax.rem(self.place + self.copies - k, self.copies) if self.shares[a] > 1 else 0
        where = self.rows(a, self.owner_of(side, step), share)
        return self.remote(
            self.wholes[a].at[where],
            self.wholes[a].at[where],
            self.core_send.at[a, side, step, k],
            self.core_recv.at[a, side, step, k],
            (self.place, self.partner),
        )

    def rows_all(self, a):
        whole = self.shards[a].shape[0]
        return pl.ds(pl.multiple_of(self.me * whole, TILE), whole)

    def pair_copy(self, a):
        return self.remote(
            self.shards[a],
            self.wholes[a].at[self.rows_all(a)],
            self.pair_send.at[a],
            self.pair_recv.at[a],
            (self.place, self.partner),
        )

    def local_copy(self, a):
        return pltpu.make_async_copy(
            self.shards[a], self.wholes[a].at[self.rows_all(a)], self.local_sem.at[a]
        )

    def start(self):
        for a in range(len(self.shards)):
            for side in range(2):

                @pl.when(self.sends(side))
                def _(a=a, side=side):
                    self.first_copy(a, side).start()

        for a in range(len(self.shards)):
            self.pair_copy(a).start()
            self.local_copy(a).start()

    def hand_over(self, a, side, step):
        for k in self.peers(a):
            self.peer_copy(a, side, step, k).wait_recv()
            self.core_copy(a, side, step, k).start()

    def advance(self, step):
        for a in range(len(self.shards)):
            for side in range(2):

                @pl.when(self.has(side, step))
                def _(a=a, side=side):
                    self.line_copy(a, side, step - 1).wait_recv()

                    @pl.when(self.sends(side))
                    def _():
                        self.line_copy(a, side, step).start()

                    for k in self.peers(a):
                        self.peer_copy(a, side, step, k).start()
                    self.core_copy(a, side, step, 0).start()

        for a in range(len(self.shards)):
            for side in range(2):

                @pl.when((step > 1) & self.has(side, step - 1))
                def _(a=a, side=side):
                    self.hand_over(a, side, step - 1)

    def finish(self):
        last = self.chips - 1
        for a in range(len(self.shards)):
            for side in range(2):

                @pl.when(self.has(side, last))
                def _(a=a, side=side):
                    self.hand_over(a, side, last)

        def settle(step, _):
            for a in range(len(self.shards)):
                for side in range(2):

                    @pl.when(self.has(side, step))
                    def _(a=a, side=side):
                        @pl.when(self.sends(side))
                        def _():
                            self.line_copy(a, side, step).wait_send()

                        for k in self.peers(a):
                            self.peer_copy(a, side, step, k).wait_send()
                            self.core_copy(a, side, step, k).wait_send()
                            self.core_copy(a, side, step, k).wait_recv()
                        self.core_copy(a, side, step, 0).wait_send()
                        self.core_copy(a, side, step, 0).wait_recv()

            return 0

        lax.fori_loop(1, self.chips, settle, 0)
        for a in range(len(self.shards)):
            for side in range(2):

                @pl.when(self.sends(side))
                def _(a=a, side=side):
                    self.first_copy(a, side).wait_send()

            self.pair_copy(a).wait_send()
            self.pair_copy(a).wait_recv()
            self.local_copy(a).wait()


def shares_of(shards):
    copies = lax.axis_size("dp")
    return [copies if shard.shape[0] % (TILE * copies) == 0 else 1 for shard in shards]


def whole_shapes(shards):
    size = lax.axis_size("fsdp")
    return [jax.ShapeDtypeStruct((size * s.shape[0], *s.shape[1:]), s.dtype) for s in shards]


def gather_kernel(shares, *refs):
    count = len(shares)
    gather = Gather(shares, refs[:count], refs[count : 2 * count], refs[2 * count :])
    gather.greet()
    gather.start()

    def advance(step, _):
        gather.advance(step)
        return 0

    lax.fori_loop(1, gather.chips, advance, 0)
    gather.finish()


def gather_shards(identity, *shards):
    count = len(shards)
    anywhere = pl.BlockSpec(memory_space=pl.ANY)
    return pl.pallas_call(
        functools.partial(gather_kernel, shares_of(shards)),
        out_shape=whole_shapes(shards),
        in_specs=[anywhere] * count,
        out_specs=[anywhere] * count,
        scratch_shapes=Gather.scratch(count),
        compiler_params=pltpu.CompilerParams(collective_id=identity, has_side_effects=True),
        cost_estimate=SMALL,
        name="gather_shards",
    )(*shards)


def across(number, other):
    total, bit = 0, 1
    while bit < lax.axis_size("fsdp") // 2:
        total = total + bit * ((number // bit % 2 + other // bit % 2) % 2)
        bit *= 2
    return total


def greet(place, me, chip, chips):
    mesh = pl.DeviceIdType.MESH
    barrier = pltpu.get_barrier_semaphore()
    partner = 2 * chip + 1 - me % 2
    pl.semaphore_signal(barrier, inc=1, device_id=(place, partner), device_id_type=mesh)

    @pl.when(chip > 0)
    def _():
        pl.semaphore_signal(barrier, inc=1, device_id=(place, me - 2), device_id_type=mesh)

    @pl.when(chip < chips - 1)
    def _():
        pl.semaphore_signal(barrier, inc=1, device_id=(place, me + 2), device_id_type=mesh)

    neighbours = jnp.minimum(chip, 1) + jnp.minimum(chips - 1 - chip, 1)
    pl.semaphore_wait(barrier, 1 + neighbours)


def feed_kernel(
    valid,
    hidden_ref,
    backs_ref,
    gate_ref,
    up_ref,
    down_ref,
    inner_ref,
    gate_grad_ref,
    up_grad_ref,
    rows_ref,
    back_ref,
    small_ref,
    land,
    held,
    line_send,
    line_recv,
    core_send,
    core_recv,
    own_sem,
    back_sem,
    out_sem,
):
    mesh = pl.DeviceIdType.MESH
    place, me = lax.axis_index("dp"), lax.axis_index("fsdp")
    chips = lax.axis_size("fsdp") // 2
    chip, core = me // 2, me % 2
    block = hidden_ref.shape[0]
    position, tile = pl.program_id(0), pl.program_id(1)
    tiles = pl.num_programs(1)
    source = across(chip, position)
    owners = (2 * source + core, 2 * source + 1 - core)
    slot = lax.rem(position, 2)

    def sends(side):
        return chip < chips - 1 if side == 0 else chip > 0

    def has(side, step):
        return chip >= step if side == 0 else chip + step <= chips - 1

    def line_copy(side, step):
        owner = me - 2 * step if side == 0 else me + 2 * step
        target = me + 2 if side == 0 else me - 2
        return pltpu.make_async_remote_copy(
            src_ref=land.at[owner],
            dst_ref=land.at[owner],
            send_sem=line_send.at[side, step],
            recv_sem=line_recv.at[side, step],
            device_id=(place, target),
            device_id_type=mesh,
        )

    def line_arrival(side, step):
        owner = me - 2 * step if side == 0 else me + 2 * step
        return pltpu.make_async_remote_copy(
            src_ref=land.at[owner],
            dst_ref=land.at[owner],
            send_sem=line_send.at[side, step - 1],
            recv_sem=line_recv.at[side, step - 1],
            device_id=(place, me + 2 if side == 0 else me - 2),
            device_id_type=mesh,
        )

    def core_copy(owner_chip):
        owner = 2 * owner_chip + core
        return pltpu.make_async_remote_copy(
            src_ref=land.at[owner],
            dst_ref=land.at[owner],
            send_sem=core_send.at[owner_chip],
            recv_sem=core_recv.at[owner_chip],
            device_id=(place, 2 * chip + 1 - core),
            device_id_type=mesh,
        )

    def back_copies(at):
        origin = across(chip, at)
        to = lax.rem(at, 2)
        return [
            pltpu.make_async_copy(
                backs_ref.at[pl.ds(pl.multiple_of(owner * block, TILE), block)],
                held.at[to, half],
                back_sem.at[to, half],
            )
            for half, owner in enumerate((2 * origin + core, 2 * origin + 1 - core))
        ]

    def out_copies():
        copies = []
        for half in range(2):
            where = pl.ds(pl.multiple_of((2 * position + half) * valid, TILE), valid)
            rows, back = land.at[owners[half]], held.at[slot, half]
            for source_ref, target, small in ((rows, rows_ref, 0), (back, back_ref, 1)):
                copies.append((source_ref.at[pl.ds(0, valid)], target.at[where]))
                copies.append(
                    (
                        source_ref.at[pl.ds(valid, block - valid)],
                        small_ref.at[small, position, half],
                    )
                )
        return [
            pltpu.make_async_copy(source_ref, target, out_sem.at[i])
            for i, (source_ref, target) in enumerate(copies)
        ]

    @pl.when((position == 0) & (tile == 0))
    def _():
        for copy in back_copies(0):
            copy.start()
        own = pltpu.make_async_copy(hidden_ref, land.at[me], own_sem)
        own.start()
        greet(place, me, chip, chips)
        own.wait()
        for side in range(2):

            @pl.when(sends(side))
            def _(side=side):
                line_copy(side, 0).start()

        core_copy(chip).start()

    @pl.when(tile == 0)
    def _():
        for side in range(2):

            @pl.when((position > 0) & has(side, position))
            def _(side=side):
                line_arrival(side, position).wait_recv()

                @pl.when(sends(side))
                def _():
                    line_copy(side, position).start()

                core_copy(chip - position if side == 0 else chip + position).start()

        core_copy(source).wait_recv()
        for copy in back_copies(position):
            copy.wait()
        for copy in out_copies():
            copy.start()

        @pl.when(position < chips - 1)
        def _():
            for copy in back_copies(position + 1):
                copy.start()

    root = math.sqrt(2.0 / math.pi)
    for half in range(2):
        where = slice(half * valid, (half + 1) * valid)
        rows = land[owners[half], :valid]
        back = held[slot, half, :valid]
        gate = multiply(rows, gate_ref[...])
        upper = multiply(rows, up_ref[...])
        inner_grad = multiply_right(back, down_ref[...])
        square = gate * gate
        bent = jnp.tanh(root * gate * (1.0 + 0.044715 * square))
        half_up = 0.5 + 0.5 * bent
        active = gate * half_up
        slope = half_up + (0.5 * root) * gate * (1.0 - bent * bent) * (1.0 + 0.134145 * square)
        inner_ref[where] = (active * upper).astype(LOW)
        gate_grad_ref[where] = (inner_grad * upper * slope).astype(LOW)
        up_grad_ref[where] = (inner_grad * active).astype(LOW)

    @pl.when(tile == tiles - 1)
    def _():
        for copy in out_copies():
            copy.wait()

    @pl.when((tile == tiles - 1) & (position == chips - 1))
    def _():
        for side in range(2):

            @pl.when(sends(side))
            def _(side=side):
                line_copy(side, 0).wait_send()

        for owner in range(chips):
            core_copy(owner).wait_send()

        def finish(step, _):
            for side in range(2):

                @pl.when(sends(side) & has(side, step))
                def _(side=side):
                    line_copy(side, step).wait_send()

            return 0

        lax.fori_loop(1, chips, finish, 0)


def feed_all(valid, hidden, backs, gate, up, down):
    block, width = hidden.shape
    size = lax.axis_size("fsdp")
    chips = size // 2
    units = gate.shape[1]
    tile = math.gcd(units, 512)
    column = pl.BlockSpec((width, tile), lambda p, j: (0, j))
    anywhere = pl.BlockSpec(memory_space=pl.ANY)
    total = chips * 2 * valid
    dma = pltpu.SemaphoreType.DMA
    return pl.pallas_call(
        functools.partial(feed_kernel, valid),
        out_shape=[jax.ShapeDtypeStruct((total, units), LOW)] * 3
        + [jax.ShapeDtypeStruct((total, width), LOW)] * 2
        + [jax.ShapeDtypeStruct((2, chips, 2, block - valid, width), LOW)],
        grid=(chips, units // tile),
        in_specs=[anywhere, anywhere, column, column]
        + [pl.BlockSpec((tile, width), lambda p, j: (j, 0))],
        out_specs=[pl.BlockSpec((2 * valid, tile), lambda p, j: (p, j))] * 3 + [anywhere] * 3,
        scratch_shapes=[
            pltpu.VMEM((size, block, width), LOW),
            pltpu.VMEM((2, 2, block, width), LOW),
            dma((2, chips)),
            dma((2, chips)),
            dma((chips,)),
            dma((chips,)),
            dma,
            dma((2, 2)),
            dma((8,)),
        ],
        compiler_params=pltpu.CompilerParams(
            collective_id=1, has_side_effects=True, vmem_limit_bytes=58 * MIB
        ),
        cost_estimate=SMALL,
        name="feed_all",
    )(hidden, backs, gate, up, down)


def collect_kernel(valid, transposed, count, width, *refs):
    grads, weights = refs[:count], refs[count : 2 * count]
    small_ref, total_ref = refs[2 * count : 2 * count + 2]
    mine, other, pair, arrive = refs[2 * count + 2 : 2 * count + 6]
    line_send, line_recv, core_send, core_recv = refs[2 * count + 6 :]
    mesh = pl.DeviceIdType.MESH
    place, me = lax.axis_index("dp"), lax.axis_index("fsdp")
    chips = lax.axis_size("fsdp") // 2
    chip, core = me // 2, me % 2
    turn, tile = pl.program_id(0), pl.program_id(1)
    tiles = pl.num_programs(1)
    span = small_ref.shape[-1]
    target = across(chip, chips - 1 - turn)
    slot = lax.rem(turn, 2)
    columns = pl.ds(pl.multiple_of(tile * span, 128), span)

    def core_copy(at_turn, at_tile):
        where = pl.ds(pl.multiple_of(at_tile * span, 128), span)
        owner = across(chip, chips - 1 - at_turn)
        return pltpu.make_async_remote_copy(
            src_ref=other.at[lax.rem(at_turn, 2), :, where],
            dst_ref=pair.at[owner, :, where],
            send_sem=core_send.at[lax.rem(at_turn, 2), at_tile],
            recv_sem=core_recv.at[owner, at_tile],
            device_id=(place, 2 * chip + 1 - core),
            device_id_type=mesh,
        )

    def valid_at(side, step):
        return chip <= step - 1 if side == 0 else chip >= chips - step

    def fed(side):
        return chip > 0 if side == 0 else chip < chips - 1

    def owner_at(side, step):
        return chip + chips - step if side == 0 else chip - chips + step

    def line_copy(side, step):
        return pltpu.make_async_remote_copy(
            src_ref=mine.at[owner_at(side, step)],
            dst_ref=arrive.at[side, step - 1],
            send_sem=line_send.at[side, step - 1],
            recv_sem=line_recv.at[side, step - 1],
            device_id=(place, me + 2 if side == 0 else me - 2),
            device_id_type=mesh,
        )

    def line_arrival(side, step):
        return pltpu.make_async_remote_copy(
            src_ref=mine.at[chip],
            dst_ref=arrive.at[side, step - 1],
            send_sem=line_send.at[side, step - 1],
            recv_sem=line_recv.at[side, step - 1],
            device_id=(place, me + 2 if side == 0 else me - 2),
            device_id_type=mesh,
        )

    @pl.when((turn == 0) & (tile == 0))
    def _():
        greet(place, me, chip, chips)

    @pl.when((turn > 0) & (tile == 0))
    def _():
        done = across(chip, chips - turn)

        def take(at_tile, _):
            core_copy(turn - 1, at_tile).wait_recv()
            return 0

        lax.fori_loop(0, tiles, take, 0)
        mine[done] = (mine[done].astype(FULL) + pair[done].astype(FULL)).astype(LOW)
        for side in range(2):

            @pl.when(valid_at(side, turn))
            def _(side=side):
                owner = owner_at(side, turn)

                @pl.when((turn > 1) & fed(side))
                def _():
                    line_arrival(side, turn - 1).wait_recv()
                    mine[owner] = (
                        mine[owner].astype(FULL) + arrive[side, turn - 2].astype(FULL)
                    ).astype(LOW)

                line_copy(side, turn).start()

    @pl.when(turn > 1)
    def _():
        core_copy(turn - 2, tile).wait_send()

    for half in range(2):
        where = slice(half * valid, (half + 1) * valid)
        part = None
        for grad, weight in zip(grads, weights):
            product = (multiply_right if transposed else multiply)(grad[where], weight[...])
            part = product if part is None else part + product
        if half == 0:
            mine[target, :valid, columns] = part.astype(LOW)
            mine[target, valid:, columns] = small_ref[0, 0]
        else:
            other[slot, :valid, columns] = part.astype(LOW)
            other[slot, valid:, columns] = small_ref[0, 1]
    core_copy(turn, tile).start()

    @pl.when((turn == chips - 1) & (tile == tiles - 1))
    def _():
        def take(at_tile, _):
            core_copy(turn, at_tile).wait_recv()
            core_copy(turn, at_tile).wait_send()

            @pl.when(turn > 0)
            def _():
                core_copy(turn - 1, at_tile).wait_send()

            return 0

        lax.fori_loop(0, tiles, take, 0)
        total_ref[...] = mine[chip].astype(FULL) + pair[chip].astype(FULL)
        for side in range(2):

            @pl.when(fed(side))
            def _(side=side):
                line_arrival(side, chips - 1).wait_recv()
                total_ref[...] += arrive[side, chips - 2].astype(FULL)

        def finish(step, _):
            for side in range(2):

                @pl.when(valid_at(side, step))
                def _(side=side):
                    line_copy(side, step).wait_send()

            return 0

        lax.fori_loop(1, chips, finish, 0)


def collect(identity, valid, transposed, grads, weights, small, width):
    chips = lax.axis_size("fsdp") // 2
    units = grads[0].shape[1]
    extra = small.shape[2]
    block = valid + extra
    tile = math.gcd(width, 256)
    count = len(grads)
    rows = pl.BlockSpec((2 * valid, units), lambda t, j: (chips - 1 - t, 0))
    if transposed:
        weight = pl.BlockSpec((tile, units), lambda t, j: (j, 0))
    else:
        weight = pl.BlockSpec((units, tile), lambda t, j: (0, j))
    dma = pltpu.SemaphoreType.DMA
    return pl.pallas_call(
        functools.partial(collect_kernel, valid, transposed, count, width),
        out_shape=jax.ShapeDtypeStruct((block, width), FULL),
        grid=(chips, width // tile),
        in_specs=[rows] * count
        + [weight] * count
        + [pl.BlockSpec((1, 2, extra, tile), lambda t, j: (chips - 1 - t, 0, 0, j))],
        out_specs=pl.BlockSpec((block, width), lambda t, j: (0, 0)),
        scratch_shapes=[
            pltpu.VMEM((chips, block, width), LOW),
            pltpu.VMEM((2, block, width), LOW),
            pltpu.VMEM((chips, block, width), LOW),
            pltpu.VMEM((2, chips - 1, block, width), LOW),
            dma((2, chips - 1)),
            dma((2, chips - 1)),
            dma((2, width // tile)),
            dma((chips, width // tile)),
        ],
        compiler_params=pltpu.CompilerParams(
            collective_id=identity, has_side_effects=True, vmem_limit_bytes=62 * MIB
        ),
        cost_estimate=SMALL,
        name="collect",
    )(*grads, *weights, small)


def part_kernel(
    valid, inner_ref, down_ref, small_ref, out_ref, mine, other, pair, core_send, core_recv, out_sem
):
    place, me = lax.axis_index("dp"), lax.axis_index("fsdp")
    partner = (place, me + 1 - 2 * (me % 2))
    mesh = pl.DeviceIdType.MESH
    turn, tile = pl.program_id(0), pl.program_id(1)
    turns, tiles = pl.num_programs(0), pl.num_programs(1)
    span = small_ref.shape[-1]
    slot = lax.rem(turn, 2)
    columns = pl.ds(pl.multiple_of(tile * span, 128), span)

    def core_copy(at_turn, at_tile):
        where = pl.ds(pl.multiple_of(at_tile * span, 128), span)
        return pltpu.make_async_remote_copy(
            src_ref=other.at[lax.rem(at_turn, 2), :, where],
            dst_ref=pair.at[at_turn, :, where],
            send_sem=core_send.at[lax.rem(at_turn, 2), at_tile],
            recv_sem=core_recv.at[at_turn, at_tile],
            device_id=partner,
            device_id_type=mesh,
        )

    def out_copy(at_turn):
        return pltpu.make_async_copy(mine.at[at_turn], out_ref.at[at_turn], out_sem.at[at_turn])

    def settle(at_turn):
        def take(at_tile, _):
            core_copy(at_turn, at_tile).wait_recv()
            return 0

        lax.fori_loop(0, tiles, take, 0)
        mine[at_turn] = (mine[at_turn].astype(FULL) + pair[at_turn].astype(FULL)).astype(LOW)
        out_copy(at_turn).start()

    @pl.when((turn == 0) & (tile == 0))
    def _():
        barrier = pltpu.get_barrier_semaphore()
        pl.semaphore_signal(barrier, inc=1, device_id=partner, device_id_type=mesh)
        pl.semaphore_wait(barrier, 1)

    @pl.when((turn > 0) & (tile == 0))
    def _():
        settle(turn - 1)

    @pl.when(turn > 1)
    def _():
        core_copy(turn - 2, tile).wait_send()

    for half in range(2):
        where = slice(half * valid, (half + 1) * valid)
        part = multiply(inner_ref[where], down_ref[...]).astype(LOW)
        if half == 0:
            mine[turn, :valid, columns] = part
            mine[turn, valid:, columns] = small_ref[0, 0]
        else:
            other[slot, :valid, columns] = part
            other[slot, valid:, columns] = small_ref[0, 1]
    core_copy(turn, tile).start()

    @pl.when((turn == turns - 1) & (tile == tiles - 1))
    def _():
        settle(turn)

        def take(at_tile, _):
            core_copy(turn, at_tile).wait_send()

            @pl.when(turn > 0)
            def _():
                core_copy(turn - 1, at_tile).wait_send()

            return 0

        lax.fori_loop(0, tiles, take, 0)
        for at_turn in range(mine.shape[0]):
            out_copy(at_turn).wait()


def part_chunks(valid, inner, down, small):
    chips, _, extra, width = small.shape
    units = inner.shape[1]
    tile = math.gcd(width, 512)
    block = (valid + extra, width)
    dma = pltpu.SemaphoreType.DMA
    return pl.pallas_call(
        functools.partial(part_kernel, valid),
        out_shape=jax.ShapeDtypeStruct((chips, *block), LOW),
        grid=(chips, width // tile),
        in_specs=[
            pl.BlockSpec((2 * valid, units), lambda p, j: (p, 0)),
            pl.BlockSpec((units, tile), lambda p, j: (0, j)),
            pl.BlockSpec((1, 2, extra, tile), lambda p, j: (p, 0, 0, j)),
        ],
        out_specs=pl.BlockSpec(memory_space=pl.ANY),
        scratch_shapes=[
            pltpu.VMEM((chips, *block), LOW),
            pltpu.VMEM((2, *block), LOW),
            pltpu.VMEM((chips, *block), LOW),
            dma((2, width // tile)),
            dma((chips, width // tile)),
            dma((chips,)),
        ],
        compiler_params=pltpu.CompilerParams(
            collective_id=11, has_side_effects=True, vmem_limit_bytes=52 * MIB
        ),
        cost_estimate=SMALL,
        name="part_chunks",
    )(inner, down, small)


def norm_back(rows, gain, grad):
    factor = lax.rsqrt(jnp.mean(rows * rows, axis=-1, keepdims=True) + EPS)
    scaled = gain * grad
    inner = jnp.mean(rows * scaled, axis=-1, keepdims=True)
    rows_grad = factor * scaled - (factor * factor * factor * inner) * rows
    return rows_grad, jnp.sum(grad * rows * factor, axis=0, keepdims=True)


def middle_kernel(grad_ref, rows_ref, back_ref, gain_ref, weight_ref, total_ref, low_ref, mixed_ref, part_ref):
    @pl.when(pl.program_id(0) == 0)
    def _():
        rows_grad, part_ref[...] = norm_back(rows_ref[...], gain_ref[...], grad_ref[...])
        total = back_ref[...].astype(FULL) + rows_grad
        total_ref[...] = total
        low_ref[...] = total.astype(LOW)

    mixed_ref[...] = multiply_right(low_ref[...], weight_ref[...]).astype(LOW)


def middle_back(grad, rows, back, gain, weight):
    count, width = rows.shape
    features = weight.shape[0]
    tile = math.gcd(features, 512)
    whole = pl.BlockSpec((count, width), lambda j: (0, 0))
    return pl.pallas_call(
        middle_kernel,
        out_shape=[
            jax.ShapeDtypeStruct((count, width), FULL),
            jax.ShapeDtypeStruct((count, width), LOW),
            jax.ShapeDtypeStruct((count, features), LOW),
            jax.ShapeDtypeStruct((1, width), FULL),
        ],
        grid=(features // tile,),
        in_specs=[whole, whole, whole, pl.BlockSpec((1, width), lambda j: (0, 0))]
        + [pl.BlockSpec((tile, width), lambda j: (j, 0))],
        out_specs=[whole, whole, pl.BlockSpec((count, tile), lambda j: (0, j))]
        + [pl.BlockSpec((1, width), lambda j: (0, 0))],
        compiler_params=pltpu.CompilerParams(vmem_limit_bytes=56 * MIB),
        cost_estimate=SMALL,
        name="middle_back",
    )(grad, rows, back, gain.reshape(1, width), weight)


def entry_kernel(query_ref, kv_ref, rows_ref, total_ref, gain_ref, weight_ref, out_ref, part_ref, held):
    tile = weight_ref.shape[0]
    where = pl.ds(pl.multiple_of(pl.program_id(0) * tile, 128), tile)
    features = query_ref.shape[1]
    held[:, where] = multiply_right(query_ref[...], weight_ref[:, :features]) + multiply_right(
        kv_ref[...], weight_ref[:, features:]
    )

    @pl.when(pl.program_id(0) == pl.num_programs(0) - 1)
    def _():
        rows_grad, part_ref[...] = norm_back(rows_ref[...].astype(FULL), gain_ref[...], held[...])
        out_ref[...] = total_ref[...] + rows_grad


def entry_back(query_grad, kv_grad, rows, total, gain, weight):
    count, width = rows.shape
    tile = math.gcd(width, 512)
    fixed = lambda j: (0, 0)
    whole = pl.BlockSpec((count, width), fixed)
    return pl.pallas_call(
        entry_kernel,
        out_shape=[
            jax.ShapeDtypeStruct((count, width), FULL),
            jax.ShapeDtypeStruct((1, width), FULL),
        ],
        grid=(width // tile,),
        in_specs=[
            pl.BlockSpec(query_grad.shape, fixed),
            pl.BlockSpec(kv_grad.shape, fixed),
            whole,
            whole,
            pl.BlockSpec((1, width), fixed),
            pl.BlockSpec((tile, weight.shape[1]), lambda j: (j, 0)),
        ],
        out_specs=[whole, pl.BlockSpec((1, width), fixed)],
        scratch_shapes=[pltpu.VMEM((count, width), FULL)],
        compiler_params=pltpu.CompilerParams(vmem_limit_bytes=56 * MIB),
        cost_estimate=SMALL,
        name="entry_back",
    )(query_grad, kv_grad, rows, total, gain.reshape(1, width), weight)


class CopySum:
    def __init__(self, split, values, totals, arrived, whole, sems):
        self.split, self.values, self.totals = split, values, totals
        self.arrived, self.whole = arrived, whole
        self.part_send, self.part_recv, self.whole_send, self.whole_recv = sems
        self.copies = lax.axis_size("dp")
        self.place, self.me = lax.axis_index("dp"), lax.axis_index("fsdp")

    @staticmethod
    def split_of(shapes):
        return [shape[0] % (TILE * lax.axis_size("dp")) == 0 for shape in shapes]

    @staticmethod
    def scratch(shapes):
        copies = lax.axis_size("dp")
        arrived, whole = [], []
        for (rows, columns), parts in zip(shapes, CopySum.split_of(shapes)):
            arrived.append((copies - 1, rows // copies, columns) if parts else (copies, rows, columns))
            whole.append((rows, columns) if parts else (TILE, 128))
        return [pltpu.VMEM(shape, LOW) for shape in arrived + whole]

    def rows(self, a, owner):
        part = self.values[a].shape[0] // self.copies
        return pl.ds(pl.multiple_of(owner * part, TILE), part)

    def part_copy(self, a, k):
        peer = lax.rem(self.place + k, self.copies)
        value, arrived = self.values[a], self.arrived[a]
        return pltpu.make_async_remote_copy(
            src_ref=value.at[self.rows(a, peer)] if self.split[a] else value,
            dst_ref=arrived.at[k - 1] if self.split[a] else arrived.at[self.place],
            send_sem=self.part_send.at[a, k],
            recv_sem=self.part_recv.at[a, k],
            device_id=(peer, self.me),
            device_id_type=pl.DeviceIdType.MESH,
        )

    def whole_copy(self, a, k):
        where = self.rows(a, self.place)
        return pltpu.make_async_remote_copy(
            src_ref=self.whole[a].at[where],
            dst_ref=self.whole[a].at[where],
            send_sem=self.whole_send.at[a, k],
            recv_sem=self.whole_recv.at[a, k],
            device_id=(lax.rem(self.place + k, self.copies), self.me),
            device_id_type=pl.DeviceIdType.MESH,
        )

    def send(self, a):
        for k in range(1, self.copies):
            self.part_copy(a, k).start()

    def reduce(self, a):
        value, arrived = self.values[a], self.arrived[a]
        if not self.split[a]:
            arrived[self.place] = value[...]
        for k in range(1, self.copies):
            self.part_copy(a, k).wait_recv()
        if self.split[a]:
            total = value[self.rows(a, self.place)].astype(FULL)
            for k in range(1, self.copies):
                total = total + arrived[k - 1].astype(FULL)
            self.whole[a][self.rows(a, self.place)] = total.astype(LOW)
            for k in range(1, self.copies):
                self.whole_copy(a, k).start()
        else:
            total = arrived[0].astype(FULL)
            for k in range(1, self.copies):
                total = total + arrived[k].astype(FULL)
            self.totals[a][...] = total

    def finish(self, a):
        for k in range(1, self.copies):
            self.part_copy(a, k).wait_send()
            if self.split[a]:
                self.whole_copy(a, k).wait_send()
                self.whole_copy(a, k).wait_recv()
        if self.split[a]:
            self.totals[a][...] = self.whole[a][...].astype(FULL)


def tail_kernel(split, *refs):
    count = len(split)
    given = count - 7
    inputs, refs = refs[:given], refs[given:]
    summed_ref, left_ref, right_ref = refs[:3]
    totals, all_ref, refs = refs[3 : 3 + count], refs[3 + count], refs[4 + count :]
    arrived, whole, refs = refs[:count], refs[count : 2 * count], refs[2 * count :]
    held, arrive, total, own, right_all, refs = *refs[:3], refs[3:10], refs[10], refs[11:]
    load_sem, right_sem, line_send, line_recv = refs[:4]
    sums = CopySum(split, (*inputs, *own), totals, arrived, whole, refs[4:8])
    gather = Gather([1], [right_ref], [all_ref], refs[8:])
    mesh = pl.DeviceIdType.MESH
    place, me = lax.axis_index("dp"), lax.axis_index("fsdp")
    chips = lax.axis_size("fsdp") // 2
    chip = me // 2

    load = pltpu.make_async_copy(summed_ref, held, load_sem)
    load.start()
    gather.greet()
    gather.start()
    load.wait()

    def valid_at(side, step):
        return chip <= step - 1 if side == 0 else chip >= chips - step

    def fed(side):
        return chip > 0 if side == 0 else chip < chips - 1

    def line_copy(side, step, owner):
        return pltpu.make_async_remote_copy(
            src_ref=held.at[owner],
            dst_ref=arrive.at[side, step - 1],
            send_sem=line_send.at[side, step - 1],
            recv_sem=line_recv.at[side, step - 1],
            device_id=(place, me + 2 if side == 0 else me - 2),
            device_id_type=mesh,
        )

    for step in range(1, chips):
        for side in range(2):

            @pl.when(valid_at(side, step))
            def _(step=step, side=side):
                owner = chip + chips - step if side == 0 else chip - chips + step
                if step > 1:

                    @pl.when(fed(side))
                    def _():
                        line_copy(side, step - 1, chip).wait_recv()
                        held[owner] = (
                            held[owner].astype(FULL) + arrive[side, step - 2].astype(FULL)
                        ).astype(LOW)

                line_copy(side, step, owner).start()

        gather.advance(step)
        if step == 1:
            for a in range(given):
                sums.send(a)
        if step == min(2, chips - 1):
            for a in range(given):
                sums.reduce(a)
    gather.finish()
    fetch = pltpu.make_async_copy(all_ref, right_all, right_sem)
    fetch.start()
    fetch.wait()

    def spread(value, targets):
        start = 0
        for target in targets:
            target[...] = value[:, start : start + target.shape[1]].astype(LOW)
            start += target.shape[1]

    spread(multiply_left(left_ref[...], right_all[...]), own[:3])
    for a in range(given, given + 3):
        sums.send(a)
    total[...] = held[chip].astype(FULL)
    for side in range(2):

        @pl.when(fed(side))
        def _(side=side):
            line_copy(side, chips - 1, chip).wait_recv()
            total[...] += arrive[side, chips - 2].astype(FULL)

    rows = own[3].shape[0]
    spread(total[:rows], own[3:6])
    spread(total[rows:], own[6:])
    for a in range(given + 3, count):
        sums.send(a)
    for a in range(given):
        sums.finish(a)
    for a in range(given, count):
        sums.reduce(a)
    for step in range(1, chips):
        for side in range(2):

            @pl.when(valid_at(side, step))
            def _(step=step, side=side):
                line_copy(side, step, chip).wait_send()

    for a in range(given, count):
        sums.finish(a)


def tail_sums(values, summed, rows, left, right, columns):
    chips, block = summed.shape[0], summed.shape[1:]
    own = [(count, width) for count in (left.shape[1], rows) for width in columns]
    own += [(block[0] - rows, block[1])]
    shapes = [value.shape for value in values] + own
    count = len(shapes)
    dma = pltpu.SemaphoreType.DMA
    copies = lax.axis_size("dp")
    inside = pl.BlockSpec(memory_space=pltpu.VMEM)
    anywhere = pl.BlockSpec(memory_space=pl.ANY)
    outs = pl.pallas_call(
        functools.partial(tail_kernel, CopySum.split_of(shapes)),
        out_shape=[jax.ShapeDtypeStruct(shape, FULL) for shape in shapes] + whole_shapes([right]),
        in_specs=[inside] * len(values) + [anywhere, inside, anywhere],
        out_specs=[inside] * count + [anywhere],
        scratch_shapes=CopySum.scratch(shapes)
        + [
            pltpu.VMEM((chips, *block), LOW),
            pltpu.VMEM((2, chips - 1, *block), LOW),
            pltpu.VMEM(block, FULL),
            *(pltpu.VMEM(shape, LOW) for shape in own),
            pltpu.VMEM((2 * chips * right.shape[0], right.shape[1]), LOW),
            dma,
            dma,
            dma((2, chips - 1)),
            dma((2, chips - 1)),
        ]
        + [dma((count, copies))] * 4
        + Gather.scratch(1),
        compiler_params=pltpu.CompilerParams(
            collective_id=6, has_side_effects=True, vmem_limit_bytes=58 * MIB
        ),
        cost_estimate=pl.CostEstimate(
            flops=30_000_000_000, bytes_accessed=1, transcendentals=0
        ),
        name="tail_sums",
    )(*values, summed, left, right)
    return outs[:count]


def widen_kernel(*refs):
    count = len(refs) - 1
    for k, ref in enumerate(refs[:-1]):

        @pl.when(pl.program_id(0) == k)
        def _(ref=ref):
            refs[-1][...] = ref[...].astype(FULL)


def widen(*values):
    count, (rows, columns) = len(values), values[0].shape
    tile = math.gcd(rows, 256)
    return pl.pallas_call(
        widen_kernel,
        out_shape=jax.ShapeDtypeStruct((count * rows, columns), FULL),
        grid=(count, rows // tile),
        in_specs=[pl.BlockSpec((tile, columns), lambda k, i: (i, 0))] * count,
        out_specs=pl.BlockSpec((tile, columns), lambda k, i: (k * (rows // tile) + i, 0)),
        compiler_params=pltpu.CompilerParams(vmem_limit_bytes=32 * MIB),
        cost_estimate=SMALL,
        name="widen",
    )(*values)


def share_kernel(core_ref, left_ref, right_ref, *refs):
    rows = left_ref.shape[1]
    refs[-1][0, :rows] = multiply_left(left_ref[...], right_ref[...]).astype(LOW)
    if len(refs) > 1:
        refs[-1][0, rows:] = refs[0][0]


def weight_shares(core, left, right, gains=None):
    size = lax.axis_size("fsdp")
    chips = size // 2
    count, rows = left.shape[0], left.shape[1] // size
    width, total, extra = right.shape[1], rows, []
    if gains is not None:
        total += gains.shape[1]
        extra = [pl.BlockSpec((1, *gains.shape[1:]), lambda c, core: (2 * c + core[0], 0, 0))]
    return pl.pallas_call(
        share_kernel,
        out_shape=jax.ShapeDtypeStruct((chips, total, width), LOW),
        grid_spec=pltpu.PrefetchScalarGridSpec(
            num_scalar_prefetch=1,
            grid=(chips,),
            in_specs=[
                pl.BlockSpec((count, rows), lambda c, core: (0, 2 * c + core[0])),
                pl.BlockSpec((count, width), lambda c, core: (0, 0)),
            ]
            + extra,
            out_specs=pl.BlockSpec((1, total, width), lambda c, core: (c, 0, 0)),
        ),
        compiler_params=pltpu.CompilerParams(vmem_limit_bytes=48 * MIB),
        cost_estimate=SMALL,
        name="weight_shares",
    )(
        jnp.reshape(core, (1,)).astype(jnp.int32),
        left,
        right,
        *([] if gains is None else [gains]),
    )


def entry_forward_kernel(rows_ref, gain_ref, weight_ref, hidden_ref, out_ref):
    @pl.when(pl.program_id(0) == 0)
    def _():
        hidden_ref[...] = normalize(rows_ref[...].astype(FULL), gain_ref[...]).astype(LOW)

    out_ref[...] = multiply(hidden_ref[...], weight_ref[...]).astype(LOW)


def entry_forward(rows, gain, weight):
    count, width = rows.shape
    columns = weight.shape[1]
    tile = math.gcd(columns, 512)
    whole = pl.BlockSpec((count, width), lambda j: (0, 0))
    return pl.pallas_call(
        entry_forward_kernel,
        out_shape=[
            jax.ShapeDtypeStruct((count, width), LOW),
            jax.ShapeDtypeStruct((count, columns), LOW),
        ],
        grid=(columns // tile,),
        in_specs=[
            whole,
            pl.BlockSpec((1, width), lambda j: (0, 0)),
            pl.BlockSpec((width, tile), lambda j: (0, j)),
        ],
        out_specs=[whole, pl.BlockSpec((count, tile), lambda j: (0, j))],
        compiler_params=pltpu.CompilerParams(vmem_limit_bytes=48 * MIB),
        cost_estimate=SMALL,
        name="entry_forward",
    )(rows, gain.reshape(1, width), weight)


def middle_forward_kernel(mixed_ref, rows_ref, gain_ref, weight_ref, *refs):
    mid_ref, hidden_ref = refs[-2:]
    tile = weight_ref.shape[1]
    where = pl.ds(pl.multiple_of(pl.program_id(0) * tile, 128), tile)
    mid_ref[:, where] = rows_ref[:, where].astype(FULL) + multiply(mixed_ref[...], weight_ref[...])

    @pl.when(pl.program_id(0) == pl.num_programs(0) - 1)
    def _():
        count = mid_ref.shape[0]
        hidden_ref[:count] = normalize(mid_ref[...], gain_ref[...]).astype(LOW)
        if len(refs) > 2:
            hidden_ref[count:] = refs[0][...]


def middle_forward(mixed, rows, gain, weight, below=None):
    count, width = rows.shape
    features = mixed.shape[1]
    tile = math.gcd(width, 512)
    fixed = lambda j: (0, 0)
    extra = [] if below is None else [below]
    total = count + sum(value.shape[0] for value in extra)
    return pl.pallas_call(
        middle_forward_kernel,
        out_shape=[
            jax.ShapeDtypeStruct((count, width), FULL),
            jax.ShapeDtypeStruct((total, width), LOW),
        ],
        grid=(width // tile,),
        in_specs=[
            pl.BlockSpec((count, features), fixed),
            pl.BlockSpec((count, width), fixed),
            pl.BlockSpec((1, width), fixed),
            pl.BlockSpec((features, tile), lambda j: (0, j)),
        ]
        + [pl.BlockSpec(value.shape, fixed) for value in extra],
        out_specs=[pl.BlockSpec((count, width), fixed), pl.BlockSpec((total, width), fixed)],
        compiler_params=pltpu.CompilerParams(vmem_limit_bytes=48 * MIB),
        cost_estimate=SMALL,
        name="middle_forward",
    )(mixed, rows, gain.reshape(1, width), weight, *extra)


def stacked(refs, columns=slice(None)):
    return jnp.concatenate([ref[0, :, columns] for ref in refs], axis=0)


def softmax_of(queries, keys, bias, scale):
    scores = multiply_right(queries, keys) * scale + bias
    raised = jnp.exp(scores - jnp.max(scores, axis=-1, keepdims=True))
    return raised / jnp.sum(raised, axis=-1, keepdims=True)


def mix_kernel(scale, features, shares, *refs):
    count = len(shares)
    prefix_ref, action_ref, prefix_all_ref, action_all_ref, bias_ref = refs[:5]
    shards, refs = refs[5 : 5 + count], refs[5 + count :]
    prefix_out, action_out, kv_out = refs[:3]
    wholes, refs = refs[3 : 3 + count], refs[3 + count :]
    held, send_sem, recv_sem, out_sem = refs[:4]
    gather = Gather(shares, shards, wholes, refs[4:])
    copies = lax.axis_size("dp")
    place, me = lax.axis_index("dp"), lax.axis_index("fsdp")
    item, head = pl.program_id(0), pl.program_id(1)
    items, rows = prefix_all_ref.shape[0], prefix_ref.shape[1]
    heads = pl.num_programs(1)
    turn = item * heads + head

    def copy(at, k):
        return pltpu.make_async_remote_copy(
            src_ref=held.at[0, at],
            dst_ref=held.at[k, at],
            send_sem=send_sem.at[at, k],
            recv_sem=recv_sem.at[at, k],
            device_id=(lax.rem(place + k, copies), me),
            device_id_type=pl.DeviceIdType.MESH,
        )

    @pl.when((item == 0) & (head == 0))
    def _():
        for at in range(items):
            held[0, at, :rows] = prefix_all_ref[at, :, features:]
            held[0, at, rows:] = action_all_ref[at, :, features:]
        gather.greet()
        for at in range(items):
            for k in range(1, copies):
                copy(at, k).start()
        gather.start()

    @pl.when(head == 0)
    def _():
        for k in range(1, copies):
            copy(item, k).wait_recv()

    every = 2 if gather.chips <= items * features // kv_out.shape[3] else 1

    @pl.when((turn > 0) & (lax.rem(turn, every) == 0) & (turn < every * gather.chips))
    def _():
        gather.advance(turn // every)

    queries = stacked((prefix_ref, action_ref))
    kv = jnp.concatenate([held[k, item] for k in range(copies)], axis=0)
    head_size = kv.shape[1] // 2
    probs = softmax_of(queries, kv[:, :head_size], bias_ref[0], scale).astype(LOW)
    mixed = multiply(probs, kv[:, head_size:]).astype(LOW)
    prefix_out[0] = mixed[:rows]
    action_out[0] = mixed[rows:]

    @pl.when((item == items - 1) & (head == pl.num_programs(1) - 1))
    def _():
        whole = pltpu.make_async_copy(held, kv_out, out_sem)
        whole.start()
        for at in range(items):
            for k in range(1, copies):
                copy(at, k).wait_send()
        whole.wait()
        gather.finish()


def mix_back_kernel(scale, shares, *refs):
    count = len(shares)
    prefix_ref, action_ref, prefix_grad_ref, action_grad_ref, bias_ref, kv_ref = refs[:6]
    shards, refs = refs[6 : 6 + count], refs[6 + count :]
    prefix_out, action_out, kv_out = refs[:3]
    wholes, refs = refs[3 : 3 + count], refs[3 + count :]
    total, own, sent, arrived, send_sem, recv_sem = refs[:6]
    gather = Gather(shares, shards, wholes, refs[6:])
    copies = lax.axis_size("dp")
    place, me = lax.axis_index("dp"), lax.axis_index("fsdp")
    item, head = pl.program_id(0), pl.program_id(1)
    items, heads = pl.num_programs(0), pl.num_programs(1)
    rows = prefix_ref.shape[1]
    step = rows + action_ref.shape[1]
    turn = item * heads + head

    def copy(at, k):
        return pltpu.make_async_remote_copy(
            src_ref=sent.at[at, k - 1],
            dst_ref=arrived.at[at, k - 1],
            send_sem=send_sem.at[at, k],
            recv_sem=recv_sem.at[at, k],
            device_id=(lax.rem(place + copies - k, copies), me),
            device_id_type=pl.DeviceIdType.MESH,
        )

    @pl.when(turn == 0)
    def _():
        gather.greet()
        gather.start()

    @pl.when((turn > 0) & (turn < gather.chips))
    def _():
        gather.advance(turn)

    @pl.when(head == 0)
    def _():
        total[...] = jnp.zeros_like(total)

    queries = stacked((prefix_ref, action_ref))
    grads = stacked((prefix_grad_ref, action_grad_ref))
    kv = jnp.concatenate([kv_ref[k, 0] for k in range(copies)], axis=0)
    head_size = kv.shape[1] // 2
    keys, values = kv[:, :head_size], kv[:, head_size:]
    probs = softmax_of(queries, keys, bias_ref[0], scale)
    probs_grad = multiply_right(grads, values)
    delta = jnp.sum(probs * probs_grad, axis=-1, keepdims=True)
    score_grad = (probs * (probs_grad - delta)).astype(LOW)
    query_grad = (multiply(score_grad, keys) * scale).astype(LOW)
    prefix_out[0] = query_grad[:rows]
    action_out[0] = query_grad[rows:]
    total[:, :head_size] += multiply_left(score_grad, queries) * scale
    total[:, head_size:] += multiply_left(probs.astype(LOW), grads)

    @pl.when(head == heads - 1)
    def _():
        own[item] = total[:step]
        for k in range(1, copies):
            sent[item, k - 1] = total[k * step : (k + 1) * step].astype(LOW)
            copy(item, k).start()

    @pl.when((item == items - 1) & (head == heads - 1))
    def _():
        for at in range(kv_out.shape[0]):
            for k in range(1, copies):
                copy(at, k).wait_recv()
                copy(at, k).wait_send()
            summed = own[at]
            for k in range(1, copies):
                summed = summed + arrived[at, k - 1].astype(FULL)
            kv_out[at] = summed.astype(LOW)
        gather.finish()


def mix_call(scale, heads, prefix, action, bias, grads=None, kv=None, shards=()):
    copies = lax.axis_size("dp")
    items, prefix_rows, columns = prefix.shape
    action_rows = action.shape[1]
    rows, length = prefix_rows + action_rows, bias.shape[2]
    head_size = columns // (heads + 2)
    features = heads * head_size
    per_head = [
        pl.BlockSpec((1, prefix_rows, head_size), lambda i, h: (i, 0, h)),
        pl.BlockSpec((1, action_rows, head_size), lambda i, h: (i, 0, h)),
    ]
    bias_spec = pl.BlockSpec((1, rows, length), lambda i, h: (i, 0, 0))
    shapes = [
        jax.ShapeDtypeStruct((items, prefix_rows, features), LOW),
        jax.ShapeDtypeStruct((items, action_rows, features), LOW),
    ]
    dma = pltpu.SemaphoreType.DMA
    sems = [dma((items, copies)), dma((items, copies))]
    block = (rows, 2 * head_size)
    if grads is None:
        return pl.pallas_call(
            functools.partial(mix_kernel, scale, features, shares_of(shards)),
            out_shape=shapes
            + [jax.ShapeDtypeStruct((copies, items, *block), LOW)]
            + whole_shapes(shards),
            grid=(items, heads),
            in_specs=per_head
            + [
                pl.BlockSpec(prefix.shape, lambda i, h: (0, 0, 0)),
                pl.BlockSpec(action.shape, lambda i, h: (0, 0, 0)),
                bias_spec,
            ]
            + [pl.BlockSpec(memory_space=pl.ANY)] * len(shards),
            out_specs=per_head + [pl.BlockSpec(memory_space=pl.ANY)] * (1 + len(shards)),
            scratch_shapes=[pltpu.VMEM((copies, items, *block), LOW), *sems, dma]
            + Gather.scratch(len(shards)),
            compiler_params=pltpu.CompilerParams(
                collective_id=7, has_side_effects=True, vmem_limit_bytes=48 * MIB
            ),
            cost_estimate=SMALL,
            name="mix",
        )(prefix, action, prefix, action, bias, *shards)
    return pl.pallas_call(
        functools.partial(mix_back_kernel, scale, shares_of(shards)),
        out_shape=shapes + [jax.ShapeDtypeStruct((items, *block), LOW)] + whole_shapes(shards),
        grid=(items, heads),
        in_specs=per_head * 2
        + [bias_spec, pl.BlockSpec((copies, 1, *block), lambda i, h: (0, i, 0, 0))]
        + [pl.BlockSpec(memory_space=pl.ANY)] * len(shards),
        out_specs=per_head
        + [pl.BlockSpec((items, *block), lambda i, h: (0, 0, 0))]
        + [pl.BlockSpec(memory_space=pl.ANY)] * len(shards),
        scratch_shapes=[
            pltpu.VMEM((length, 2 * head_size), FULL),
            pltpu.VMEM((items, *block), FULL),
            pltpu.VMEM((items, copies - 1, *block), LOW),
            pltpu.VMEM((items, copies - 1, *block), LOW),
            *sems,
            *Gather.scratch(len(shards)),
        ],
        compiler_params=pltpu.CompilerParams(
            collective_id=8, has_side_effects=True, vmem_limit_bytes=48 * MIB
        ),
        cost_estimate=SMALL,
        name="mix_back",
    )(prefix, action, *grads, bias, kv, *shards)


def body(
    prefix_in,
    action_in,
    valid_count,
    prefix_before,
    prefix_query,
    prefix_key,
    prefix_value,
    prefix_output,
    prefix_middle,
    prefix_gate,
    prefix_up,
    prefix_down,
    action_before,
    action_query,
    action_key,
    action_value,
    action_output,
    action_middle,
    action_gate,
    action_up,
    action_down,
    prefix_cotangent,
    action_cotangent,
):
    line = Line()
    shards = line.size
    copies = lax.axis_size("dp")
    items, prefix_rows, width = prefix_in.shape
    action_rows = action_in.shape[1]
    action_width = action_in.shape[2]
    head_size = prefix_key.shape[1]
    features = prefix_query.shape[1]
    heads = features // head_size
    columns = features + 2 * head_size
    prefix_length = prefix_rows * copies
    scale = head_size ** (-0.5)
    place = lax.axis_index("dp")
    prefix_pad, action_pad = rounded(prefix_rows), rounded(action_rows)
    prefix_tokens, action_tokens = items * prefix_pad, items * action_pad
    folded = action_tokens * action_width // width
    folded_pad = rounded(folded)

    def padded(prefix, action):
        prefix = jnp.pad(prefix, ((0, 0), (0, prefix_pad - prefix_rows), (0, 0)))
        action = jnp.pad(action, ((0, 0), (0, action_pad - action_rows), (0, 0)))
        return prefix.reshape(prefix_tokens, width), action.reshape(action_tokens, action_width)

    def trimmed(prefix, action):
        prefix = prefix.reshape(items, prefix_pad, width)[:, :prefix_rows]
        return prefix, action.reshape(items, action_pad, action_width)[:, :action_rows]

    def fold(action):
        rows = action.reshape(-1, folded, width)
        return jnp.pad(rows, ((0, 0), (0, folded_pad - folded), (0, 0)))

    def unfold(rows):
        return rows[:folded].reshape(action_tokens, action_width)

    def pack(prefix, action):
        return jnp.concatenate([prefix, fold(action)[0]], axis=0)

    def unpack(packed):
        return packed[:prefix_tokens], unfold(packed[prefix_tokens:])

    share, action_share = prefix_before.shape[0], action_before.shape[0]
    cuts = [0, share, 2 * share, 2 * share + action_share, 2 * share + 2 * action_share]
    gain_rows = rounded(-(-cuts[4] // 128))
    gains = jnp.concatenate([prefix_before, prefix_middle, action_before, action_middle])
    gains = jnp.pad(gains, (0, gain_rows * 128 - cuts[4])).reshape(gain_rows, 128)
    prefix_qkv, action_qkv, gains = gather_shards(
        0,
        jnp.concatenate([prefix_query, prefix_key, prefix_value], axis=1),
        jnp.concatenate([action_query, action_key, action_value], axis=1),
        gains,
    )
    gains = gains.reshape(shards, gain_rows * 128).astype(FULL)
    prefix_gain_in, prefix_gain, action_gain_in, action_gain = (
        gains[:, cuts[i] : cuts[i + 1]].reshape(-1) for i in range(4)
    )

    live = (place * action_rows + jnp.arange(action_rows))[None, :] < valid_count[:, None]
    prefix_back, action_back = padded(
        prefix_cotangent,
        jnp.where(live[:, :, None], action_cotangent, jnp.zeros_like(action_cotangent)),
    )
    backs = lax.all_gather(pack(prefix_back, action_back), "fsdp", axis=0, tiled=True)

    prefix_flat, action_flat = padded(prefix_in, action_in)
    prefix_hidden, prefix_all = entry_forward(prefix_flat, prefix_gain_in, prefix_qkv)
    prefix_all = prefix_all.reshape(items, prefix_pad, columns)
    action_hidden, action_all = entry_forward(action_flat, action_gain_in, action_qkv)
    action_all = action_all.reshape(items, action_pad, columns)
    far = copies * (prefix_rows + action_rows)

    def places(owner):
        prefix = jnp.arange(prefix_pad)
        action = jnp.arange(action_pad)
        return jnp.concatenate(
            [
                jnp.where(prefix < prefix_rows, owner * prefix_rows + prefix, far),
                jnp.where(
                    action < action_rows, prefix_length + owner * action_rows + action, far
                ),
            ]
        )

    query_place = places(place)
    key_place = jnp.concatenate([places((place + copies - k) % copies) for k in range(copies)])
    later = (query_place[:, None] >= prefix_length) & (key_place[None, :] <= query_place[:, None])
    allowed = (key_place[None, None, :] < prefix_length) | later[None] & (
        key_place[None, None, :] < prefix_length + valid_count[:, None, None]
    )
    bias = jnp.where(allowed, 0.0, NEGATIVE).astype(FULL)
    prefix_mixed, action_mixed, kv, prefix_o, action_o = mix_call(
        scale, heads, prefix_all, action_all, bias, shards=(prefix_output, action_output)
    )
    backs, prefix_mixed = lax.optimization_barrier((backs, prefix_mixed))
    action_mixed = action_mixed.reshape(action_tokens, features)
    prefix_mixed = prefix_mixed.reshape(prefix_tokens, features)
    action_mid, action_ffn = middle_forward(action_mixed, action_flat, action_gain, action_o)
    prefix_mid, hidden = middle_forward(
        prefix_mixed, prefix_flat, prefix_gain, prefix_o, fold(action_ffn)[0]
    )
    inner, gate_grad, up_grad, all_rows, all_back, small = feed_all(
        prefix_tokens, hidden, backs, prefix_gate, prefix_up, prefix_down
    )
    action_rows_all, action_back_all = (
        small[i, :, :, :folded].reshape(shards * action_tokens, action_width) for i in range(2)
    )
    action_inner, pull = jax.vjp(
        activate, multiply(action_rows_all, action_gate), multiply(action_rows_all, action_up)
    )
    action_inner = action_inner.astype(LOW)
    action_gate_grad, action_up_grad = (
        v.astype(LOW) for v in pull(multiply_right(action_back_all, action_down))
    )

    down_grad = multiply_left(inner, all_back).astype(LOW)
    action_feed = tuple(
        v.astype(LOW)
        for v in (
            multiply_left(action_rows_all, action_gate_grad),
            multiply_left(action_rows_all, action_up_grad),
            multiply_left(action_inner, action_back_all),
        )
    )
    gate_weight_grad = multiply_left(all_rows, gate_grad).astype(LOW)
    gate_grad, up_grad, down_grad, gate_weight_grad = lax.optimization_barrier(
        (gate_grad, up_grad, down_grad, gate_weight_grad)
    )
    def halves(rows):
        return fold(rows.astype(LOW)).reshape(line.chips, 2, folded_pad, width)

    up_weight_grad = multiply_left(all_rows, up_grad).astype(LOW)
    gate_grad, up_grad, down_grad, gate_weight_grad, up_weight_grad, action_feed = (
        lax.optimization_barrier(
            (gate_grad, up_grad, down_grad, gate_weight_grad, up_weight_grad, action_feed)
        )
    )
    feed_sums = lax.psum((down_grad, gate_weight_grad, up_weight_grad, *action_feed), "dp")
    parts = part_chunks(
        prefix_tokens,
        lax.optimization_barrier((inner, up_weight_grad))[0],
        prefix_down,
        halves(multiply(action_inner, action_down)),
    )
    sent, gate_grad = lax.optimization_barrier((parts, gate_grad))
    out_sums = Relay(line, sent, lambda chip: line.chip ^ chip)
    out_sums.advance(1)
    small = halves(
        multiply_right(action_gate_grad, action_gate) + multiply_right(action_up_grad, action_up)
    )
    feed_back = collect(
        2, prefix_tokens, True, (gate_grad, up_grad), (prefix_gate, prefix_up), small, width
    )
    feed_back = out_sums.after(feed_back)
    out_sums.advance(2)

    prefix_mid_grad, prefix_low, prefix_mixed_grad, prefix_middle_part = middle_back(
        feed_back, prefix_mid, prefix_back, prefix_gain, prefix_o
    )
    action_mid_grad, action_low, action_mixed_grad, action_middle_part = middle_back(
        unfold(feed_back[prefix_tokens:]), action_mid, action_back, action_gain, action_o
    )
    sent = line.pairs(9, prefix_mixed, prefix_low)
    output_sums = Relay(line, sent, lambda chip: chip)
    output_sums.advance(1)
    mixed_grads = (
        prefix_mixed_grad.reshape(items, prefix_pad, features),
        action_mixed_grad.reshape(items, action_pad, features),
    )
    tokens_all = jnp.concatenate([action_hidden, action_mixed, action_low], axis=1)
    prefix_query_grad, action_query_grad, kv_grad, tokens_all = mix_call(
        scale, heads, prefix_all, action_all, bias, mixed_grads, kv, (tokens_all,)
    )
    kv_grad = output_sums.after(out_sums.after(kv_grad))
    output_sums.advance(2)
    prefix_qkv_grad = jnp.concatenate([prefix_query_grad, kv_grad[:, :prefix_pad]], axis=2)
    action_qkv_grad = jnp.concatenate([action_query_grad, kv_grad[:, prefix_pad:]], axis=2)
    prefix_qkv_grad = prefix_qkv_grad.reshape(prefix_tokens, columns)
    action_qkv_grad = action_qkv_grad.reshape(action_tokens, columns)
    prefix_grad, prefix_before_part = entry_back(
        prefix_query_grad.reshape(prefix_tokens, features),
        kv_grad[:, :prefix_pad].reshape(prefix_tokens, 2 * head_size),
        prefix_flat,
        prefix_mid_grad,
        prefix_gain_in,
        prefix_qkv,
    )
    action_grad, action_before_part = entry_back(
        action_query_grad.reshape(action_tokens, features),
        kv_grad[:, prefix_pad:].reshape(action_tokens, 2 * head_size),
        action_flat,
        action_mid_grad,
        action_gain_in,
        action_qkv,
    )
    prefix_grad, action_grad = trimmed(prefix_grad, action_grad)

    gain_parts = jnp.concatenate(
        [
            part.reshape(shards, -1)
            for part in (
                prefix_before_part,
                prefix_middle_part,
                action_before_part,
                action_middle_part,
            )
        ],
        axis=1,
    )
    gain_rows = rounded(-(-cuts[4] // columns))
    gain_parts = jnp.pad(gain_parts, ((0, 0), (0, gain_rows * columns - cuts[4])))
    gain_parts = gain_parts.astype(LOW).reshape(shards, gain_rows, columns)
    gain_parts = output_sums.after(gain_parts)
    output_sums.advance(3)
    sent = line.pairs(10, prefix_hidden, prefix_qkv_grad, gain_parts)
    edges = [0]
    for part in (action_width, features, action_width):
        edges.append(edges[-1] + part)
    hidden_all, mixed_all, low_all = (
        tokens_all[:, start:stop] for start, stop in zip(edges, edges[1:])
    )
    rows = action_query.shape[0]
    hidden_slice = lax.dynamic_slice_in_dim(hidden_all, line.place * rows, rows, 1)
    rows = action_output.shape[0]
    action_output_owned = multiply_left(
        lax.dynamic_slice_in_dim(mixed_all, line.place * rows, rows, 1), low_all
    )
    output_owned, action_output_owned, *qkv_owned, gain_owned = tail_sums(
        [output_sums.finish().astype(LOW), action_output_owned.astype(LOW)],
        sent,
        prefix_query.shape[0],
        hidden_slice,
        action_qkv_grad,
        (features, head_size, head_size),
    )
    feed_sums, output_owned, sent = lax.optimization_barrier((feed_sums, output_owned, sent))
    out_sums.advance(3)
    out_sums.arrived, output_owned = lax.optimization_barrier((out_sums.arrived, output_owned))
    feed_sums = [widen(value) for value in feed_sums]
    sums = unpack(out_sums.finish())
    prefix_out, action_out = trimmed(
        (prefix_mid + sums[0]).astype(LOW), (action_mid + sums[1]).astype(LOW)
    )
    gain_owned = gain_owned.reshape(-1)
    return (
        prefix_out,
        action_out,
        prefix_grad,
        action_grad,
        gain_owned[cuts[0] : cuts[1]],
        *qkv_owned[3:],
        output_owned,
        gain_owned[cuts[1] : cuts[2]],
        feed_sums[1],
        feed_sums[2],
        feed_sums[0],
        gain_owned[cuts[2] : cuts[3]],
        *qkv_owned[:3],
        action_output_owned,
        gain_owned[cuts[3] : cuts[4]],
        *feed_sums[3:],
    )


def solution(mesh):
    tokens = P("fsdp", "dp", None)
    rows, columns, vector = P("fsdp", None), P(None, "fsdp"), P("fsdp")
    weights = (vector, rows, rows, rows, rows, vector, columns, columns, rows)
    return jax.shard_map(
        body,
        mesh=mesh,
        in_specs=(tokens, tokens, vector, *weights, *weights, tokens, tokens),
        out_specs=(tokens, tokens, tokens, tokens, *weights, *weights),
        check_vma=False,
    )
```
